32 devices in a mesh: row: 8 (over y, x, core), col: 4 (over z).
Axes of the slice: x: 2, y: 2, z: 4, core: 2. Of those that a mesh axis runs over, the one named last changes fastest.
Arguments:
- covariance: float32 [12288, 12288], P('row', 'col'), may hold values from -6 to 6
- east_wind: float32 [96, 128], replicated, may hold values from -0.3 to 0.3
- north_wind: float32 [96, 128], replicated, may hold values from -0.3 to 0.3
- diffuse_lon: float32 [96, 128], replicated, may hold values from 0.05 to 0.2
- diffuse_lat: float32 [96, 128], replicated, may hold values from 0.05 to 0.2
Outputs:
- propagated: float32 [12288, 12288], P('row', 'col')
The draws below stay inside these ranges and needn't reach their ends.
All inputs are finite; a program needn't handle non-finite values.
Results may differ from the reference program's by a relative error of at most 0.00002.
Values sent between devices are 32-bit elements; how exact they have to be, the bound alone decides.
A program may use at most 192 MiB of HBM per device.

```python
import math
import jax
import jax.numpy as jnp
from jax import lax

NLAT = 96
NLON = 128
STEPS = 3
ORDER = 12288


def level_of(stream_key, dims, pieces, low, top_value):
    loudness = 1.0
    for axis_at, parts in pieces:
        steps = jax.random.uniform(jax.random.fold_in(jax.random.fold_in(stream_key, 6), axis_at), (parts,), jnp.float32, low / len(pieces), top_value / len(pieces))
        loudness = loudness * jnp.repeat(jnp.exp(steps), dims[axis_at] // parts).reshape((-1,) + (1,) * (len(dims) - 1 - axis_at))
    return loudness


def scatter_about(own_key, dims, scale, limit, pieces=(), held_as=jnp.bfloat16):
    values = jax.random.normal(own_key, dims, jnp.float32) * scale
    if len(pieces) > 0:
        values = level_of(own_key, dims, pieces, -0.22, 0.18) * values
    return jnp.clip(values, min=-limit, max=limit).astype(held_as)


def setup_inputs(seed: int = 0) -> dict:
    keys = jax.random.split(jax.random.key(seed), 6)
    covariance = scatter_about(keys[0], (ORDER, ORDER), 1.0, 6.0, ((0, 8), (1, 4)), jnp.float32)
    east_wind = jnp.clip(jax.random.uniform(keys[1], (NLAT, NLON), jnp.float32, -0.3, 0.3), -0.3, 0.3)
    north_wind = jnp.clip(jax.random.uniform(keys[2], (NLAT, NLON), jnp.float32, -0.3, 0.3), -0.3, 0.3)
    diffuse_lon = jnp.clip(jnp.exp(jax.random.uniform(keys[3], (NLAT, NLON), jnp.float32, math.log(0.05), math.log(0.2))), 0.05, 0.2)
    diffuse_lat = jnp.clip(jnp.exp(jax.random.uniform(keys[4], (NLAT, NLON), jnp.float32, math.log(0.05), math.log(0.2))), 0.05, 0.2)
    return dict(covariance=covariance, east_wind=east_wind, north_wind=north_wind, diffuse_lon=diffuse_lon, diffuse_lat=diffuse_lat)


def advect(widened, lat_dim, east_wind, north_wind, diffuse_lon, diffuse_lat):
    length = widened.shape[lat_dim]
    north = lax.slice_in_dim(widened, 2, length, axis=lat_dim)
    south = lax.slice_in_dim(widened, 0, length - 2, axis=lat_dim)
    center = lax.slice_in_dim(widened, 1, length - 1, axis=lat_dim)
    eastern = jnp.roll(center, -1, lat_dim + 1)
    western = jnp.roll(center, 1, lat_dim + 1)
    return (center - 0.5 * east_wind * (eastern - western) - 0.5 * north_wind * (north - south)
            + diffuse_lon * (eastern - 2.0 * center + western)
            + diffuse_lat * (north - 2.0 * center + south))


def reference(covariance, east_wind, north_wind, diffuse_lon, diffuse_lat):
    values = covariance.reshape(NLAT, NLON, ORDER)
    coefs = [c[:, :, None] for c in (east_wind, north_wind, diffuse_lon, diffuse_lat)]
    for section in range(STEPS):
        widened = jnp.pad(values, ((1, 1), (0, 0), (0, 0)))
        values = advect(widened, 0, *coefs)
    values = values.reshape(ORDER, NLAT, NLON)
    coefs = [c[None] for c in (east_wind, north_wind, diffuse_lon, diffuse_lat)]
    for section in range(STEPS):
        widened = jnp.pad(values, ((0, 0), (1, 1), (0, 0)))
        values = advect(widened, 1, *coefs)
    return values.reshape(ORDER, ORDER)
```

```python
import functools

import jax
import jax.numpy as jnp
from jax import lax
from jax.experimental import pallas as pl
from jax.experimental.pallas import tpu as pltpu
from jax.sharding import PartitionSpec as P

NLON = 128
STEPS = 3
UNIT = STEPS * NLON
WIDE = 256
BLOCK = 192
VMEM = 52 * 1024 * 1024


OFFSETS = [(y, x) for y in range(-STEPS, STEPS + 1) for x in range(-STEPS + abs(y), STEPS + 1 - abs(y))]


def power_kernel(east_wind, north_wind, diffuse_lon, diffuse_lat, plain, rolled):
    lon, lat = diffuse_lon[...], diffuse_lat[...]
    half_east, half_north = 0.5 * east_wind[...], 0.5 * north_wind[...]
    one = {
        (0, 0): 1.0 - 2.0 * lon - 2.0 * lat,
        (0, 1): lon - half_east,
        (0, -1): lon + half_east,
        (1, 0): lat - half_north,
        (-1, 0): lat + half_north,
    }
    lines = lon.shape[0]
    line = lax.broadcasted_iota(jnp.int32, lon.shape, 0)

    def seen(field, y, x):
        if x:
            return pltpu.roll(field, -x % NLON, 1)
        if y:
            edge = lines - 1 if y > 0 else 0
            return jnp.where(line == edge, 0.0, pltpu.roll(field, -y % lines, 0))
        return field

    power = dict(one)
    for _ in range(STEPS - 1):
        made = {}
        for (y, x), field in power.items():
            for (sy, sx), scale in one.items():
                term = scale * seen(field, sy, sx)
                at = (y + sy, x + sx)
                made[at] = made[at] + term if at in made else term
        power = made
    for k, (y, x) in enumerate(OFFSETS):
        plain[k] = power[y, x]
        rolled[k] = pltpu.roll(power[y, x], x % NLON, 1)


def powers(tables):
    shape = jax.ShapeDtypeStruct((len(OFFSETS),) + tables[0].shape, jnp.float32)
    return pl.pallas_call(
        power_kernel,
        out_shape=(shape, shape),
        compiler_params=pltpu.CompilerParams(vmem_limit_bytes=VMEM),
        cost_estimate=pl.CostEstimate(flops=10**7, bytes_accessed=10**7, transcendentals=0),
    )(*tables)


def split(value):
    high = value.astype(jnp.bfloat16)
    return high, (value - high.astype(jnp.float32)).astype(jnp.bfloat16)


def block_kernel(made, transposed, offset, table, out):
    base = offset[0] + pl.program_id(0) * made
    sub = lax.broadcasted_iota(jnp.int32, (NLON, NLON), 0)
    lane = lax.broadcasted_iota(jnp.int32, (NLON, NLON), 1)
    away = (sub - lane if transposed else lane - sub) & (NLON - 1)
    read = made + 2 * STEPS
    for a in range(made):
        for b in range(read):
            y = b - a - STEPS
            value = jnp.zeros((NLON, NLON), jnp.float32)
            for k, (oy, x) in enumerate(OFFSETS):
                if oy == y:
                    line = table[k, pl.ds(base + a, 1), :]
                    value = jnp.where(away == x % NLON, jnp.broadcast_to(line, (NLON, NLON)), value)
            high, low = split(value)
            mine, theirs = slice(a * NLON, (a + 1) * NLON), slice(b * NLON, (b + 1) * NLON)
            if transposed:
                out[0, theirs, mine] = high
                out[0, slice((read + b) * NLON, (read + b + 1) * NLON), mine] = low
            else:
                out[0, mine, theirs] = high
                out[0, slice((made + a) * NLON, (made + a + 1) * NLON), theirs] = low


def blocks_of(table, offset, groups, made, transposed):
    read = made + 2 * STEPS
    shape = (2 * read * NLON, made * NLON) if transposed else (2 * made * NLON, read * NLON)
    return pl.pallas_call(
        functools.partial(block_kernel, made, transposed),
        grid=(groups,),
        in_specs=[
            pl.BlockSpec(memory_space=pltpu.SMEM),
            pl.BlockSpec(table.shape, lambda i: (0, 0, 0)),
        ],
        out_specs=pl.BlockSpec((1,) + shape, lambda i: (i, 0, 0)),
        out_shape=jax.ShapeDtypeStruct((groups,) + shape, jnp.bfloat16),
        compiler_params=pltpu.CompilerParams(vmem_limit_bytes=VMEM),
        cost_estimate=pl.CostEstimate(flops=10**7, bytes_accessed=2 * 10**7, transcendentals=0),
    )(offset.reshape(1).astype(jnp.int32), table)


def dot(a, b):
    return jnp.dot(a, b, preferred_element_type=jnp.float32)


def stencil(c, east, west, north, south, coef):
    return coef[0] * c + coef[1] * east + coef[2] * west + coef[3] * north + coef[4] * south


def column_kernel(parts, sides, *refs):
    ins, tables, out = refs[: len(parts)], refs[len(parts)], refs[-1]
    for side, (names, first, count) in enumerate(sides):

        def source(line):
            part, at = divmod(line, STEPS)
            return ins[names[part]][at * NLON : (at + 1) * NLON, :]

        lines = count + 2 * STEPS
        got = {}
        for line in range(lines):
            got[0, line] = source(line)
            for step in range(1, STEPS + 1):
                mid = line - step
                if mid < step:
                    continue
                c = got[step - 1, mid]
                row = first + mid - 1
                value = stencil(
                    c,
                    pltpu.roll(c, NLON - 1, 0),
                    pltpu.roll(c, 1, 0),
                    got[step - 1, mid + 1],
                    got[step - 1, mid - 1],
                    [tables[k, row] for k in range(5)],
                )
                got.pop((step - 1, mid - 1))
                if step < STEPS:
                    got[step, mid] = value
                else:
                    at = sum(s[2] for s in sides[:side]) + mid - STEPS
                    out[at * NLON : (at + 1) * NLON, :] = value


def column_sweep(arrays, sides, width, coefs):
    total = sum(count for _, _, count in sides) * NLON
    in_specs = [
        pl.BlockSpec((UNIT, NLON), functools.partial(lambda i, r, c, skip: (r, jnp.where(i < UNIT // NLON, i + c, i + c + skip)), r=r, c=c, skip=skip)) for _, r, c, skip in arrays
    ]
    in_specs.append(pl.BlockSpec(coefs.shape, lambda i: (0, 0, 0, 0)))
    work = total * width
    return pl.pallas_call(
        functools.partial(column_kernel, arrays, sides),
        grid=(width // NLON,),
        in_specs=in_specs,
        out_specs=pl.BlockSpec((total, NLON), lambda i: (0, i)),
        out_shape=jax.ShapeDtypeStruct((total, width), jnp.float32),
        compiler_params=pltpu.CompilerParams(vmem_limit_bytes=VMEM),
        cost_estimate=pl.CostEstimate(flops=work * 40, bytes_accessed=work * 12, transcendentals=0),
    )(*[a[0] for a in arrays], coefs)


def row_kernel(count, *refs):
    ins, tables, out, both = refs[: count + 2], refs[count + 2], refs[-2], refs[-1]
    rows = out.shape[0]
    read = (2 + 2 * STEPS) * NLON
    for n, ref in enumerate(ins):
        cols = slice(n * UNIT, (n + 1) * UNIT)
        both[:rows, cols], both[rows:, cols] = split(ref[...])
    for pair in range(count * STEPS // 2):
        cols = slice(pair * 2 * NLON, pair * 2 * NLON + read)
        first = dot(both[:, cols], tables[pair, :read, :])
        other = dot(both[:rows, cols], tables[pair, read:, :])
        out[:, pair * 2 * NLON : (pair + 1) * 2 * NLON] = first[:rows] + (first[rows:] + other)


def row_sweep(arrays, part, tables, out_rows, row_block, out_cols, col_block, buffer):
    count = len(arrays) - 2
    rows = arrays[0][0].shape[0]
    pairs = count * STEPS // 2
    in_specs = [pl.BlockSpec((BLOCK, UNIT), functools.partial(lambda i, c: (i, c), c=c)) for _, c in arrays]
    in_specs.append(
        pl.BlockSpec((pairs,) + tables.shape[1:], lambda i: (part, 0, 0), pipeline_mode=pl.Buffered(1))
    )
    operands = [a for a, _ in arrays] + [tables]
    aliases = {}
    if buffer is not None:
        in_specs.append(pl.BlockSpec(memory_space=pl.ANY))
        operands.append(buffer)
        aliases = {len(operands) - 1: 0}
    work = rows * count * UNIT
    return pl.pallas_call(
        functools.partial(row_kernel, count),
        grid=(rows // BLOCK,),
        in_specs=in_specs,
        out_specs=pl.BlockSpec((BLOCK, count * UNIT), lambda i: (row_block(i), col_block)),
        out_shape=jax.ShapeDtypeStruct((out_rows, out_cols), jnp.float32),
        input_output_aliases=aliases,
        scratch_shapes=[pltpu.VMEM((2 * BLOCK, len(arrays) * UNIT), jnp.bfloat16)],
        compiler_params=pltpu.CompilerParams(vmem_limit_bytes=VMEM),
        cost_estimate=pl.CostEstimate(flops=work * 40, bytes_accessed=work * 12, transcendentals=0),
    )(*operands)


def exchange(first, last, axis):
    devices = lax.axis_size(axis)
    up = [(i, i + 1) for i in range(devices - 1)]
    down = [(j, i) for i, j in up]
    return lax.ppermute(last, axis, up), lax.ppermute(first, axis, down)


def coefficients(tables, offset, lines):
    east_wind, north_wind, diffuse_lon, diffuse_lat = tables
    made = jnp.stack(
        [
            1.0 - 2.0 * diffuse_lon - 2.0 * diffuse_lat,
            diffuse_lon - 0.5 * east_wind,
            diffuse_lon + 0.5 * east_wind,
            diffuse_lat - 0.5 * north_wind,
            diffuse_lat + 0.5 * north_wind,
        ]
    )
    edge = STEPS - 1
    made = jnp.pad(made, ((0, 0), (edge, edge), (0, 0)))
    return lax.dynamic_slice_in_dim(made, offset, lines + 2 * edge, 1)


def body(covariance, east_wind, north_wind, diffuse_lon, diffuse_lat):
    tables = (east_wind, north_wind, diffuse_lon, diffuse_lat)
    rows, cols = covariance.shape
    row_lines, col_lines = rows // NLON, cols // NLON
    row_units, col_units = rows // UNIT, cols // UNIT
    row_coefs = coefficients(tables, lax.axis_index("row") * row_lines, row_lines)
    row_coefs = jnp.broadcast_to(row_coefs[:, :, :, None], row_coefs.shape + (NLON,))
    plain, _ = powers(tables)
    col_tables = blocks_of(plain, lax.axis_index("col") * col_lines, col_lines // 2, 2, True)

    if col_units == 1:
        pieces = [[0]]
    else:
        pieces = [[0, col_units - 1]]
        half = col_units // 2
        if col_units % 2 == 0 and col_units >= 6:
            pieces += [list(range(1, half + 1)), list(range(half + 1, col_units - 1))]
        elif col_units > 2:
            pieces += [list(range(1, col_units - 1))]

    def columns(units, low, high):
        parts = []
        for u in units:
            if parts and parts[-1][1] == u:
                parts[-1][1] = u + 1
            else:
                parts.append([u, u + 1])
        return jnp.concatenate([covariance[low:high, a * UNIT : b * UNIT] for a, b in parts], axis=1)

    halos = [exchange(columns(p, 0, UNIT), columns(p, rows - UNIT, rows), "row") for p in pieces]

    inner = None
    if row_units > 2:
        inner = column_sweep(
            [(covariance, r, 0, 0) for r in range(row_units)],
            [(list(range(row_units)), STEPS, row_lines - 2 * STEPS)],
            cols,
            row_coefs,
        )

    outer = []
    where = {}
    for k, (units, (before, after)) in enumerate(zip(pieces, halos)):
        width = len(units) * UNIT
        skip = (cols - 2 * UNIT) // NLON if k == 0 and col_units > 1 else 0
        blocks = [(covariance, r, units[0] * (UNIT // NLON), skip) for r in range(row_units)]
        if row_units == 1:
            arrays = [(before, 0, 0, 0), blocks[0], (after, 0, 0, 0)]
            sides = [([0, 1, 2], 0, STEPS)]
        else:
            arrays = [(before, 0, 0, 0), blocks[0], blocks[1], blocks[-2], blocks[-1], (after, 0, 0, 0)]
            sides = [([0, 1, 2], 0, STEPS), ([3, 4, 5], row_lines - STEPS, STEPS)]
        outer.append(column_sweep(arrays, sides, width, row_coefs))
        for at, u in enumerate(units):
            where[u] = (k, at)

    out_blocks, tiles = rows // BLOCK, UNIT // BLOCK
    halves = [list(range(col_units))]
    if len(pieces) == 3:
        halves = [list(range(half)), list(range(half, col_units))]

    edges = outer[0]
    outer_halo = exchange(edges[:, :UNIT], edges[:, -UNIT:], "col")
    out = None
    if inner is not None:
        inner_halo = exchange(inner[:, :UNIT], inner[:, cols - UNIT :], "col")
        arrays = [(inner_halo[0], 0)] + [(inner, u) for u in range(col_units)] + [(inner_halo[1], 0)]
        out = row_sweep(arrays, 0, col_tables, rows, lambda i: i + tiles, cols, 0, out)

    def outer_row(i):
        return jnp.where(i < tiles, i, i + out_blocks - 2 * tiles) if row_units > 1 else i

    for h, units in enumerate(halves):
        arrays = []
        for u in [units[0] - 1] + units + [units[-1] + 1]:
            if u < 0:
                arrays.append((outer_halo[0], 0))
            elif u == col_units:
                arrays.append((outer_halo[1], 0))
            else:
                arrays.append((outer[where[u][0]], where[u][1]))
        out = row_sweep(arrays, h, col_tables, rows, outer_row, cols, h, out)
    return out


LANES = 128
SUBS = 8
PAD = 8
HALO = STEPS * NLON
PAIR = 2
RBLOCK = 32
MESH = pl.DeviceIdType.MESH


def tile_order(tiles):
    edges = list(range(STEPS)) + list(range(tiles - STEPS, tiles))
    return edges, list(range(STEPS, tiles - STEPS))


def detours(row_devices, tiles):
    if row_devices != 8:
        return None
    _, middle = tile_order(tiles)
    carried = [t for n, t in enumerate(middle) if n % 3]
    return dict(low=3, high=4, up_by=7, down_by=0, tiles=carried)


def fused_kernel(row_devices, col_devices, lines, tiles, cov, ew, nw, dlon, dlat, out, relay, big, fwd, one, two, pads, ctab, rtab,
                 load_sem, up_send, up_recv, down_send, down_recv, hop_send, hop_recv, z_send, z_recv, out_sem):
    r, c = lax.axis_index("row"), lax.axis_index("col")
    rows = lines * NLON
    edges, middle = tile_order(tiles)
    detour = detours(row_devices, tiles)
    carried = detour["tiles"] if detour else []
    has_up, has_down = r < row_devices - 1, r > 0
    has_right, has_left = c < col_devices - 1, c > 0

    partners = [(has_up, {"row": jnp.minimum(r + 1, row_devices - 1)}), (has_down, {"row": jnp.maximum(r - 1, 0)})]
    partners += [(has_right, {"col": jnp.minimum(c + 1, col_devices - 1)}), (has_left, {"col": jnp.maximum(c - 1, 0)})]
    if detour:
        for a in (detour["low"], detour["high"]):
            for b in (detour["up_by"], detour["down_by"]):
                partners += [(r == a, {"row": b}), (r == b, {"row": a})]
    barrier = pltpu.get_barrier_semaphore()
    count = 0
    for there, place in partners:
        count = count + there.astype(jnp.int32)

        @pl.when(there)
        def _():
            pl.semaphore_signal(barrier, inc=1, device_id=place, device_id_type=MESH)

    def load(t):
        return pltpu.make_async_copy(cov.at[:, pl.ds(pl.multiple_of(t * LANES, LANES), LANES)], big.at[t, pl.ds(PAD + HALO, rows), :], load_sem.at[t])

    def lanes(t):
        return pl.ds(pl.multiple_of(t * LANES, LANES), LANES)

    top, bottom = pl.ds(0, HALO), pl.ds(rows - HALO, HALO)
    before, after = pl.ds(PAD, HALO), pl.ds(PAD + HALO + rows, HALO)

    def up(t):
        return pltpu.make_async_remote_copy(cov.at[bottom, lanes(t)], big.at[t, before, :], up_send.at[t], up_recv.at[t],
                                            device_id={"row": jnp.minimum(r + 1, row_devices - 1)}, device_id_type=MESH)

    def down(t):
        return pltpu.make_async_remote_copy(cov.at[top, lanes(t)], big.at[t, after, :], down_send.at[t], down_recv.at[t],
                                            device_id={"row": jnp.maximum(r - 1, 0)}, device_id_type=MESH)

    def up_first(k, t):
        return pltpu.make_async_remote_copy(cov.at[bottom, lanes(t)], relay.at[k], up_send.at[t], hop_recv.at[k],
                                            device_id={"row": detour["up_by"]}, device_id_type=MESH)

    def down_first(k, t):
        return pltpu.make_async_remote_copy(cov.at[top, lanes(t)], relay.at[k], down_send.at[t], hop_recv.at[k],
                                            device_id={"row": detour["down_by"]}, device_id_type=MESH)

    def up_second(k, t):
        return pltpu.make_async_remote_copy(relay.at[k], big.at[t, before, :], hop_send.at[k], up_recv.at[t],
                                            device_id={"row": detour["high"]}, device_id_type=MESH)

    def down_second(k, t):
        return pltpu.make_async_remote_copy(relay.at[k], big.at[t, after, :], hop_send.at[k], down_recv.at[t],
                                            device_id={"row": detour["low"]}, device_id_type=MESH)

    for t in edges:
        load(t).start()
    pl.semaphore_wait(barrier, count)

    for t in edges + middle:
        if t in carried:
            k = carried.index(t)
            low, high = r == detour["low"], r == detour["high"]

            @pl.when(low)
            def _():
                up_first(k, t).start()

            @pl.when(high)
            def _():
                down_first(k, t).start()
        else:
            low = high = r < 0

        @pl.when(has_up & ~low)
        def _():
            up(t).start()

        @pl.when(has_down & ~high)
        def _():
            down(t).start()
    for t in middle:
        load(t).start()

    def relay_step(k):
        t = carried[k]

        @pl.when(r == detour["up_by"])
        def _():
            up_first(k, t).wait_recv()
            up_second(k, t).start()

        @pl.when(r == detour["down_by"])
        def _():
            down_first(k, t).wait_recv()
            down_second(k, t).start()

    east_wind, north_wind, lon, lat = ew[...], nw[...], dlon[...], dlat[...]
    half_east, half_north = 0.5 * east_wind, 0.5 * north_wind
    made = [1.0 - 2.0 * lon - 2.0 * lat, lon - half_east, lon + half_east, lat - half_north, lat + half_north]
    grid_lines = lon.shape[0]
    edge = STEPS - 1
    spread = -(-(lines + 2 * edge) // SUBS) * SUBS
    for k, table in enumerate(made):
        pads[k, pl.ds(0, PAD), :] = jnp.zeros((PAD, LANES), jnp.float32)
        pads[k, pl.ds(PAD, grid_lines), :] = table
        pads[k, pl.ds(PAD + grid_lines, spread), :] = jnp.zeros((spread, LANES), jnp.float32)
    wide = -(-(tiles + 2 * edge) // SUBS) * SUBS
    for k in range(len(made)):
        rtab[k] = pads[k, pl.ds(c * tiles + PAD - edge, wide), :]
        mine = pads[k, pl.ds(r * lines + PAD - edge, spread), :]
        turned = jnp.transpose(jnp.concatenate([mine, jnp.zeros((LANES - spread, LANES), jnp.float32)], axis=0))
        for i in range(lines + 2 * edge):
            ctab[k, i] = jnp.broadcast_to(turned[:, i : i + 1], (NLON, LANES))

    @pl.when(~has_down)
    def _():
        def clear(t, _):
            big[t, before, :] = jnp.zeros((HALO, LANES), jnp.float32)
            return 0
        lax.fori_loop(0, tiles, clear, 0)

    @pl.when(~has_up)
    def _():
        def clear(t, _):
            big[t, after, :] = jnp.zeros((HALO, LANES), jnp.float32)
            return 0
        lax.fori_loop(0, tiles, clear, 0)

    @pl.when(~has_left)
    def _():
        fwd[pl.ds(0, STEPS)] = jnp.zeros((STEPS, rows, LANES), jnp.float32)

    @pl.when(~has_right)
    def _():
        fwd[pl.ds(tiles + STEPS, STEPS)] = jnp.zeros((STEPS, rows, LANES), jnp.float32)

    sub = lax.broadcasted_iota(jnp.int32, (SUBS, LANES), 0)

    def line_step(line, load_from, store_to):
        for g in range(NLON // SUBS):
            at = g * SUBS
            coef = [ctab[k, line - 1, pl.ds(at, SUBS), :] for k in range(5)]
            for n in range(PAIR):
                ref, base = load_from(n)
                base = pl.multiple_of(base, SUBS)
                here = ref[pl.ds(base + at, SUBS), :]
                east = ref[pl.ds(base + at + 1, SUBS), :]
                west = ref[pl.ds(base + at - 1, SUBS), :]
                if g == NLON // SUBS - 1:
                    east = jnp.where(sub == SUBS - 1, ref[pl.ds(base, 1), :], east)
                if g == 0:
                    west = jnp.where(sub == 0, ref[pl.ds(base + NLON - 1, 1), :], west)
                north = ref[pl.ds(base + at + NLON, SUBS), :]
                south = ref[pl.ds(base + at - NLON, SUBS), :]
                value = (coef[0] * here + coef[1] * east) + (coef[2] * west + coef[3] * north) + coef[4] * south
                to, start = store_to(n)
                to[pl.ds(pl.multiple_of(start + at, SUBS), SUBS), :] = value

    def column_pass(pair, lo, hi):
        first = lo - 2

        def row(line):
            return PAD + (line - first) * NLON

        def step1(line, _):
            line_step(line, lambda n: (big.at[pair[n]], PAD + line * NLON), lambda n: (one.at[n], row(line)))
            return 0

        def step2(line, _):
            line_step(line, lambda n: (one.at[n], row(line)), lambda n: (two.at[n], row(line)))
            return 0

        def step3(line, _):
            line_step(line, lambda n: (two.at[n], row(line)), lambda n: (fwd.at[pair[n] + STEPS], (line - STEPS) * NLON))
            return 0

        lax.fori_loop(lo - 2, hi + 2, step1, 0)
        lax.fori_loop(lo - 1, hi + 1, step2, 0)
        lax.fori_loop(lo, hi, step3, 0)

    def row_pass(a, b, start, stop, store):
        def block(i, _):
            at = pl.multiple_of(start + i * RBLOCK, RBLOCK)
            got = {}
            for tile in range(a - STEPS, b + STEPS):
                got[0, tile] = fwd[tile + STEPS, pl.ds(at, RBLOCK), :]
                for step in range(1, STEPS + 1):
                    mid = tile - step
                    if mid < a - STEPS + step:
                        continue
                    here = got[step - 1, mid]
                    coef = [rtab[k, pl.ds(mid + edge, 1), :] for k in range(5)]
                    value = (
                        (coef[0] * here + coef[1] * pltpu.roll(here, LANES - 1, 1))
                        + (coef[2] * pltpu.roll(here, 1, 1) + coef[3] * got[step - 1, mid + 1])
                        + coef[4] * got[step - 1, mid - 1]
                    )
                    got.pop((step - 1, mid - 1))
                    if step < STEPS:
                        got[step, mid] = value
                    else:
                        store(mid, at, value)
            return 0

        lax.fori_loop(0, (stop - start) // RBLOCK, block, 0)

    inner = pl.ds(HALO, rows - 2 * HALO)

    def z_copy(part, right):
        where = (inner, top, bottom)[part]
        first, there = (tiles, 0) if right else (STEPS, tiles + STEPS)
        other = jnp.minimum(c + 1, col_devices - 1) if right else jnp.maximum(c - 1, 0)
        n = 2 * part + (1 if right else 0)
        return pltpu.make_async_remote_copy(fwd.at[pl.ds(first, STEPS), where, :], fwd.at[pl.ds(there, STEPS), where, :],
                                            z_send.at[n], z_recv.at[n], device_id={"col": other}, device_id_type=MESH)

    def z_start(part):
        @pl.when(has_right)
        def _():
            z_copy(part, True).start()

        @pl.when(has_left)
        def _():
            z_copy(part, False).start()

    def z_wait(part):
        @pl.when(has_right)
        def _():
            z_copy(part, True).wait_send()
            z_copy(part, False).wait_recv()

        @pl.when(has_left)
        def _():
            z_copy(part, False).wait_send()
            z_copy(part, True).wait_recv()

    def inner_out(t):
        return pltpu.make_async_copy(fwd.at[t + STEPS, inner, :], out.at[inner, lanes(t)], out_sem.at[0, t])

    def outer_out(side, t):
        rows_there = bottom if side else top
        return pltpu.make_async_copy(big.at[t, pl.ds(PAD + HALO + (rows - HALO if side else 0), HALO), :], out.at[rows_there, lanes(t)], out_sem.at[1 + side, t])

    def arrive(t):
        @pl.when(has_down)
        def _():
            up(t).wait_recv()

        @pl.when(has_up)
        def _():
            down(t).wait_recv()

    inner_lines = (2 * STEPS, lines)
    north_lines, south_lines = (STEPS, 2 * STEPS), (lines, lines + STEPS)

    pairs = [edges[n : n + PAIR] for n in range(0, len(edges), PAIR)]
    for pair in pairs:
        for t in pair:
            load(t).wait()
        column_pass(pair, *inner_lines)
    z_start(0)

    steps = len(carried)
    middle_pairs = len(middle) // PAIR
    taken = 0
    group = 3
    for at in range(0, middle_pairs, group):
        n = min(group, middle_pairs - at)

        def some(i, _):
            t = middle[0] + (at + i) * PAIR
            for m in range(PAIR):
                load(t + m).wait()
            column_pass([t + m for m in range(PAIR)], *inner_lines)
            return 0

        lax.fori_loop(0, n, some, 0)
        while taken < steps * (at + n) // middle_pairs:
            relay_step(taken)
            taken += 1

    for pair in pairs:
        for t in pair:
            arrive(t)
        column_pass(pair, *north_lines)
        column_pass(pair, *south_lines)
    z_start(1)
    z_start(2)

    z_wait(0)

    def keep_inner(tile, at, value):
        fwd[tile + STEPS, pl.ds(at, RBLOCK), :] = value

    row_pass(0, tiles, HALO, rows - HALO, keep_inner)
    for t in range(tiles):
        inner_out(t).start()

    def keep_outer(tile, at, value):
        big[tile, pl.ds(pl.multiple_of(PAD + HALO + at, SUBS), RBLOCK), :] = value

    done = 0
    waited = False
    for at in range(0, middle_pairs, group):
        n = min(group, middle_pairs - at)

        def some(i, _):
            t = middle[0] + (at + i) * PAIR
            for m in range(PAIR):
                arrive(t + m)
            pair = [t + m for m in range(PAIR)]
            column_pass(pair, *north_lines)
            column_pass(pair, *south_lines)
            return 0

        lax.fori_loop(0, n, some, 0)
        last = at + n == middle_pairs
        upto = tiles if last else middle[0] + (at + n) * PAIR - STEPS
        if not last and at == 0:
            continue
        if not waited:
            z_wait(1)
            z_wait(2)
            waited = True
        row_pass(done, upto, 0, HALO, keep_outer)
        row_pass(done, upto, rows - HALO, rows, keep_outer)
        for t in range(done, upto):
            outer_out(0, t).start()
            outer_out(1, t).start()
        done = upto

    for t in range(tiles):
        if t in carried:
            low, high = r == detour["low"], r == detour["high"]
        else:
            low = high = r < 0
        k = carried.index(t) if t in carried else 0

        @pl.when(has_up)
        def _():
            up(t).wait_send()

        @pl.when(has_down)
        def _():
            down(t).wait_send()
    for k, t in enumerate(carried):
        @pl.when(r == detour["up_by"])
        def _():
            up_second(k, t).wait_send()

        @pl.when(r == detour["down_by"])
        def _():
            down_second(k, t).wait_send()
    for t in range(tiles):
        inner_out(t).wait()
        outer_out(0, t).wait()
        outer_out(1, t).wait()


def fused_body(row_devices, col_devices, covariance, east_wind, north_wind, diffuse_lon, diffuse_lat):
    rows, cols = covariance.shape
    lines, tiles = rows // NLON, cols // NLON
    edge = STEPS - 1
    spread = -(-(lines + 2 * edge) // SUBS) * SUBS
    wide = -(-(tiles + 2 * edge) // SUBS) * SUBS
    slack = PAD + east_wind.shape[0] + max(spread, wide)
    detour = detours(row_devices, tiles)
    hops = len(detour["tiles"]) if detour else 1
    deep = lines - 2 * STEPS + 4
    f32 = jnp.float32
    out, _ = pl.pallas_call(
        functools.partial(fused_kernel, row_devices, col_devices, lines, tiles),
        in_specs=[pl.BlockSpec(memory_space=pl.ANY)] + [pl.BlockSpec(memory_space=pltpu.VMEM)] * 4,
        out_specs=[pl.BlockSpec(memory_space=pl.ANY)] * 2,
        out_shape=[jax.ShapeDtypeStruct((rows, cols), f32), jax.ShapeDtypeStruct((hops, HALO, LANES), f32)],
        scratch_shapes=[
            pltpu.VMEM((tiles, 2 * PAD + 2 * HALO + rows, LANES), f32),
            pltpu.VMEM((tiles + 2 * STEPS, rows, LANES), f32),
            pltpu.VMEM((PAIR, 2 * PAD + deep * NLON, LANES), f32),
            pltpu.VMEM((PAIR, 2 * PAD + deep * NLON, LANES), f32),
            pltpu.VMEM((5, slack, LANES), f32),
            pltpu.VMEM((5, lines + 2 * edge, NLON, LANES), f32),
            pltpu.VMEM((5, wide, LANES), f32),
            pltpu.SemaphoreType.DMA((tiles,)),
            pltpu.SemaphoreType.DMA((tiles,)),
            pltpu.SemaphoreType.DMA((tiles,)),
            pltpu.SemaphoreType.DMA((tiles,)),
            pltpu.SemaphoreType.DMA((tiles,)),
            pltpu.SemaphoreType.DMA((hops,)),
            pltpu.SemaphoreType.DMA((hops,)),
            pltpu.SemaphoreType.DMA((6,)),
            pltpu.SemaphoreType.DMA((6,)),
            pltpu.SemaphoreType.DMA((3, tiles)),
        ],
        compiler_params=pltpu.CompilerParams(collective_id=0, has_side_effects=True, vmem_limit_bytes=64 * 1024 * 1024),
    )(covariance, east_wind, north_wind, diffuse_lon, diffuse_lat)
    return out


def solution(mesh):
    row_devices, col_devices = mesh.shape["row"], mesh.shape["col"]

    def run(covariance, *tables):
        lines, tiles = covariance.shape[0] // NLON, covariance.shape[1] // NLON
        if lines > 2 * STEPS and tiles >= 4 * STEPS and (tiles - 2 * STEPS) % PAIR == 0:
            return fused_body(row_devices, col_devices, covariance, *tables)
        return body(covariance, *tables)

    return jax.shard_map(
        run,
        mesh=mesh,
        in_specs=(P("row", "col"), P(), P(), P(), P()),
        out_specs=P("row", "col"),
        check_vma=False,
    )
```

```python
import functools

import jax
import jax.numpy as jnp
from jax import lax
from jax.experimental import pallas as pl
from jax.experimental.pallas import tpu as pltpu
from jax.sharding import PartitionSpec as P

NLON = 128
STEPS = 3
UNIT = STEPS * NLON
WIDE = 256
BLOCK = 192
VMEM = 52 * 1024 * 1024


OFFSETS = [(y, x) for y in range(-STEPS, STEPS + 1) for x in range(-STEPS + abs(y), STEPS + 1 - abs(y))]


def power_kernel(east_wind, north_wind, diffuse_lon, diffuse_lat, plain, rolled):
    lon, lat = diffuse_lon[...], diffuse_lat[...]
    half_east, half_north = 0.5 * east_wind[...], 0.5 * north_wind[...]
    one = {
        (0, 0): 1.0 - 2.0 * lon - 2.0 * lat,
        (0, 1): lon - half_east,
        (0, -1): lon + half_east,
        (1, 0): lat - half_north,
        (-1, 0): lat + half_north,
    }
    lines = lon.shape[0]
    line = lax.broadcasted_iota(jnp.int32, lon.shape, 0)

    def seen(field, y, x):
        if x:
            return pltpu.roll(field, -x % NLON, 1)
        if y:
            edge = lines - 1 if y > 0 else 0
            return jnp.where(line == edge, 0.0, pltpu.roll(field, -y % lines, 0))
        return field

    power = dict(one)
    for _ in range(STEPS - 1):
        made = {}
        for (y, x), field in power.items():
            for (sy, sx), scale in one.items():
                term = scale * seen(field, sy, sx)
                at = (y + sy, x + sx)
                made[at] = made[at] + term if at in made else term
        power = made
    for k, (y, x) in enumerate(OFFSETS):
        plain[k] = power[y, x]
        rolled[k] = pltpu.roll(power[y, x], x % NLON, 1)


def powers(tables):
    shape = jax.ShapeDtypeStruct((len(OFFSETS),) + tables[0].shape, jnp.float32)
    return pl.pallas_call(
        power_kernel,
        out_shape=(shape, shape),
        compiler_params=pltpu.CompilerParams(vmem_limit_bytes=VMEM),
        cost_estimate=pl.CostEstimate(flops=10**7, bytes_accessed=10**7, transcendentals=0),
    )(*tables)


def split(value):
    high = value.astype(jnp.bfloat16)
    return high, (value - high.astype(jnp.float32)).astype(jnp.bfloat16)


def block_kernel(made, transposed, offset, table, out):
    base = offset[0] + pl.program_id(0) * made
    sub = lax.broadcasted_iota(jnp.int32, (NLON, NLON), 0)
    lane = lax.broadcasted_iota(jnp.int32, (NLON, NLON), 1)
    away = (sub - lane if transposed else lane - sub) & (NLON - 1)
    read = made + 2 * STEPS
    for a in range(made):
        for b in range(read):
            y = b - a - STEPS
            value = jnp.zeros((NLON, NLON), jnp.float32)
            for k, (oy, x) in enumerate(OFFSETS):
                if oy == y:
                    line = table[k, pl.ds(base + a, 1), :]
                    value = jnp.where(away == x % NLON, jnp.broadcast_to(line, (NLON, NLON)), value)
            high, low = split(value)
            mine, theirs = slice(a * NLON, (a + 1) * NLON), slice(b * NLON, (b + 1) * NLON)
            if transposed:
                out[0, theirs, mine] = high
                out[0, slice((read + b) * NLON, (read + b + 1) * NLON), mine] = low
            else:
                out[0, mine, theirs] = high
                out[0, slice((made + a) * NLON, (made + a + 1) * NLON), theirs] = low


def blocks_of(table, offset, groups, made, transposed):
    read = made + 2 * STEPS
    shape = (2 * read * NLON, made * NLON) if transposed else (2 * made * NLON, read * NLON)
    return pl.pallas_call(
        functools.partial(block_kernel, made, transposed),
        grid=(groups,),
        in_specs=[
            pl.BlockSpec(memory_space=pltpu.SMEM),
            pl.BlockSpec(table.shape, lambda i: (0, 0, 0)),
        ],
        out_specs=pl.BlockSpec((1,) + shape, lambda i: (i, 0, 0)),
        out_shape=jax.ShapeDtypeStruct((groups,) + shape, jnp.bfloat16),
        compiler_params=pltpu.CompilerParams(vmem_limit_bytes=VMEM),
        cost_estimate=pl.CostEstimate(flops=10**7, bytes_accessed=2 * 10**7, transcendentals=0),
    )(offset.reshape(1).astype(jnp.int32), table)


def dot(a, b):
    return jnp.dot(a, b, preferred_element_type=jnp.float32)


def stencil(c, east, west, north, south, coef):
    return coef[0] * c + coef[1] * east + coef[2] * west + coef[3] * north + coef[4] * south


def column_kernel(parts, sides, *refs):
    ins, tables, out = refs[: len(parts)], refs[len(parts)], refs[-1]
    for side, (names, first, count) in enumerate(sides):

        def source(line):
            part, at = divmod(line, STEPS)
            return ins[names[part]][at * NLON : (at + 1) * NLON, :]

        lines = count + 2 * STEPS
        got = {}
        for line in range(lines):
            got[0, line] = source(line)
            for step in range(1, STEPS + 1):
                mid = line - step
                if mid < step:
                    continue
                c = got[step - 1, mid]
                row = first + mid - 1
                value = stencil(
                    c,
                    pltpu.roll(c, NLON - 1, 0),
                    pltpu.roll(c, 1, 0),
                    got[step - 1, mid + 1],
                    got[step - 1, mid - 1],
                    [tables[k, row] for k in range(5)],
                )
                got.pop((step - 1, mid - 1))
                if step < STEPS:
                    got[step, mid] = value
                else:
                    at = sum(s[2] for s in sides[:side]) + mid - STEPS
                    out[at * NLON : (at + 1) * NLON, :] = value


def column_sweep(arrays, sides, width, coefs):
    total = sum(count for _, _, count in sides) * NLON
    in_specs = [
        pl.BlockSpec((UNIT, NLON), functools.partial(lambda i, r, c, skip: (r, jnp.where(i < UNIT // NLON, i + c, i + c + skip)), r=r, c=c, skip=skip)) for _, r, c, skip in arrays
    ]
    in_specs.append(pl.BlockSpec(coefs.shape, lambda i: (0, 0, 0, 0)))
    work = total * width
    return pl.pallas_call(
        functools.partial(column_kernel, arrays, sides),
        grid=(width // NLON,),
        in_specs=in_specs,
        out_specs=pl.BlockSpec((total, NLON), lambda i: (0, i)),
        out_shape=jax.ShapeDtypeStruct((total, width), jnp.float32),
        compiler_params=pltpu.CompilerParams(vmem_limit_bytes=VMEM),
        cost_estimate=pl.CostEstimate(flops=work * 40, bytes_accessed=work * 12, transcendentals=0),
    )(*[a[0] for a in arrays], coefs)


def row_kernel(count, *refs):
    ins, tables, out, both = refs[: count + 2], refs[count + 2], refs[-2], refs[-1]
    rows = out.shape[0]
    read = (2 + 2 * STEPS) * NLON
    for n, ref in enumerate(ins):
        cols = slice(n * UNIT, (n + 1) * UNIT)
        both[:rows, cols], both[rows:, cols] = split(ref[...])
    for pair in range(count * STEPS // 2):
        cols = slice(pair * 2 * NLON, pair * 2 * NLON + read)
        first = dot(both[:, cols], tables[pair, :read, :])
        other = dot(both[:rows, cols], tables[pair, read:, :])
        out[:, pair * 2 * NLON : (pair + 1) * 2 * NLON] = first[:rows] + (first[rows:] + other)


def row_sweep(arrays, part, tables, out_rows, row_block, out_cols, col_block, buffer):
    count = len(arrays) - 2
    rows = arrays[0][0].shape[0]
    pairs = count * STEPS // 2
    in_specs = [pl.BlockSpec((BLOCK, UNIT), functools.partial(lambda i, c: (i, c), c=c)) for _, c in arrays]
    in_specs.append(
        pl.BlockSpec((pairs,) + tables.shape[1:], lambda i: (part, 0, 0), pipeline_mode=pl.Buffered(1))
    )
    operands = [a for a, _ in arrays] + [tables]
    aliases = {}
    if buffer is not None:
        in_specs.append(pl.BlockSpec(memory_space=pl.ANY))
        operands.append(buffer)
        aliases = {len(operands) - 1: 0}
    work = rows * count * UNIT
    return pl.pallas_call(
        functools.partial(row_kernel, count),
        grid=(rows // BLOCK,),
        in_specs=in_specs,
        out_specs=pl.BlockSpec((BLOCK, count * UNIT), lambda i: (row_block(i), col_block)),
        out_shape=jax.ShapeDtypeStruct((out_rows, out_cols), jnp.float32),
        input_output_aliases=aliases,
        scratch_shapes=[pltpu.VMEM((2 * BLOCK, len(arrays) * UNIT), jnp.bfloat16)],
        compiler_params=pltpu.CompilerParams(vmem_limit_bytes=VMEM),
        cost_estimate=pl.CostEstimate(flops=work * 40, bytes_accessed=work * 12, transcendentals=0),
    )(*operands)


def exchange(first, last, axis):
    devices = lax.axis_size(axis)
    up = [(i, i + 1) for i in range(devices - 1)]
    down = [(j, i) for i, j in up]
    return lax.ppermute(last, axis, up), lax.ppermute(first, axis, down)


def coefficients(tables, offset, lines):
    east_wind, north_wind, diffuse_lon, diffuse_lat = tables
    made = jnp.stack(
        [
            1.0 - 2.0 * diffuse_lon - 2.0 * diffuse_lat,
            diffuse_lon - 0.5 * east_wind,
            diffuse_lon + 0.5 * east_wind,
            diffuse_lat - 0.5 * north_wind,
            diffuse_lat + 0.5 * north_wind,
        ]
    )
    edge = STEPS - 1
    made = jnp.pad(made, ((0, 0), (edge, edge), (0, 0)))
    return lax.dynamic_slice_in_dim(made, offset, lines + 2 * edge, 1)


def body(covariance, east_wind, north_wind, diffuse_lon, diffuse_lat):
    tables = (east_wind, north_wind, diffuse_lon, diffuse_lat)
    rows, cols = covariance.shape
    row_lines, col_lines = rows // NLON, cols // NLON
    row_units, col_units = rows // UNIT, cols // UNIT
    row_coefs = coefficients(tables, lax.axis_index("row") * row_lines, row_lines)
    row_coefs = jnp.broadcast_to(row_coefs[:, :, :, None], row_coefs.shape + (NLON,))
    plain, _ = powers(tables)
    col_tables = blocks_of(plain, lax.axis_index("col") * col_lines, col_lines // 2, 2, True)

    if col_units == 1:
        pieces = [[0]]
    else:
        pieces = [[0, col_units - 1]]
        half = col_units // 2
        if col_units % 2 == 0 and col_units >= 6:
            pieces += [list(range(1, half + 1)), list(range(half + 1, col_units - 1))]
        elif col_units > 2:
            pieces += [list(range(1, col_units - 1))]

    def columns(units, low, high):
        parts = []
        for u in units:
            if parts and parts[-1][1] == u:
                parts[-1][1] = u + 1
            else:
                parts.append([u, u + 1])
        return jnp.concatenate([covariance[low:high, a * UNIT : b * UNIT] for a, b in parts], axis=1)

    halos = [exchange(columns(p, 0, UNIT), columns(p, rows - UNIT, rows), "row") for p in pieces]

    inner = None
    if row_units > 2:
        inner = column_sweep(
            [(covariance, r, 0, 0) for r in range(row_units)],
            [(list(range(row_units)), STEPS, row_lines - 2 * STEPS)],
            cols,
            row_coefs,
        )

    outer = []
    where = {}
    for k, (units, (before, after)) in enumerate(zip(pieces, halos)):
        width = len(units) * UNIT
        skip = (cols - 2 * UNIT) // NLON if k == 0 and col_units > 1 else 0
        blocks = [(covariance, r, units[0] * (UNIT // NLON), skip) for r in range(row_units)]
        if row_units == 1:
            arrays = [(before, 0, 0, 0), blocks[0], (after, 0, 0, 0)]
            sides = [([0, 1, 2], 0, STEPS)]
        else:
            arrays = [(before, 0, 0, 0), blocks[0], blocks[1], blocks[-2], blocks[-1], (after, 0, 0, 0)]
            sides = [([0, 1, 2], 0, STEPS), ([3, 4, 5], row_lines - STEPS, STEPS)]
        outer.append(column_sweep(arrays, sides, width, row_coefs))
        for at, u in enumerate(units):
            where[u] = (k, at)

    out_blocks, tiles = rows // BLOCK, UNIT // BLOCK
    halves = [list(range(col_units))]
    if len(pieces) == 3:
        halves = [list(range(half)), list(range(half, col_units))]

    edges = outer[0]
    outer_halo = exchange(edges[:, :UNIT], edges[:, -UNIT:], "col")
    out = None
    if inner is not None:
        inner_halo = exchange(inner[:, :UNIT], inner[:, cols - UNIT :], "col")
        arrays = [(inner_halo[0], 0)] + [(inner, u) for u in range(col_units)] + [(inner_halo[1], 0)]
        out = row_sweep(arrays, 0, col_tables, rows, lambda i: i + tiles, cols, 0, out)

    def outer_row(i):
        return jnp.where(i < tiles, i, i + out_blocks - 2 * tiles) if row_units > 1 else i

    for h, units in enumerate(halves):
        arrays = []
        for u in [units[0] - 1] + units + [units[-1] + 1]:
            if u < 0:
                arrays.append((outer_halo[0], 0))
            elif u == col_units:
                arrays.append((outer_halo[1], 0))
            else:
                arrays.append((outer[where[u][0]], where[u][1]))
        out = row_sweep(arrays, h, col_tables, rows, outer_row, cols, h, out)
    return out


LANES = 128
SUBS = 8
PAD = 8
HALO = STEPS * NLON
PAIR = 2
RBLOCK = 96
PIECE = 192
MESH = pl.DeviceIdType.MESH


def tile_order(tiles):
    edges = list(range(STEPS)) + list(range(tiles - STEPS, tiles))
    return edges, list(range(STEPS, tiles - STEPS))


def detours(row_devices, tiles):
    if row_devices != 8:
        return None
    _, middle = tile_order(tiles)
    carried = [t for n, t in enumerate(middle) if n % 3]
    return dict(low=3, high=4, up_by=7, down_by=0, tiles=carried)


def fused_kernel(row_devices, col_devices, lines, tiles, cov, ew, nw, dlon, dlat, fwd, rtab, relay, big, one, two, pads, ctab,
                 load_sem, up_send, up_recv, down_send, down_recv, hop_send, hop_recv, z_send, z_recv):
    r, c = lax.axis_index("row"), lax.axis_index("col")
    rows = lines * NLON
    edges, middle = tile_order(tiles)
    detour = detours(row_devices, tiles)
    carried = detour["tiles"] if detour else []
    has_up, has_down = r < row_devices - 1, r > 0
    has_right, has_left = c < col_devices - 1, c > 0

    partners = [(has_up, {"row": jnp.minimum(r + 1, row_devices - 1)}), (has_down, {"row": jnp.maximum(r - 1, 0)})]
    partners += [(has_right, {"col": jnp.minimum(c + 1, col_devices - 1)}), (has_left, {"col": jnp.maximum(c - 1, 0)})]
    if detour:
        for a in (detour["low"], detour["high"]):
            for b in (detour["up_by"], detour["down_by"]):
                partners += [(r == a, {"row": b}), (r == b, {"row": a})]
    barrier = pltpu.get_barrier_semaphore()
    count = 0
    for there, place in partners:
        count = count + there.astype(jnp.int32)

        @pl.when(there)
        def _():
            pl.semaphore_signal(barrier, inc=1, device_id=place, device_id_type=MESH)

    def load(t):
        return pltpu.make_async_copy(cov.at[:, pl.ds(pl.multiple_of(t * LANES, LANES), LANES)], big.at[t, pl.ds(PAD + HALO, rows), :], load_sem.at[t])

    def lanes(t):
        return pl.ds(pl.multiple_of(t * LANES, LANES), LANES)

    top, bottom = pl.ds(0, HALO), pl.ds(rows - HALO, HALO)
    before, after = pl.ds(PAD, HALO), pl.ds(PAD + HALO + rows, HALO)

    def up(t):
        return pltpu.make_async_remote_copy(cov.at[bottom, lanes(t)], big.at[t, before, :], up_send.at[t], up_recv.at[t],
                                            device_id={"row": jnp.minimum(r + 1, row_devices - 1)}, device_id_type=MESH)

    def down(t):
        return pltpu.make_async_remote_copy(cov.at[top, lanes(t)], big.at[t, after, :], down_send.at[t], down_recv.at[t],
                                            device_id={"row": jnp.maximum(r - 1, 0)}, device_id_type=MESH)

    def up_first(k, t):
        return pltpu.make_async_remote_copy(cov.at[bottom, lanes(t)], relay.at[k], up_send.at[t], hop_recv.at[k],
                                            device_id={"row": detour["up_by"]}, device_id_type=MESH)

    def down_first(k, t):
        return pltpu.make_async_remote_copy(cov.at[top, lanes(t)], relay.at[k], down_send.at[t], hop_recv.at[k],
                                            device_id={"row": detour["down_by"]}, device_id_type=MESH)

    def up_second(k, t):
        return pltpu.make_async_remote_copy(relay.at[k], big.at[t, before, :], hop_send.at[k], up_recv.at[t],
                                            device_id={"row": detour["high"]}, device_id_type=MESH)

    def down_second(k, t):
        return pltpu.make_async_remote_copy(relay.at[k], big.at[t, after, :], hop_send.at[k], down_recv.at[t],
                                            device_id={"row": detour["low"]}, device_id_type=MESH)

    for t in edges:
        load(t).start()
    pl.semaphore_wait(barrier, count)

    for t in edges + middle:
        if t in carried:
            k = carried.index(t)
            low, high = r == detour["low"], r == detour["high"]

            @pl.when(low)
            def _():
                up_first(k, t).start()

            @pl.when(high)
            def _():
                down_first(k, t).start()
        else:
            low = high = r < 0

        @pl.when(has_up & ~low)
        def _():
            up(t).start()

        @pl.when(has_down & ~high)
        def _():
            down(t).start()
    for t in middle:
        load(t).start()

    def relay_step(k):
        t = carried[k]

        @pl.when(r == detour["up_by"])
        def _():
            up_first(k, t).wait_recv()
            up_second(k, t).start()

        @pl.when(r == detour["down_by"])
        def _():
            down_first(k, t).wait_recv()
            down_second(k, t).start()

    east_wind, north_wind, lon, lat = ew[...], nw[...], dlon[...], dlat[...]
    half_east, half_north = 0.5 * east_wind, 0.5 * north_wind
    made = [1.0 - 2.0 * lon - 2.0 * lat, lon - half_east, lon + half_east, lat - half_north, lat + half_north]
    grid_lines = lon.shape[0]
    edge = STEPS - 1
    spread = -(-(lines + 2 * edge) // SUBS) * SUBS
    for k, table in enumerate(made):
        pads[k, pl.ds(0, PAD), :] = jnp.zeros((PAD, LANES), jnp.float32)
        pads[k, pl.ds(PAD, grid_lines), :] = table
        pads[k, pl.ds(PAD + grid_lines, spread), :] = jnp.zeros((spread, LANES), jnp.float32)
    wide = -(-(tiles + 2 * edge) // SUBS) * SUBS
    for k in range(len(made)):
        rtab[k] = pads[k, pl.ds(c * tiles + PAD - edge, wide), :]
        mine = pads[k, pl.ds(r * lines + PAD - edge, spread), :]
        turned = jnp.transpose(jnp.concatenate([mine, jnp.zeros((LANES - spread, LANES), jnp.float32)], axis=0))
        for i in range(lines + 2 * edge):
            ctab[k, i] = jnp.broadcast_to(turned[:, i : i + 1], (NLON, LANES))

    @pl.when(~has_down)
    def _():
        def clear(t, _):
            big[t, before, :] = jnp.zeros((HALO, LANES), jnp.float32)
            return 0
        lax.fori_loop(0, tiles, clear, 0)

    @pl.when(~has_up)
    def _():
        def clear(t, _):
            big[t, after, :] = jnp.zeros((HALO, LANES), jnp.float32)
            return 0
        lax.fori_loop(0, tiles, clear, 0)

    @pl.when(~has_left)
    def _():
        fwd[pl.ds(0, STEPS)] = jnp.zeros((STEPS, rows, LANES), jnp.float32)

    @pl.when(~has_right)
    def _():
        fwd[pl.ds(tiles + STEPS, STEPS)] = jnp.zeros((STEPS, rows, LANES), jnp.float32)

    sub = lax.broadcasted_iota(jnp.int32, (SUBS, LANES), 0)

    def line_step(pair, line, source, stores, keeps=()):
        for g in range(NLON // SUBS):
            at = g * SUBS
            coef = [ctab[k, line - 1, pl.ds(at, SUBS), :] for k in range(5)]
            for n in range(len(pair)):

                def read(d, shift=0, count=SUBS):
                    ref, base = source(n, d)
                    return ref[pl.ds(pl.multiple_of(base, SUBS) + shift, count), :]

                def write(place, value):
                    ref, base = place
                    ref[pl.ds(pl.multiple_of(base + at, SUBS), SUBS), :] = value

                seen = {d: read(d, at) for d in (-1, 0, 1)}
                east, west = read(0, at + 1), read(0, at - 1)
                if g == NLON // SUBS - 1:
                    east = jnp.where(sub == SUBS - 1, read(0, 0, 1), east)
                if g == 0:
                    west = jnp.where(sub == 0, read(0, NLON - 1, 1), west)
                value = (coef[0] * seen[0] + coef[1] * east) + (coef[2] * west + coef[3] * seen[1]) + coef[4] * seen[-1]
                for place in stores(n):
                    write(place, value)
                for d, place in keeps:
                    write(place(n), seen[d])

    def in_big(pair, n, slot):
        return big.at[pair[n]], PAD + slot * NLON

    def in_fwd(pair, n, line):
        return fwd.at[pair[n] + STEPS], (line - STEPS) * NLON

    def inner_columns(pair):
        kept_one = {4: 5, 5: 6, lines: lines - 1, lines + 1: lines}
        kept_two = {5: 7, 6: 8, lines - 1: lines - 3, lines: lines - 2}

        def at_one(n, line):
            return one.at[n], PAD + (line - 4) * NLON

        def at_two(n, line):
            return two.at[n], PAD + (line - 5) * NLON

        def step1(line, _):
            line_step(pair, line, lambda n, d: in_big(pair, n, line + d), lambda n: [at_one(n, line)])
            return 0

        def step2(line, keep):
            places = lambda n: [at_two(n, line)] + ([in_big(pair, n, kept_two[line])] if keep else [])
            keeps = [(d, functools.partial(lambda n, slot: in_big(pair, n, slot), slot=kept_one[line + d]))
                     for d in ((-1, 0) if line == 5 else (0, 1))] if keep and line in (5, lines) else []
            line_step(pair, line, lambda n, d: at_one(n, line + d), places, keeps)

        def step2_plain(line, _):
            step2(line, False)
            return 0

        def step3(line, _):
            line_step(pair, line, lambda n, d: at_two(n, line + d), lambda n: [in_fwd(pair, n, line)])
            return 0

        lax.fori_loop(4, lines + 2, step1, 0)
        step2(5, True)
        step2(6, True)
        lax.fori_loop(7, lines - 1, step2_plain, 0)
        step2(lines - 1, True)
        step2(lines, True)
        lax.fori_loop(6, lines, step3, 0)

    def outer_columns(pair, south):
        ones = [("one", k) for k in range(STEPS)]
        twos = [("two", k) for k in range(STEPS)]
        if south:
            first = [lines + 2, lines + 1, lines]
            after_one = [("big", lines - 1), ("big", lines)] + ones
            after_two = [("big", lines - 3), ("big", lines - 2)] + twos
        else:
            first = [1, 2, 3]
            after_one = ones + [("big", 5), ("big", 6)]
            after_two = twos + [("big", 7), ("big", 8)]

        def place(n, where):
            name, k = where
            if name == "big":
                return in_big(pair, n, k)
            return (one if name == "one" else two).at[n], PAD + k * NLON

        for k in range(STEPS):
            line = first[0] + k
            line_step(pair, line, lambda n, d: in_big(pair, n, line + d), lambda n: [place(n, ones[k])])
        for k in range(STEPS):
            line_step(pair, first[1] + k, lambda n, d: place(n, after_one[k + 1 + d]), lambda n: [place(n, twos[k])])
        for k in range(STEPS):
            line = first[2] + k
            line_step(pair, line, lambda n, d: place(n, after_two[k + 1 + d]), lambda n: [in_fwd(pair, n, line)])

    odd = r % 2 == 1
    quick, slow = odd_rows(odd, rows)

    def quick_columns(pair):
        @pl.when(odd)
        def _():
            for t in pair:
                up(t).wait_recv()
            outer_columns(pair, False)

        @pl.when(~odd)
        def _():
            for t in pair:
                down(t).wait_recv()
            outer_columns(pair, True)

    def slow_columns(pair):
        @pl.when(odd)
        def _():
            @pl.when(has_up)
            def _():
                for t in pair:
                    down(t).wait_recv()
            outer_columns(pair, True)

        @pl.when(~odd)
        def _():
            @pl.when(has_down)
            def _():
                for t in pair:
                    up(t).wait_recv()
            outer_columns(pair, False)

    pieces = (rows - 2 * HALO) // PIECE
    side = HALO // PIECE

    def piece_start(part):
        on_quick, on_slow = quick + (part - pieces) * PIECE, slow + (part - pieces - side) * PIECE
        start = jnp.where(part < pieces, HALO + part * PIECE, jnp.where(part < pieces + side, on_quick, on_slow))
        return pl.multiple_of(start, PIECE)

    def z_copy(part, right):
        where = pl.ds(piece_start(part), PIECE)
        first, there = (tiles, 0) if right else (STEPS, tiles + STEPS)
        other = jnp.minimum(c + 1, col_devices - 1) if right else jnp.maximum(c - 1, 0)
        n = 2 * part + (1 if right else 0)
        return pltpu.make_async_remote_copy(fwd.at[pl.ds(first, STEPS), where, :], fwd.at[pl.ds(there, STEPS), where, :],
                                            z_send.at[n], z_recv.at[n], device_id={"col": other}, device_id_type=MESH)

    def z_start(part, _):
        @pl.when(has_right)
        def _():
            z_copy(part, True).start()

        @pl.when(has_left)
        def _():
            z_copy(part, False).start()
        return 0

    def z_wait(part, _):
        @pl.when(has_right)
        def _():
            z_copy(part, True).wait_send()
            z_copy(part, False).wait_recv()

        @pl.when(has_left)
        def _():
            z_copy(part, False).wait_send()
            z_copy(part, True).wait_recv()
        return 0

    def pair_of(i):
        got = []
        for n in range(PAIR):
            m = i * PAIR + n
            got.append(jnp.where(m < 2 * STEPS, m + (m // STEPS) * (tiles - 2 * STEPS), m - STEPS))
        return got

    edge_pairs, all_pairs = 2 * STEPS // PAIR, tiles // PAIR

    def early(i, _):
        pair = pair_of(i)
        for t in pair:
            load(t).wait()
        inner_columns(pair)
        quick_columns(pair)

        @pl.when(i == edge_pairs - 1)
        def _():
            lax.fori_loop(0, pieces + side, z_start, 0)

        if detour:
            for k in range(len(carried)):
                @pl.when(i == k * all_pairs // len(carried))
                def _():
                    relay_step(k)
        return 0

    lax.fori_loop(0, all_pairs, early, 0)

    def keep(tile, at, value):
        fwd[tile, pl.ds(at, RBLOCK), :] = value

    def ready_rows(part, _):
        z_wait(part, 0)
        row_pass(fwd, rtab, 0, tiles, piece_start(part), PIECE, keep)
        return 0

    groups = slow_groups(all_pairs - edge_pairs)
    stops = []
    at = edge_pairs
    for n in groups[:-1]:
        at += n
        stops.append(at)

    def late(i, _):
        slow_columns(pair_of(i))

        @pl.when(i == edge_pairs - 1)
        def _():
            lax.fori_loop(pieces + side, pieces + 2 * side, z_start, 0)
            lax.fori_loop(0, pieces + side, ready_rows, 0)

        done = 0
        for n, stop in enumerate(stops):
            upto = stop * PAIR - 2 * STEPS

            @pl.when(i == stop - 1)
            def _():
                if n == 0:
                    lax.fori_loop(pieces + side, pieces + 2 * side, z_wait, 0)
                row_pass(fwd, rtab, done, upto, slow, HALO, keep)
            done = upto
        return 0

    lax.fori_loop(0, all_pairs, late, 0)

    def sent(t, _):
        @pl.when(has_up)
        def _():
            up(t).wait_send()

        @pl.when(has_down)
        def _():
            down(t).wait_send()
        return 0

    lax.fori_loop(0, tiles, sent, 0)
    for k, t in enumerate(carried):
        @pl.when(r == detour["up_by"])
        def _():
            up_second(k, t).wait_send()

        @pl.when(r == detour["down_by"])
        def _():
            down_second(k, t).wait_send()


def slow_groups(pairs):
    groups = []
    while pairs > 3:
        groups.append(3)
        pairs -= 3
    return groups + [pairs - 1, 1] if pairs > 1 else groups + [pairs]


def rest(tiles):
    pairs = (tiles - 2 * STEPS) // PAIR
    return STEPS + (pairs - slow_groups(pairs)[-1]) * PAIR - STEPS


def odd_rows(odd, rows):
    return jnp.where(odd, 0, rows - HALO), jnp.where(odd, rows - HALO, 0)


def row_pass(fwd, rtab, a, b, start, count, store):
    edge = STEPS - 1

    def block(i, _):
        at = pl.multiple_of(start + i * RBLOCK, RBLOCK)
        got = {}
        for tile in range(a - STEPS, b + STEPS):
            got[0, tile] = fwd[tile + STEPS, pl.ds(at, RBLOCK), :]
            for step in range(1, STEPS + 1):
                mid = tile - step
                if mid < a - STEPS + step:
                    continue
                here = got[step - 1, mid]
                coef = [rtab[k, pl.ds(mid + edge, 1), :] for k in range(5)]
                value = (
                    (coef[0] * here + coef[1] * pltpu.roll(here, LANES - 1, 1))
                    + (coef[2] * pltpu.roll(here, 1, 1) + coef[3] * got[step - 1, mid + 1])
                    + coef[4] * got[step - 1, mid - 1]
                )
                got.pop((step - 1, mid - 1))
                if step < STEPS:
                    got[step, mid] = value
                else:
                    store(mid, at, value)
        return 0

    lax.fori_loop(0, count // RBLOCK, block, 0)


def finish_kernel(tiles, fwd, rtab, out, last, done_sem, slow_sem):
    rows = out.shape[0]
    begin = rest(tiles)
    quick, slow = odd_rows(lax.axis_index("row") % 2 == 1, rows)
    ready = pl.ds(pl.multiple_of(jnp.where(quick == 0, 0, HALO), SUBS), rows - HALO)
    late = pl.ds(pl.multiple_of(slow, SUBS), HALO)

    def lanes(t):
        return pl.ds(t * LANES, LANES)

    copies = [pltpu.make_async_copy(fwd.at[t, ready, :], out.at[ready, lanes(t)], done_sem.at[t]) for t in range(tiles)]
    copies += [pltpu.make_async_copy(fwd.at[t, late, :], out.at[late, lanes(t)], slow_sem.at[t]) for t in range(begin)]
    for copy in copies:
        copy.start()

    def keep(tile, at, value):
        last[tile - begin, pl.ds(pl.multiple_of(at - slow, SUBS), RBLOCK), :] = value

    row_pass(fwd, rtab, begin, tiles, slow, HALO, keep)
    ends = [pltpu.make_async_copy(last.at[t - begin], out.at[late, lanes(t)], slow_sem.at[t]) for t in range(begin, tiles)]
    for copy in ends:
        copy.start()
    for copy in copies + ends:
        copy.wait()


def fused_body(row_devices, col_devices, covariance, east_wind, north_wind, diffuse_lon, diffuse_lat):
    rows, cols = covariance.shape
    lines, tiles = rows // NLON, cols // NLON
    edge = STEPS - 1
    spread = -(-(lines + 2 * edge) // SUBS) * SUBS
    wide = -(-(tiles + 2 * edge) // SUBS) * SUBS
    slack = PAD + east_wind.shape[0] + max(spread, wide)
    detour = detours(row_devices, tiles)
    hops = len(detour["tiles"]) if detour else 1
    f32 = jnp.float32
    held = (tiles + 2 * STEPS, rows, LANES)
    room = 64 * 1024 * 1024 - 4 * held[0] * held[1] * held[2] - 1024 * 1024
    fwd, rtab, _ = pl.pallas_call(
        functools.partial(fused_kernel, row_devices, col_devices, lines, tiles),
        in_specs=[pl.BlockSpec(memory_space=pl.ANY)] + [pl.BlockSpec(memory_space=pltpu.VMEM)] * 4,
        out_specs=[pl.BlockSpec(memory_space=pltpu.VMEM)] * 2 + [pl.BlockSpec(memory_space=pl.ANY)],
        out_shape=[pltpu.VMEM(held, f32), jax.ShapeDtypeStruct((5, wide, LANES), f32), jax.ShapeDtypeStruct((hops, HALO, LANES), f32)],
        scratch_shapes=[
            pltpu.VMEM((tiles, 2 * PAD + 2 * HALO + rows, LANES), f32),
            pltpu.VMEM((PAIR, 2 * PAD + (lines - 2) * NLON, LANES), f32),
            pltpu.VMEM((PAIR, 2 * PAD + (lines - 4) * NLON, LANES), f32),
            pltpu.VMEM((5, slack, LANES), f32),
            pltpu.VMEM((5, lines + 2 * edge, NLON, LANES), f32),
            pltpu.SemaphoreType.DMA((tiles,)),
            pltpu.SemaphoreType.DMA((tiles,)),
            pltpu.SemaphoreType.DMA((tiles,)),
            pltpu.SemaphoreType.DMA((tiles,)),
            pltpu.SemaphoreType.DMA((tiles,)),
            pltpu.SemaphoreType.DMA((hops,)),
            pltpu.SemaphoreType.DMA((hops,)),
            pltpu.SemaphoreType.DMA((2 * rows // PIECE,)),
            pltpu.SemaphoreType.DMA((2 * rows // PIECE,)),
        ],
        compiler_params=pltpu.CompilerParams(collective_id=0, has_side_effects=True, vmem_limit_bytes=room),
    )(covariance, east_wind, north_wind, diffuse_lon, diffuse_lat)
    return pl.pallas_call(
        functools.partial(finish_kernel, tiles),
        in_specs=[pl.BlockSpec(memory_space=pltpu.VMEM)] * 2,
        out_specs=pl.BlockSpec(memory_space=pl.ANY),
        out_shape=jax.ShapeDtypeStruct((rows, cols), f32),
        scratch_shapes=[
            pltpu.VMEM((tiles - rest(tiles), HALO, LANES), f32),
            pltpu.SemaphoreType.DMA((tiles,)),
            pltpu.SemaphoreType.DMA((tiles,)),
        ],
        compiler_params=pltpu.CompilerParams(vmem_limit_bytes=room),
    )(pltpu.with_memory_space_constraint(fwd, pltpu.VMEM), rtab)


def solution(mesh):
    row_devices, col_devices = mesh.shape["row"], mesh.shape["col"]

    def run(covariance, *tables):
        lines, tiles = covariance.shape[0] // NLON, covariance.shape[1] // NLON
        if lines >= 4 * STEPS and tiles >= 4 * STEPS and (tiles - 2 * STEPS) % PAIR == 0:
            return fused_body(row_devices, col_devices, covariance, *tables)
        return body(covariance, *tables)

    return jax.shard_map(
        run,
        mesh=mesh,
        in_specs=(P("row", "col"), P(), P(), P(), P()),
        out_specs=P("row", "col"),
        check_vma=False,
    )
```

```python
import functools
import math

import jax
import jax.numpy as jnp
from jax import lax
from jax.experimental import pallas as pl
from jax.experimental.pallas import tpu as pltpu
from jax.sharding import PartitionSpec as P

NLON = 128
STEPS = 3
UNIT = STEPS * NLON
WIDE = 256
BLOCK = 192
VMEM = 52 * 1024 * 1024


OFFSETS = [(y, x) for y in range(-STEPS, STEPS + 1) for x in range(-STEPS + abs(y), STEPS + 1 - abs(y))]


def power_kernel(east_wind, north_wind, diffuse_lon, diffuse_lat, plain, rolled):
    lon, lat = diffuse_lon[...], diffuse_lat[...]
    half_east, half_north = 0.5 * east_wind[...], 0.5 * north_wind[...]
    one = {
        (0, 0): 1.0 - 2.0 * lon - 2.0 * lat,
        (0, 1): lon - half_east,
        (0, -1): lon + half_east,
        (1, 0): lat - half_north,
        (-1, 0): lat + half_north,
    }
    lines = lon.shape[0]
    line = lax.broadcasted_iota(jnp.int32, lon.shape, 0)

    def seen(field, y, x):
        if x:
            return pltpu.roll(field, -x % NLON, 1)
        if y:
            edge = lines - 1 if y > 0 else 0
            return jnp.where(line == edge, 0.0, pltpu.roll(field, -y % lines, 0))
        return field

    power = dict(one)
    for _ in range(STEPS - 1):
        made = {}
        for (y, x), field in power.items():
            for (sy, sx), scale in one.items():
                term = scale * seen(field, sy, sx)
                at = (y + sy, x + sx)
                made[at] = made[at] + term if at in made else term
        power = made
    for k, (y, x) in enumerate(OFFSETS):
        plain[k] = power[y, x]
        rolled[k] = pltpu.roll(power[y, x], x % NLON, 1)


def powers(tables):
    shape = jax.ShapeDtypeStruct((len(OFFSETS),) + tables[0].shape, jnp.float32)
    return pl.pallas_call(
        power_kernel,
        out_shape=(shape, shape),
        compiler_params=pltpu.CompilerParams(vmem_limit_bytes=VMEM),
        cost_estimate=pl.CostEstimate(flops=10**7, bytes_accessed=10**7, transcendentals=0),
    )(*tables)


def split(value):
    high = value.astype(jnp.bfloat16)
    return high, (value - high.astype(jnp.float32)).astype(jnp.bfloat16)


def block_kernel(made, transposed, offset, table, out):
    base = offset[0] + pl.program_id(0) * made
    sub = lax.broadcasted_iota(jnp.int32, (NLON, NLON), 0)
    lane = lax.broadcasted_iota(jnp.int32, (NLON, NLON), 1)
    away = (sub - lane if transposed else lane - sub) & (NLON - 1)
    read = made + 2 * STEPS
    for a in range(made):
        for b in range(read):
            y = b - a - STEPS
            value = jnp.zeros((NLON, NLON), jnp.float32)
            for k, (oy, x) in enumerate(OFFSETS):
                if oy == y:
                    line = table[k, pl.ds(base + a, 1), :]
                    value = jnp.where(away == x % NLON, jnp.broadcast_to(line, (NLON, NLON)), value)
            high, low = split(value)
            mine, theirs = slice(a * NLON, (a + 1) * NLON), slice(b * NLON, (b + 1) * NLON)
            if transposed:
                out[0, theirs, mine] = high
                out[0, slice((read + b) * NLON, (read + b + 1) * NLON), mine] = low
            else:
                out[0, mine, theirs] = high
                out[0, slice((made + a) * NLON, (made + a + 1) * NLON), theirs] = low


def blocks_of(table, offset, groups, made, transposed):
    read = made + 2 * STEPS
    shape = (2 * read * NLON, made * NLON) if transposed else (2 * made * NLON, read * NLON)
    return pl.pallas_call(
        functools.partial(block_kernel, made, transposed),
        grid=(groups,),
        in_specs=[
            pl.BlockSpec(memory_space=pltpu.SMEM),
            pl.BlockSpec(table.shape, lambda i: (0, 0, 0)),
        ],
        out_specs=pl.BlockSpec((1,) + shape, lambda i: (i, 0, 0)),
        out_shape=jax.ShapeDtypeStruct((groups,) + shape, jnp.bfloat16),
        compiler_params=pltpu.CompilerParams(vmem_limit_bytes=VMEM),
        cost_estimate=pl.CostEstimate(flops=10**7, bytes_accessed=2 * 10**7, transcendentals=0),
    )(offset.reshape(1).astype(jnp.int32), table)


def dot(a, b):
    return jnp.dot(a, b, preferred_element_type=jnp.float32)


def stencil(c, east, west, north, south, coef):
    return coef[0] * c + coef[1] * east + coef[2] * west + coef[3] * north + coef[4] * south


def column_kernel(parts, sides, *refs):
    ins, tables, out = refs[: len(parts)], refs[len(parts)], refs[-1]
    for side, (names, first, count) in enumerate(sides):

        def source(line):
            part, at = divmod(line, STEPS)
            return ins[names[part]][at * NLON : (at + 1) * NLON, :]

        lines = count + 2 * STEPS
        got = {}
        for line in range(lines):
            got[0, line] = source(line)
            for step in range(1, STEPS + 1):
                mid = line - step
                if mid < step:
                    continue
                c = got[step - 1, mid]
                row = first + mid - 1
                value = stencil(
                    c,
                    pltpu.roll(c, NLON - 1, 0),
                    pltpu.roll(c, 1, 0),
                    got[step - 1, mid + 1],
                    got[step - 1, mid - 1],
                    [tables[k, row] for k in range(5)],
                )
                got.pop((step - 1, mid - 1))
                if step < STEPS:
                    got[step, mid] = value
                else:
                    at = sum(s[2] for s in sides[:side]) + mid - STEPS
                    out[at * NLON : (at + 1) * NLON, :] = value


def column_sweep(arrays, sides, width, coefs):
    total = sum(count for _, _, count in sides) * NLON
    in_specs = [
        pl.BlockSpec((UNIT, NLON), functools.partial(lambda i, r, c, skip: (r, jnp.where(i < UNIT // NLON, i + c, i + c + skip)), r=r, c=c, skip=skip)) for _, r, c, skip in arrays
    ]
    in_specs.append(pl.BlockSpec(coefs.shape, lambda i: (0, 0, 0, 0)))
    work = total * width
    return pl.pallas_call(
        functools.partial(column_kernel, arrays, sides),
        grid=(width // NLON,),
        in_specs=in_specs,
        out_specs=pl.BlockSpec((total, NLON), lambda i: (0, i)),
        out_shape=jax.ShapeDtypeStruct((total, width), jnp.float32),
        compiler_params=pltpu.CompilerParams(vmem_limit_bytes=VMEM),
        cost_estimate=pl.CostEstimate(flops=work * 40, bytes_accessed=work * 12, transcendentals=0),
    )(*[a[0] for a in arrays], coefs)


def row_kernel(count, *refs):
    ins, tables, out, both = refs[: count + 2], refs[count + 2], refs[-2], refs[-1]
    rows = out.shape[0]
    read = (2 + 2 * STEPS) * NLON
    for n, ref in enumerate(ins):
        cols = slice(n * UNIT, (n + 1) * UNIT)
        both[:rows, cols], both[rows:, cols] = split(ref[...])
    for pair in range(count * STEPS // 2):
        cols = slice(pair * 2 * NLON, pair * 2 * NLON + read)
        first = dot(both[:, cols], tables[pair, :read, :])
        other = dot(both[:rows, cols], tables[pair, read:, :])
        out[:, pair * 2 * NLON : (pair + 1) * 2 * NLON] = first[:rows] + (first[rows:] + other)


def row_sweep(arrays, part, tables, out_rows, row_block, out_cols, col_block, buffer):
    count = len(arrays) - 2
    rows = arrays[0][0].shape[0]
    pairs = count * STEPS // 2
    in_specs = [pl.BlockSpec((BLOCK, UNIT), functools.partial(lambda i, c: (i, c), c=c)) for _, c in arrays]
    in_specs.append(
        pl.BlockSpec((pairs,) + tables.shape[1:], lambda i: (part, 0, 0), pipeline_mode=pl.Buffered(1))
    )
    operands = [a for a, _ in arrays] + [tables]
    aliases = {}
    if buffer is not None:
        in_specs.append(pl.BlockSpec(memory_space=pl.ANY))
        operands.append(buffer)
        aliases = {len(operands) - 1: 0}
    work = rows * count * UNIT
    return pl.pallas_call(
        functools.partial(row_kernel, count),
        grid=(rows // BLOCK,),
        in_specs=in_specs,
        out_specs=pl.BlockSpec((BLOCK, count * UNIT), lambda i: (row_block(i), col_block)),
        out_shape=jax.ShapeDtypeStruct((out_rows, out_cols), jnp.float32),
        input_output_aliases=aliases,
        scratch_shapes=[pltpu.VMEM((2 * BLOCK, len(arrays) * UNIT), jnp.bfloat16)],
        compiler_params=pltpu.CompilerParams(vmem_limit_bytes=VMEM),
        cost_estimate=pl.CostEstimate(flops=work * 40, bytes_accessed=work * 12, transcendentals=0),
    )(*operands)


def exchange(first, last, axis):
    devices = lax.axis_size(axis)
    up = [(i, i + 1) for i in range(devices - 1)]
    down = [(j, i) for i, j in up]
    return lax.ppermute(last, axis, up), lax.ppermute(first, axis, down)


def coefficients(tables, offset, lines):
    east_wind, north_wind, diffuse_lon, diffuse_lat = tables
    made = jnp.stack(
        [
            1.0 - 2.0 * diffuse_lon - 2.0 * diffuse_lat,
            diffuse_lon - 0.5 * east_wind,
            diffuse_lon + 0.5 * east_wind,
            diffuse_lat - 0.5 * north_wind,
            diffuse_lat + 0.5 * north_wind,
        ]
    )
    edge = STEPS - 1
    made = jnp.pad(made, ((0, 0), (edge, edge), (0, 0)))
    return lax.dynamic_slice_in_dim(made, offset, lines + 2 * edge, 1)


def body(covariance, east_wind, north_wind, diffuse_lon, diffuse_lat):
    tables = (east_wind, north_wind, diffuse_lon, diffuse_lat)
    rows, cols = covariance.shape
    row_lines, col_lines = rows // NLON, cols // NLON
    row_units, col_units = rows // UNIT, cols // UNIT
    row_coefs = coefficients(tables, lax.axis_index("row") * row_lines, row_lines)
    row_coefs = jnp.broadcast_to(row_coefs[:, :, :, None], row_coefs.shape + (NLON,))
    plain, _ = powers(tables)
    col_tables = blocks_of(plain, lax.axis_index("col") * col_lines, col_lines // 2, 2, True)

    if col_units == 1:
        pieces = [[0]]
    else:
        pieces = [[0, col_units - 1]]
        half = col_units // 2
        if col_units % 2 == 0 and col_units >= 6:
            pieces += [list(range(1, half + 1)), list(range(half + 1, col_units - 1))]
        elif col_units > 2:
            pieces += [list(range(1, col_units - 1))]

    def columns(units, low, high):
        parts = []
        for u in units:
            if parts and parts[-1][1] == u:
                parts[-1][1] = u + 1
            else:
                parts.append([u, u + 1])
        return jnp.concatenate([covariance[low:high, a * UNIT : b * UNIT] for a, b in parts], axis=1)

    halos = [exchange(columns(p, 0, UNIT), columns(p, rows - UNIT, rows), "row") for p in pieces]

    inner = None
    if row_units > 2:
        inner = column_sweep(
            [(covariance, r, 0, 0) for r in range(row_units)],
            [(list(range(row_units)), STEPS, row_lines - 2 * STEPS)],
            cols,
            row_coefs,
        )

    outer = []
    where = {}
    for k, (units, (before, after)) in enumerate(zip(pieces, halos)):
        width = len(units) * UNIT
        skip = (cols - 2 * UNIT) // NLON if k == 0 and col_units > 1 else 0
        blocks = [(covariance, r, units[0] * (UNIT // NLON), skip) for r in range(row_units)]
        if row_units == 1:
            arrays = [(before, 0, 0, 0), blocks[0], (after, 0, 0, 0)]
            sides = [([0, 1, 2], 0, STEPS)]
        else:
            arrays = [(before, 0, 0, 0), blocks[0], blocks[1], blocks[-2], blocks[-1], (after, 0, 0, 0)]
            sides = [([0, 1, 2], 0, STEPS), ([3, 4, 5], row_lines - STEPS, STEPS)]
        outer.append(column_sweep(arrays, sides, width, row_coefs))
        for at, u in enumerate(units):
            where[u] = (k, at)

    out_blocks, tiles = rows // BLOCK, UNIT // BLOCK
    halves = [list(range(col_units))]
    if len(pieces) == 3:
        halves = [list(range(half)), list(range(half, col_units))]

    edges = outer[0]
    outer_halo = exchange(edges[:, :UNIT], edges[:, -UNIT:], "col")
    out = None
    if inner is not None:
        inner_halo = exchange(inner[:, :UNIT], inner[:, cols - UNIT :], "col")
        arrays = [(inner_halo[0], 0)] + [(inner, u) for u in range(col_units)] + [(inner_halo[1], 0)]
        out = row_sweep(arrays, 0, col_tables, rows, lambda i: i + tiles, cols, 0, out)

    def outer_row(i):
        return jnp.where(i < tiles, i, i + out_blocks - 2 * tiles) if row_units > 1 else i

    for h, units in enumerate(halves):
        arrays = []
        for u in [units[0] - 1] + units + [units[-1] + 1]:
            if u < 0:
                arrays.append((outer_halo[0], 0))
            elif u == col_units:
                arrays.append((outer_halo[1], 0))
            else:
                arrays.append((outer[where[u][0]], where[u][1]))
        out = row_sweep(arrays, h, col_tables, rows, outer_row, cols, h, out)
    return out


LANES = 128
SUBS = 8
PAD = 8
HALO = STEPS * NLON
PAIR = 2
RBLOCK = 96
PIECE = 192
MESH = pl.DeviceIdType.MESH


def tile_order(tiles):
    edges = list(range(STEPS)) + list(range(tiles - STEPS, tiles))
    return edges, list(range(STEPS, tiles - STEPS))


def detours(row_devices, tiles):
    if row_devices != 8:
        return None
    _, middle = tile_order(tiles)
    carried = [t for n, t in enumerate(middle) if n % 3]
    return dict(low=3, high=4, up_by=7, down_by=0, tiles=carried)


def line_step(ctab, pair, line, source, stores, keeps=()):
    sub = lax.broadcasted_iota(jnp.int32, (SUBS, LANES), 0)
    for g in range(NLON // SUBS):
        at = g * SUBS
        coef = [ctab[k, line - 1, pl.ds(at, SUBS), :] for k in range(5)]
        for n in range(len(pair)):

            def read(d, shift=0, count=SUBS):
                ref, base = source(n, d)
                return ref[pl.ds(pl.multiple_of(base, SUBS) + shift, count), :]

            def write(place, value):
                ref, base = place
                ref[pl.ds(pl.multiple_of(base + at, SUBS), SUBS), :] = value

            seen = {d: read(d, at) for d in (-1, 0, 1)}
            east, west = read(0, at + 1), read(0, at - 1)
            if g == NLON // SUBS - 1:
                east = jnp.where(sub == SUBS - 1, read(0, 0, 1), east)
            if g == 0:
                west = jnp.where(sub == 0, read(0, NLON - 1, 1), west)
            value = (coef[0] * seen[0] + coef[1] * east) + (coef[2] * west + coef[3] * seen[1]) + coef[4] * seen[-1]
            for place in stores(n):
                write(place, value)
            for d, place in keeps:
                write(place(n), seen[d])


def line_of(big, pair, n, slot):
    return big.at[pair[n]], PAD + slot * NLON


def outer_columns(big, ctab, one, two, lines, pair, south, result):
    ones = [("one", k) for k in range(STEPS)]
    twos = [("two", k) for k in range(STEPS)]
    if south:
        first = [lines + 2, lines + 1, lines]
        after_one = [("big", lines - 1), ("big", lines)] + ones
        after_two = [("big", lines - 3), ("big", lines - 2)] + twos
    else:
        first = [1, 2, 3]
        after_one = ones + [("big", 5), ("big", 6)]
        after_two = twos + [("big", 7), ("big", 8)]

    def place(n, where):
        name, k = where
        if name == "big":
            return line_of(big, pair, n, k)
        return (one if name == "one" else two).at[n], PAD + k * NLON

    for k in range(STEPS):
        line = first[0] + k
        line_step(ctab, pair, line, lambda n, d: line_of(big, pair, n, line + d), lambda n: [place(n, ones[k])])
    for k in range(STEPS):
        line_step(ctab, pair, first[1] + k, lambda n, d: place(n, after_one[k + 1 + d]), lambda n: [place(n, twos[k])])
    for k in range(STEPS):
        line = first[2] + k
        line_step(ctab, pair, line, lambda n, d: place(n, after_two[k + 1 + d]), lambda n: [result(n, line)])


def fused_kernel(row_devices, col_devices, lines, tiles, cov, ew, nw, dlon, dlat, fwd, rtab, big, ctab, relay, one, two, pads, winds,
                 wind_sem, load_sem, up_send, up_recv, down_send, down_recv, hop_send, hop_recv, z_send, z_recv):
    r, c = lax.axis_index("row"), lax.axis_index("col")
    rows = lines * NLON
    edges, middle = tile_order(tiles)
    detour = detours(row_devices, tiles)
    carried = detour["tiles"] if detour else []
    has_up, has_down = r < row_devices - 1, r > 0
    has_right, has_left = c < col_devices - 1, c > 0

    partners = [(has_up, {"row": jnp.minimum(r + 1, row_devices - 1)}), (has_down, {"row": jnp.maximum(r - 1, 0)})]
    partners += [(has_right, {"col": jnp.minimum(c + 1, col_devices - 1)}), (has_left, {"col": jnp.maximum(c - 1, 0)})]
    if detour:
        for a in (detour["low"], detour["high"]):
            for b in (detour["up_by"], detour["down_by"]):
                partners += [(r == a, {"row": b}), (r == b, {"row": a})]
    barrier = pltpu.get_barrier_semaphore()
    count = 0
    for there, place in partners:
        count = count + there.astype(jnp.int32)

        @pl.when(there)
        def _():
            pl.semaphore_signal(barrier, inc=1, device_id=place, device_id_type=MESH)

    def load(t):
        return pltpu.make_async_copy(cov.at[:, pl.ds(pl.multiple_of(t * LANES, LANES), LANES)], big.at[t, pl.ds(PAD + HALO, rows), :], load_sem.at[t])

    def lanes(t):
        return pl.ds(pl.multiple_of(t * LANES, LANES), LANES)

    top, bottom = pl.ds(0, HALO), pl.ds(rows - HALO, HALO)
    before, after = pl.ds(PAD, HALO), pl.ds(PAD + HALO + rows, HALO)

    def up(t):
        return pltpu.make_async_remote_copy(cov.at[bottom, lanes(t)], big.at[t, before, :], up_send.at[t], up_recv.at[t],
                                            device_id={"row": jnp.minimum(r + 1, row_devices - 1)}, device_id_type=MESH)

    def down(t):
        return pltpu.make_async_remote_copy(cov.at[top, lanes(t)], big.at[t, after, :], down_send.at[t], down_recv.at[t],
                                            device_id={"row": jnp.maximum(r - 1, 0)}, device_id_type=MESH)

    def up_first(k, t):
        return pltpu.make_async_remote_copy(cov.at[bottom, lanes(t)], relay.at[k], up_send.at[t], hop_recv.at[k],
                                            device_id={"row": detour["up_by"]}, device_id_type=MESH)

    def down_first(k, t):
        return pltpu.make_async_remote_copy(cov.at[top, lanes(t)], relay.at[k], down_send.at[t], hop_recv.at[k],
                                            device_id={"row": detour["down_by"]}, device_id_type=MESH)

    def up_second(k, t):
        return pltpu.make_async_remote_copy(relay.at[k], big.at[t, before, :], hop_send.at[k], up_recv.at[t],
                                            device_id={"row": detour["high"]}, device_id_type=MESH)

    def down_second(k, t):
        return pltpu.make_async_remote_copy(relay.at[k], big.at[t, after, :], hop_send.at[k], down_recv.at[t],
                                            device_id={"row": detour["low"]}, device_id_type=MESH)

    wind_copies = [pltpu.make_async_copy(ref, winds.at[k], wind_sem.at[k]) for k, ref in enumerate((ew, nw, dlon, dlat))]
    for copy in wind_copies:
        copy.start()
    for t in edges:
        load(t).start()
    pl.semaphore_wait(barrier, count)

    odd = r % 2 == 1

    def send_slow(t):
        low = high = r < 0
        if t in carried:
            k = carried.index(t)
            low, high = r == detour["low"], r == detour["high"]

            @pl.when(low)
            def _():
                up_first(k, t).start()

            @pl.when(high)
            def _():
                down_first(k, t).start()

        @pl.when(odd & has_up & ~low)
        def _():
            up(t).start()

        @pl.when(~odd & has_down & ~high)
        def _():
            down(t).start()

    def send_quick(t):
        @pl.when(odd)
        def _():
            down(t).start()

        @pl.when(~odd)
        def _():
            up(t).start()

    for t in edges:
        send_slow(t)
    for t in edges:
        send_quick(t)
    for t in middle:
        send_slow(t)
    for t in middle:
        load(t).start()
    for t in middle:
        send_quick(t)

    def relay_step(k):
        t = carried[k]

        @pl.when(r == detour["up_by"])
        def _():
            up_first(k, t).wait_recv()
            up_second(k, t).start()

        @pl.when(r == detour["down_by"])
        def _():
            down_first(k, t).wait_recv()
            down_second(k, t).start()

    for copy in wind_copies:
        copy.wait()
    east_wind, north_wind, lon, lat = (winds[k] for k in range(4))
    half_east, half_north = 0.5 * east_wind, 0.5 * north_wind
    made = [1.0 - 2.0 * lon - 2.0 * lat, lon - half_east, lon + half_east, lat - half_north, lat + half_north]
    grid_lines = lon.shape[0]
    edge = STEPS - 1
    spread = -(-(lines + 2 * edge) // SUBS) * SUBS
    for k, table in enumerate(made):
        pads[k, pl.ds(0, PAD), :] = jnp.zeros((PAD, LANES), jnp.float32)
        pads[k, pl.ds(PAD, grid_lines), :] = table
        pads[k, pl.ds(PAD + grid_lines, spread), :] = jnp.zeros((spread, LANES), jnp.float32)
    wide = -(-(tiles + 2 * edge) // SUBS) * SUBS
    for k in range(len(made)):
        rtab[k] = pads[k, pl.ds(c * tiles + PAD - edge, wide), :]
        mine = pads[k, pl.ds(r * lines + PAD - edge, spread), :]
        turned = jnp.transpose(jnp.concatenate([mine, jnp.zeros((LANES - spread, LANES), jnp.float32)], axis=0))
        for i in range(lines + 2 * edge):
            ctab[k, i] = jnp.broadcast_to(turned[:, i : i + 1], (NLON, LANES))

    @pl.when(~has_down)
    def _():
        def clear(t, _):
            big[t, before, :] = jnp.zeros((HALO, LANES), jnp.float32)
            return 0
        lax.fori_loop(0, tiles, clear, 0)

    @pl.when(~has_up)
    def _():
        def clear(t, _):
            big[t, after, :] = jnp.zeros((HALO, LANES), jnp.float32)
            return 0
        lax.fori_loop(0, tiles, clear, 0)

    @pl.when(~has_left)
    def _():
        fwd[pl.ds(0, STEPS)] = jnp.zeros((STEPS, rows, LANES), jnp.float32)

    @pl.when(~has_right)
    def _():
        fwd[pl.ds(tiles + STEPS, STEPS)] = jnp.zeros((STEPS, rows, LANES), jnp.float32)

    def in_big(pair, n, slot):
        return line_of(big, pair, n, slot)

    def in_fwd(pair, n, line):
        return fwd.at[pair[n] + STEPS], (line - STEPS) * NLON

    def inner_columns(pair):
        kept_one = {4: 5, 5: 6, lines: lines - 1, lines + 1: lines}
        kept_two = {5: 7, 6: 8, lines - 1: lines - 3, lines: lines - 2}

        def at_one(n, line):
            return one.at[n], PAD + (line - 4) * NLON

        def at_two(n, line):
            return two.at[n], PAD + (line - 5) * NLON

        def step1(line, _):
            line_step(ctab, pair, line, lambda n, d: in_big(pair, n, line + d), lambda n: [at_one(n, line)])
            return 0

        def step2(line, keep):
            places = lambda n: [at_two(n, line)] + ([in_big(pair, n, kept_two[line])] if keep else [])
            keeps = [(d, functools.partial(lambda n, slot: in_big(pair, n, slot), slot=kept_one[line + d]))
                     for d in ((-1, 0) if line == 5 else (0, 1))] if keep and line in (5, lines) else []
            line_step(ctab, pair, line, lambda n, d: at_one(n, line + d), places, keeps)

        def step2_plain(line, _):
            step2(line, False)
            return 0

        def step3(line, _):
            line_step(ctab, pair, line, lambda n, d: at_two(n, line + d), lambda n: [in_fwd(pair, n, line)])
            return 0

        lax.fori_loop(4, lines + 2, step1, 0)
        step2(5, True)
        step2(6, True)
        lax.fori_loop(7, lines - 1, step2_plain, 0)
        step2(lines - 1, True)
        step2(lines, True)
        lax.fori_loop(6, lines, step3, 0)

    def outer(pair, south):
        outer_columns(big, ctab, one, two, lines, pair, south, lambda n, line: in_fwd(pair, n, line))

    quick, slow = odd_rows(odd, rows)

    def quick_columns(pair):
        @pl.when(odd)
        def _():
            for t in pair:
                up(t).wait_recv()
            outer(pair, False)

        @pl.when(~odd)
        def _():
            for t in pair:
                down(t).wait_recv()
            outer(pair, True)

    def slow_arrive(pair):
        @pl.when(odd & has_up)
        def _():
            for t in pair:
                down(t).wait_recv()

        @pl.when(~odd & has_down)
        def _():
            for t in pair:
                up(t).wait_recv()

    def slow_columns(pair):
        slow_arrive(pair)

        @pl.when(odd)
        def _():
            outer(pair, True)

        @pl.when(~odd)
        def _():
            outer(pair, False)

    pieces = (rows - 2 * HALO) // PIECE
    side = HALO // PIECE

    def piece_start(part):
        on_quick, on_slow = quick + (part - pieces) * PIECE, slow + (part - pieces - side) * PIECE
        start = jnp.where(part < pieces, HALO + part * PIECE, jnp.where(part < pieces + side, on_quick, on_slow))
        return pl.multiple_of(start, PIECE)

    def z_copy(part, right):
        where = pl.ds(piece_start(part), PIECE)
        first, there = (tiles, 0) if right else (STEPS, tiles + STEPS)
        other = jnp.minimum(c + 1, col_devices - 1) if right else jnp.maximum(c - 1, 0)
        n = 2 * part + (1 if right else 0)
        return pltpu.make_async_remote_copy(fwd.at[pl.ds(first, STEPS), where, :], fwd.at[pl.ds(there, STEPS), where, :],
                                            z_send.at[n], z_recv.at[n], device_id={"col": other}, device_id_type=MESH)

    def z_start(part, _):
        @pl.when(has_right)
        def _():
            z_copy(part, True).start()

        @pl.when(has_left)
        def _():
            z_copy(part, False).start()
        return 0

    def z_wait(part, _):
        @pl.when(has_right)
        def _():
            z_copy(part, True).wait_send()
            z_copy(part, False).wait_recv()

        @pl.when(has_left)
        def _():
            z_copy(part, False).wait_send()
            z_copy(part, True).wait_recv()
        return 0

    def pair_of(i):
        got = []
        for n in range(PAIR):
            m = i * PAIR + n
            got.append(jnp.where(m < 2 * STEPS, m + (m // STEPS) * (tiles - 2 * STEPS), m - STEPS))
        return got

    edge_pairs, all_pairs = 2 * STEPS // PAIR, tiles // PAIR

    def early(i, _):
        pair = pair_of(i)
        for t in pair:
            load(t).wait()
        inner_columns(pair)
        quick_columns(pair)

        @pl.when(i == edge_pairs - 1)
        def _():
            lax.fori_loop(0, pieces + side, z_start, 0)

        if detour:
            for k in range(len(carried)):
                @pl.when(i == k * all_pairs // len(carried))
                def _():
                    relay_step(k)
        return 0

    lax.fori_loop(0, all_pairs, early, 0)

    def held(tile, at):
        return fwd[tile + STEPS, pl.ds(at, RBLOCK), :]

    def keep(tile, at, value):
        fwd[tile, pl.ds(at, RBLOCK), :] = value

    def ready_rows(part, _):
        z_wait(part, 0)
        row_pass(held, rtab, 0, tiles, piece_start(part), PIECE, keep)
        return 0

    groups = slow_groups(all_pairs - edge_pairs)
    stops = []
    at = edge_pairs
    for n in groups[:-1]:
        at += n
        stops.append(at)

    def late(i, _):
        slow_columns(pair_of(i))

        @pl.when(i == edge_pairs - 1)
        def _():
            lax.fori_loop(pieces + side, pieces + 2 * side, z_start, 0)
            lax.fori_loop(0, pieces + side, ready_rows, 0)

        done = 0
        for n, stop in enumerate(stops):
            upto = stop * PAIR - 2 * STEPS

            @pl.when(i == stop - 1)
            def _():
                if n == 0:
                    lax.fori_loop(pieces + side, pieces + 2 * side, z_wait, 0)
                row_pass(held, rtab, done, upto, slow, HALO, keep)
            done = upto
        return 0

    lax.fori_loop(0, all_pairs - 1, late, 0)
    slow_arrive(pair_of(all_pairs - 1))

    def sent(t, _):
        @pl.when(has_up)
        def _():
            up(t).wait_send()

        @pl.when(has_down)
        def _():
            down(t).wait_send()
        return 0

    lax.fori_loop(0, tiles, sent, 0)
    for k, t in enumerate(carried):
        @pl.when(r == detour["up_by"])
        def _():
            up_second(k, t).wait_send()

        @pl.when(r == detour["down_by"])
        def _():
            down_second(k, t).wait_send()


def slow_groups(pairs):
    groups = []
    while pairs > 3:
        groups.append(3)
        pairs -= 3
    return groups + [pairs - 1, 1] if pairs > 1 else groups + [pairs]


def rest(tiles):
    pairs = (tiles - 2 * STEPS) // PAIR
    return STEPS + (pairs - slow_groups(pairs)[-1]) * PAIR - STEPS


def odd_rows(odd, rows):
    return jnp.where(odd, 0, rows - HALO), jnp.where(odd, rows - HALO, 0)


def row_pass(read, rtab, a, b, start, count, store):
    edge = STEPS - 1

    def block(i, _):
        at = pl.multiple_of(start + i * RBLOCK, RBLOCK)
        got = {}
        for tile in range(a - STEPS, b + STEPS):
            got[0, tile] = read(tile, at)
            for step in range(1, STEPS + 1):
                mid = tile - step
                if mid < a - STEPS + step:
                    continue
                here = got[step - 1, mid]
                coef = [rtab[k, pl.ds(mid + edge, 1), :] for k in range(5)]
                value = (
                    (coef[0] * here + coef[1] * pltpu.roll(here, LANES - 1, 1))
                    + (coef[2] * pltpu.roll(here, 1, 1) + coef[3] * got[step - 1, mid + 1])
                    + coef[4] * got[step - 1, mid - 1]
                )
                got.pop((step - 1, mid - 1))
                if step < STEPS:
                    got[step, mid] = value
                else:
                    store(mid, at, value)
        return 0

    lax.fori_loop(0, count // RBLOCK, block, 0)


def finish_kernel(tiles, fwd, rtab, big, ctab, out, last, ends, one, two, done_sem, slow_sem):
    rows = out.shape[0]
    lines = rows // NLON
    begin = rest(tiles)
    odd = lax.axis_index("row") % 2 == 1
    quick, slow = odd_rows(odd, rows)
    ready = pl.ds(pl.multiple_of(jnp.where(quick == 0, 0, HALO), SUBS), rows - HALO)
    late = pl.ds(pl.multiple_of(slow, SUBS), HALO)

    def lanes(t):
        return pl.ds(t * LANES, LANES)

    copies = [pltpu.make_async_copy(fwd.at[t, ready, :], out.at[ready, lanes(t)], done_sem.at[t]) for t in range(tiles)]
    copies += [pltpu.make_async_copy(fwd.at[t, late, :], out.at[late, lanes(t)], slow_sem.at[t]) for t in range(begin)]
    for copy in copies:
        copy.start()

    pair = [tiles - STEPS - PAIR + n for n in range(PAIR)]

    @pl.when(odd)
    def _():
        outer_columns(big, ctab, one, two, lines, pair, True, lambda n, line: (ends.at[n], (line - lines) * NLON))

    @pl.when(~odd)
    def _():
        outer_columns(big, ctab, one, two, lines, pair, False, lambda n, line: (ends.at[n], (line - STEPS) * NLON))

    def held(tile, at):
        if tile in pair:
            return ends[tile - pair[0], pl.ds(pl.multiple_of(at - slow, SUBS), RBLOCK), :]
        return fwd[tile + STEPS, pl.ds(at, RBLOCK), :]

    def keep(tile, at, value):
        last[tile - begin, pl.ds(pl.multiple_of(at - slow, SUBS), RBLOCK), :] = value

    row_pass(held, rtab, begin, tiles, slow, HALO, keep)
    copies_left = [pltpu.make_async_copy(last.at[t - begin], out.at[late, lanes(t)], slow_sem.at[t]) for t in range(begin, tiles)]
    for copy in copies_left:
        copy.start()
    for copy in copies + copies_left:
        copy.wait()


def fused_body(row_devices, col_devices, covariance, east_wind, north_wind, diffuse_lon, diffuse_lat):
    rows, cols = covariance.shape
    lines, tiles = rows // NLON, cols // NLON
    edge = STEPS - 1
    spread = -(-(lines + 2 * edge) // SUBS) * SUBS
    wide = -(-(tiles + 2 * edge) // SUBS) * SUBS
    slack = PAD + east_wind.shape[0] + max(spread, wide)
    detour = detours(row_devices, tiles)
    hops = len(detour["tiles"]) if detour else 1
    f32 = jnp.float32
    kept = [
        (tiles + 2 * STEPS, rows, LANES),
        (5, wide, LANES),
        (tiles, 2 * PAD + 2 * HALO + rows, LANES),
        (5, lines + 2 * edge, NLON, LANES),
    ]
    room = 64 * 1024 * 1024 - sum(4 * math.prod(shape) for shape in kept) - 1024 * 1024
    made = pl.pallas_call(
        functools.partial(fused_kernel, row_devices, col_devices, lines, tiles),
        in_specs=[pl.BlockSpec(memory_space=pl.ANY)] * 5,
        out_specs=[pl.BlockSpec(memory_space=pltpu.VMEM)] * len(kept) + [pl.BlockSpec(memory_space=pl.ANY)],
        out_shape=[pltpu.VMEM(shape, f32) for shape in kept] + [jax.ShapeDtypeStruct((hops, HALO, LANES), f32)],
        scratch_shapes=[
            pltpu.VMEM((PAIR, 2 * PAD + (lines - 2) * NLON, LANES), f32),
            pltpu.VMEM((PAIR, 2 * PAD + (lines - 4) * NLON, LANES), f32),
            pltpu.VMEM((5, slack, LANES), f32),
            pltpu.VMEM((4,) + east_wind.shape, f32),
            pltpu.SemaphoreType.DMA((4,)),
            pltpu.SemaphoreType.DMA((tiles,)),
            pltpu.SemaphoreType.DMA((tiles,)),
            pltpu.SemaphoreType.DMA((tiles,)),
            pltpu.SemaphoreType.DMA((tiles,)),
            pltpu.SemaphoreType.DMA((tiles,)),
            pltpu.SemaphoreType.DMA((hops,)),
            pltpu.SemaphoreType.DMA((hops,)),
            pltpu.SemaphoreType.DMA((2 * rows // PIECE,)),
            pltpu.SemaphoreType.DMA((2 * rows // PIECE,)),
        ],
        compiler_params=pltpu.CompilerParams(collective_id=0, has_side_effects=True, vmem_limit_bytes=room),
    )(covariance, east_wind, north_wind, diffuse_lon, diffuse_lat)
    return pl.pallas_call(
        functools.partial(finish_kernel, tiles),
        in_specs=[pl.BlockSpec(memory_space=pltpu.VMEM)] * len(kept),
        out_specs=pl.BlockSpec(memory_space=pl.ANY),
        out_shape=jax.ShapeDtypeStruct((rows, cols), f32),
        scratch_shapes=[
            pltpu.VMEM((tiles - rest(tiles), HALO, LANES), f32),
            pltpu.VMEM((PAIR, HALO, LANES), f32),
            pltpu.VMEM((PAIR, 2 * PAD + HALO, LANES), f32),
            pltpu.VMEM((PAIR, 2 * PAD + HALO, LANES), f32),
            pltpu.SemaphoreType.DMA((tiles,)),
            pltpu.SemaphoreType.DMA((tiles,)),
        ],
        compiler_params=pltpu.CompilerParams(vmem_limit_bytes=room),
    )(*[pltpu.with_memory_space_constraint(array, pltpu.VMEM) for array in made[: len(kept)]])


def solution(mesh):
    row_devices, col_devices = mesh.shape["row"], mesh.shape["col"]

    def run(covariance, *tables):
        lines, tiles = covariance.shape[0] // NLON, covariance.shape[1] // NLON
        if lines >= 4 * STEPS and tiles >= 4 * STEPS and (tiles - 2 * STEPS) % PAIR == 0:
            return fused_body(row_devices, col_devices, covariance, *tables)
        return body(covariance, *tables)

    return jax.shard_map(
        run,
        mesh=mesh,
        in_specs=(P("row", "col"), P(), P(), P(), P()),
        out_specs=P("row", "col"),
        check_vma=False,
    )
```

```python
import functools
import math

import jax
import jax.numpy as jnp
from jax import lax
from jax.experimental import pallas as pl
from jax.experimental.pallas import tpu as pltpu
from jax.sharding import PartitionSpec as P

NLON = 128
STEPS = 3
UNIT = STEPS * NLON
WIDE = 256
BLOCK = 192
VMEM = 52 * 1024 * 1024


OFFSETS = [(y, x) for y in range(-STEPS, STEPS + 1) for x in range(-STEPS + abs(y), STEPS + 1 - abs(y))]


def power_kernel(east_wind, north_wind, diffuse_lon, diffuse_lat, plain, rolled):
    lon, lat = diffuse_lon[...], diffuse_lat[...]
    half_east, half_north = 0.5 * east_wind[...], 0.5 * north_wind[...]
    one = {
        (0, 0): 1.0 - 2.0 * lon - 2.0 * lat,
        (0, 1): lon - half_east,
        (0, -1): lon + half_east,
        (1, 0): lat - half_north,
        (-1, 0): lat + half_north,
    }
    lines = lon.shape[0]
    line = lax.broadcasted_iota(jnp.int32, lon.shape, 0)

    def seen(field, y, x):
        if x:
            return pltpu.roll(field, -x % NLON, 1)
        if y:
            edge = lines - 1 if y > 0 else 0
            return jnp.where(line == edge, 0.0, pltpu.roll(field, -y % lines, 0))
        return field

    power = dict(one)
    for _ in range(STEPS - 1):
        made = {}
        for (y, x), field in power.items():
            for (sy, sx), scale in one.items():
                term = scale * seen(field, sy, sx)
                at = (y + sy, x + sx)
                made[at] = made[at] + term if at in made else term
        power = made
    for k, (y, x) in enumerate(OFFSETS):
        plain[k] = power[y, x]
        rolled[k] = pltpu.roll(power[y, x], x % NLON, 1)


def powers(tables):
    shape = jax.ShapeDtypeStruct((len(OFFSETS),) + tables[0].shape, jnp.float32)
    return pl.pallas_call(
        power_kernel,
        out_shape=(shape, shape),
        compiler_params=pltpu.CompilerParams(vmem_limit_bytes=VMEM),
        cost_estimate=pl.CostEstimate(flops=10**7, bytes_accessed=10**7, transcendentals=0),
    )(*tables)


def split(value):
    high = value.astype(jnp.bfloat16)
    return high, (value - high.astype(jnp.float32)).astype(jnp.bfloat16)


def block_kernel(made, transposed, offset, table, out):
    base = offset[0] + pl.program_id(0) * made
    sub = lax.broadcasted_iota(jnp.int32, (NLON, NLON), 0)
    lane = lax.broadcasted_iota(jnp.int32, (NLON, NLON), 1)
    away = (sub - lane if transposed else lane - sub) & (NLON - 1)
    read = made + 2 * STEPS
    for a in range(made):
        for b in range(read):
            y = b - a - STEPS
            value = jnp.zeros((NLON, NLON), jnp.float32)
            for k, (oy, x) in enumerate(OFFSETS):
                if oy == y:
                    line = table[k, pl.ds(base + a, 1), :]
                    value = jnp.where(away == x % NLON, jnp.broadcast_to(line, (NLON, NLON)), value)
            high, low = split(value)
            mine, theirs = slice(a * NLON, (a + 1) * NLON), slice(b * NLON, (b + 1) * NLON)
            if transposed:
                out[0, theirs, mine] = high
                out[0, slice((read + b) * NLON, (read + b + 1) * NLON), mine] = low
            else:
                out[0, mine, theirs] = high
                out[0, slice((made + a) * NLON, (made + a + 1) * NLON), theirs] = low


def blocks_of(table, offset, groups, made, transposed):
    read = made + 2 * STEPS
    shape = (2 * read * NLON, made * NLON) if transposed else (2 * made * NLON, read * NLON)
    return pl.pallas_call(
        functools.partial(block_kernel, made, transposed),
        grid=(groups,),
        in_specs=[
            pl.BlockSpec(memory_space=pltpu.SMEM),
            pl.BlockSpec(table.shape, lambda i: (0, 0, 0)),
        ],
        out_specs=pl.BlockSpec((1,) + shape, lambda i: (i, 0, 0)),
        out_shape=jax.ShapeDtypeStruct((groups,) + shape, jnp.bfloat16),
        compiler_params=pltpu.CompilerParams(vmem_limit_bytes=VMEM),
        cost_estimate=pl.CostEstimate(flops=10**7, bytes_accessed=2 * 10**7, transcendentals=0),
    )(offset.reshape(1).astype(jnp.int32), table)


def dot(a, b):
    return jnp.dot(a, b, preferred_element_type=jnp.float32)


def stencil(c, east, west, north, south, coef):
    return coef[0] * c + coef[1] * east + coef[2] * west + coef[3] * north + coef[4] * south


def column_kernel(parts, sides, *refs):
    ins, tables, out = refs[: len(parts)], refs[len(parts)], refs[-1]
    for side, (names, first, count) in enumerate(sides):

        def source(line):
            part, at = divmod(line, STEPS)
            return ins[names[part]][at * NLON : (at + 1) * NLON, :]

        lines = count + 2 * STEPS
        got = {}
        for line in range(lines):
            got[0, line] = source(line)
            for step in range(1, STEPS + 1):
                mid = line - step
                if mid < step:
                    continue
                c = got[step - 1, mid]
                row = first + mid - 1
                value = stencil(
                    c,
                    pltpu.roll(c, NLON - 1, 0),
                    pltpu.roll(c, 1, 0),
                    got[step - 1, mid + 1],
                    got[step - 1, mid - 1],
                    [tables[k, row] for k in range(5)],
                )
                got.pop((step - 1, mid - 1))
                if step < STEPS:
                    got[step, mid] = value
                else:
                    at = sum(s[2] for s in sides[:side]) + mid - STEPS
                    out[at * NLON : (at + 1) * NLON, :] = value


def column_sweep(arrays, sides, width, coefs):
    total = sum(count for _, _, count in sides) * NLON
    in_specs = [
        pl.BlockSpec((UNIT, NLON), functools.partial(lambda i, r, c, skip: (r, jnp.where(i < UNIT // NLON, i + c, i + c + skip)), r=r, c=c, skip=skip)) for _, r, c, skip in arrays
    ]
    in_specs.append(pl.BlockSpec(coefs.shape, lambda i: (0, 0, 0, 0)))
    work = total * width
    return pl.pallas_call(
        functools.partial(column_kernel, arrays, sides),
        grid=(width // NLON,),
        in_specs=in_specs,
        out_specs=pl.BlockSpec((total, NLON), lambda i: (0, i)),
        out_shape=jax.ShapeDtypeStruct((total, width), jnp.float32),
        compiler_params=pltpu.CompilerParams(vmem_limit_bytes=VMEM),
        cost_estimate=pl.CostEstimate(flops=work * 40, bytes_accessed=work * 12, transcendentals=0),
    )(*[a[0] for a in arrays], coefs)


def row_kernel(count, *refs):
    ins, tables, out, both = refs[: count + 2], refs[count + 2], refs[-2], refs[-1]
    rows = out.shape[0]
    read = (2 + 2 * STEPS) * NLON
    for n, ref in enumerate(ins):
        cols = slice(n * UNIT, (n + 1) * UNIT)
        both[:rows, cols], both[rows:, cols] = split(ref[...])
    for pair in range(count * STEPS // 2):
        cols = slice(pair * 2 * NLON, pair * 2 * NLON + read)
        first = dot(both[:, cols], tables[pair, :read, :])
        other = dot(both[:rows, cols], tables[pair, read:, :])
        out[:, pair * 2 * NLON : (pair + 1) * 2 * NLON] = first[:rows] + (first[rows:] + other)


def row_sweep(arrays, part, tables, out_rows, row_block, out_cols, col_block, buffer):
    count = len(arrays) - 2
    rows = arrays[0][0].shape[0]
    pairs = count * STEPS // 2
    in_specs = [pl.BlockSpec((BLOCK, UNIT), functools.partial(lambda i, c: (i, c), c=c)) for _, c in arrays]
    in_specs.append(
        pl.BlockSpec((pairs,) + tables.shape[1:], lambda i: (part, 0, 0), pipeline_mode=pl.Buffered(1))
    )
    operands = [a for a, _ in arrays] + [tables]
    aliases = {}
    if buffer is not None:
        in_specs.append(pl.BlockSpec(memory_space=pl.ANY))
        operands.append(buffer)
        aliases = {len(operands) - 1: 0}
    work = rows * count * UNIT
    return pl.pallas_call(
        functools.partial(row_kernel, count),
        grid=(rows // BLOCK,),
        in_specs=in_specs,
        out_specs=pl.BlockSpec((BLOCK, count * UNIT), lambda i: (row_block(i), col_block)),
        out_shape=jax.ShapeDtypeStruct((out_rows, out_cols), jnp.float32),
        input_output_aliases=aliases,
        scratch_shapes=[pltpu.VMEM((2 * BLOCK, len(arrays) * UNIT), jnp.bfloat16)],
        compiler_params=pltpu.CompilerParams(vmem_limit_bytes=VMEM),
        cost_estimate=pl.CostEstimate(flops=work * 40, bytes_accessed=work * 12, transcendentals=0),
    )(*operands)


def exchange(first, last, axis):
    devices = lax.axis_size(axis)
    up = [(i, i + 1) for i in range(devices - 1)]
    down = [(j, i) for i, j in up]
    return lax.ppermute(last, axis, up), lax.ppermute(first, axis, down)


def coefficients(tables, offset, lines):
    east_wind, north_wind, diffuse_lon, diffuse_lat = tables
    made = jnp.stack(
        [
            1.0 - 2.0 * diffuse_lon - 2.0 * diffuse_lat,
            diffuse_lon - 0.5 * east_wind,
            diffuse_lon + 0.5 * east_wind,
            diffuse_lat - 0.5 * north_wind,
            diffuse_lat + 0.5 * north_wind,
        ]
    )
    edge = STEPS - 1
    made = jnp.pad(made, ((0, 0), (edge, edge), (0, 0)))
    return lax.dynamic_slice_in_dim(made, offset, lines + 2 * edge, 1)


def body(covariance, east_wind, north_wind, diffuse_lon, diffuse_lat):
    tables = (east_wind, north_wind, diffuse_lon, diffuse_lat)
    rows, cols = covariance.shape
    row_lines, col_lines = rows // NLON, cols // NLON
    row_units, col_units = rows // UNIT, cols // UNIT
    row_coefs = coefficients(tables, lax.axis_index("row") * row_lines, row_lines)
    row_coefs = jnp.broadcast_to(row_coefs[:, :, :, None], row_coefs.shape + (NLON,))
    plain, _ = powers(tables)
    col_tables = blocks_of(plain, lax.axis_index("col") * col_lines, col_lines // 2, 2, True)

    if col_units == 1:
        pieces = [[0]]
    else:
        pieces = [[0, col_units - 1]]
        half = col_units // 2
        if col_units % 2 == 0 and col_units >= 6:
            pieces += [list(range(1, half + 1)), list(range(half + 1, col_units - 1))]
        elif col_units > 2:
            pieces += [list(range(1, col_units - 1))]

    def columns(units, low, high):
        parts = []
        for u in units:
            if parts and parts[-1][1] == u:
                parts[-1][1] = u + 1
            else:
                parts.append([u, u + 1])
        return jnp.concatenate([covariance[low:high, a * UNIT : b * UNIT] for a, b in parts], axis=1)

    halos = [exchange(columns(p, 0, UNIT), columns(p, rows - UNIT, rows), "row") for p in pieces]

    inner = None
    if row_units > 2:
        inner = column_sweep(
            [(covariance, r, 0, 0) for r in range(row_units)],
            [(list(range(row_units)), STEPS, row_lines - 2 * STEPS)],
            cols,
            row_coefs,
        )

    outer = []
    where = {}
    for k, (units, (before, after)) in enumerate(zip(pieces, halos)):
        width = len(units) * UNIT
        skip = (cols - 2 * UNIT) // NLON if k == 0 and col_units > 1 else 0
        blocks = [(covariance, r, units[0] * (UNIT // NLON), skip) for r in range(row_units)]
        if row_units == 1:
            arrays = [(before, 0, 0, 0), blocks[0], (after, 0, 0, 0)]
            sides = [([0, 1, 2], 0, STEPS)]
        else:
            arrays = [(before, 0, 0, 0), blocks[0], blocks[1], blocks[-2], blocks[-1], (after, 0, 0, 0)]
            sides = [([0, 1, 2], 0, STEPS), ([3, 4, 5], row_lines - STEPS, STEPS)]
        outer.append(column_sweep(arrays, sides, width, row_coefs))
        for at, u in enumerate(units):
            where[u] = (k, at)

    out_blocks, tiles = rows // BLOCK, UNIT // BLOCK
    halves = [list(range(col_units))]
    if len(pieces) == 3:
        halves = [list(range(half)), list(range(half, col_units))]

    edges = outer[0]
    outer_halo = exchange(edges[:, :UNIT], edges[:, -UNIT:], "col")
    out = None
    if inner is not None:
        inner_halo = exchange(inner[:, :UNIT], inner[:, cols - UNIT :], "col")
        arrays = [(inner_halo[0], 0)] + [(inner, u) for u in range(col_units)] + [(inner_halo[1], 0)]
        out = row_sweep(arrays, 0, col_tables, rows, lambda i: i + tiles, cols, 0, out)

    def outer_row(i):
        return jnp.where(i < tiles, i, i + out_blocks - 2 * tiles) if row_units > 1 else i

    for h, units in enumerate(halves):
        arrays = []
        for u in [units[0] - 1] + units + [units[-1] + 1]:
            if u < 0:
                arrays.append((outer_halo[0], 0))
            elif u == col_units:
                arrays.append((outer_halo[1], 0))
            else:
                arrays.append((outer[where[u][0]], where[u][1]))
        out = row_sweep(arrays, h, col_tables, rows, outer_row, cols, h, out)
    return out


LANES = 128
SUBS = 8
PAD = 8
HALO = STEPS * NLON
PAIR = 2
RBLOCK = 96
PIECE = 192
MESH = pl.DeviceIdType.MESH


def tile_order(tiles):
    edges = list(range(STEPS)) + list(range(tiles - STEPS, tiles))
    return edges, list(range(STEPS, tiles - STEPS))


def detours(row_devices, tiles):
    if row_devices != 8:
        return None
    _, middle = tile_order(tiles)
    carried = [t for n, t in enumerate(middle) if n % 3]
    return dict(low=3, high=4, up_by=7, down_by=0, tiles=carried)


def line_step(ctab, pair, line, source, stores, keeps=()):
    sub = lax.broadcasted_iota(jnp.int32, (SUBS, LANES), 0)
    for g in range(NLON // SUBS):
        at = g * SUBS
        coef = [ctab[k, line - 1, pl.ds(at, SUBS), :] for k in range(5)]
        for n in range(len(pair)):

            def read(d, shift=0, count=SUBS):
                ref, base = source(n, d)
                return ref[pl.ds(pl.multiple_of(base, SUBS) + shift, count), :]

            def write(place, value):
                ref, base = place
                ref[pl.ds(pl.multiple_of(base + at, SUBS), SUBS), :] = value

            seen = {d: read(d, at) for d in (-1, 0, 1)}
            east, west = read(0, at + 1), read(0, at - 1)
            if g == NLON // SUBS - 1:
                east = jnp.where(sub == SUBS - 1, read(0, 0, 1), east)
            if g == 0:
                west = jnp.where(sub == 0, read(0, NLON - 1, 1), west)
            value = (coef[0] * seen[0] + coef[1] * east) + (coef[2] * west + coef[3] * seen[1]) + coef[4] * seen[-1]
            for place in stores(n):
                write(place, value)
            for d, place in keeps:
                write(place(n), seen[d])


def line_of(big, pair, n, slot):
    return big.at[pair[n]], PAD + slot * NLON


def outer_columns(big, ctab, one, two, lines, pair, south, result):
    ones = [("one", k) for k in range(STEPS)]
    twos = [("two", k) for k in range(STEPS)]
    if south:
        first = [lines + 2, lines + 1, lines]
        after_one = [("big", lines - 1), ("big", lines)] + ones
        after_two = [("big", lines - 3), ("big", lines - 2)] + twos
    else:
        first = [1, 2, 3]
        after_one = ones + [("big", 5), ("big", 6)]
        after_two = twos + [("big", 7), ("big", 8)]

    def place(n, where):
        name, k = where
        if name == "big":
            return line_of(big, pair, n, k)
        return (one if name == "one" else two).at[n], PAD + k * NLON

    for k in range(STEPS):
        line = first[0] + k
        line_step(ctab, pair, line, lambda n, d: line_of(big, pair, n, line + d), lambda n: [place(n, ones[k])])
    for k in range(STEPS):
        line_step(ctab, pair, first[1] + k, lambda n, d: place(n, after_one[k + 1 + d]), lambda n: [place(n, twos[k])])
    for k in range(STEPS):
        line = first[2] + k
        line_step(ctab, pair, line, lambda n, d: place(n, after_two[k + 1 + d]), lambda n: [result(n, line)])


def fused_kernel(row_devices, col_devices, lines, tiles, cov, ew, nw, dlon, dlat, fwd, rtab, big, ctab, relay, one, two, pads, winds,
                 wind_sem, load_sem, up_send, up_recv, down_send, down_recv, hop_send, hop_recv, z_send, z_recv, ready_sem):
    r, c = lax.axis_index("row"), lax.axis_index("col")
    rows = lines * NLON
    edges, middle = tile_order(tiles)
    detour = detours(row_devices, tiles)
    carried = detour["tiles"] if detour else []
    has_up, has_down = r < row_devices - 1, r > 0
    has_right, has_left = c < col_devices - 1, c > 0

    partners = [(has_up, {"row": jnp.minimum(r + 1, row_devices - 1)}), (has_down, {"row": jnp.maximum(r - 1, 0)})]
    if detour:
        for a in (detour["low"], detour["high"]):
            for b in (detour["up_by"], detour["down_by"]):
                partners += [(r == a, {"row": b}), (r == b, {"row": a})]
    barrier = pltpu.get_barrier_semaphore()
    count = 0
    for there, place in partners:
        count = count + there.astype(jnp.int32)

        @pl.when(there)
        def _():
            pl.semaphore_signal(barrier, inc=1, device_id=place, device_id_type=MESH)

    def load(t):
        return pltpu.make_async_copy(cov.at[:, pl.ds(pl.multiple_of(t * LANES, LANES), LANES)], big.at[t, pl.ds(PAD + HALO, rows), :], load_sem.at[t])

    def lanes(t):
        return pl.ds(pl.multiple_of(t * LANES, LANES), LANES)

    top, bottom = pl.ds(0, HALO), pl.ds(rows - HALO, HALO)
    before, after = pl.ds(PAD, HALO), pl.ds(PAD + HALO + rows, HALO)

    def up(t):
        return pltpu.make_async_remote_copy(cov.at[bottom, lanes(t)], big.at[t, before, :], up_send.at[t], up_recv.at[t],
                                            device_id={"row": jnp.minimum(r + 1, row_devices - 1)}, device_id_type=MESH)

    def down(t):
        return pltpu.make_async_remote_copy(cov.at[top, lanes(t)], big.at[t, after, :], down_send.at[t], down_recv.at[t],
                                            device_id={"row": jnp.maximum(r - 1, 0)}, device_id_type=MESH)

    def up_first(k, t):
        return pltpu.make_async_remote_copy(cov.at[bottom, lanes(t)], relay.at[k], up_send.at[t], hop_recv.at[k],
                                            device_id={"row": detour["up_by"]}, device_id_type=MESH)

    def down_first(k, t):
        return pltpu.make_async_remote_copy(cov.at[top, lanes(t)], relay.at[k], down_send.at[t], hop_recv.at[k],
                                            device_id={"row": detour["down_by"]}, device_id_type=MESH)

    def up_second(k, t):
        return pltpu.make_async_remote_copy(relay.at[k], big.at[t, before, :], hop_send.at[k], up_recv.at[t],
                                            device_id={"row": detour["high"]}, device_id_type=MESH)

    def down_second(k, t):
        return pltpu.make_async_remote_copy(relay.at[k], big.at[t, after, :], hop_send.at[k], down_recv.at[t],
                                            device_id={"row": detour["low"]}, device_id_type=MESH)

    count = count + has_left.astype(jnp.int32)

    @pl.when(has_right)
    def _():
        pl.semaphore_signal(barrier, inc=1, device_id={"col": jnp.minimum(c + 1, col_devices - 1)}, device_id_type=MESH)

    wind_copies = [pltpu.make_async_copy(ref, winds.at[k], wind_sem.at[k]) for k, ref in enumerate((ew, nw, dlon, dlat))]
    for copy in wind_copies:
        copy.start()
    for t in edges:
        load(t).start()
    pl.semaphore_wait(barrier, count)

    odd = r % 2 == 1

    def send_slow(t):
        low = high = r < 0
        if t in carried:
            k = carried.index(t)
            low, high = r == detour["low"], r == detour["high"]

            @pl.when(low)
            def _():
                up_first(k, t).start()

            @pl.when(high)
            def _():
                down_first(k, t).start()

        @pl.when(odd & has_up & ~low)
        def _():
            up(t).start()

        @pl.when(~odd & has_down & ~high)
        def _():
            down(t).start()

    def send_quick(t):
        @pl.when(odd)
        def _():
            down(t).start()

        @pl.when(~odd)
        def _():
            up(t).start()

    for t in edges:
        send_slow(t)
    for t in edges:
        send_quick(t)
    for t in middle:
        send_slow(t)
    for t in middle:
        load(t).start()
    for t in middle:
        send_quick(t)

    @pl.when(has_left)
    def _():
        pl.semaphore_signal(ready_sem, inc=1, device_id={"col": jnp.maximum(c - 1, 0)}, device_id_type=MESH)

    def relay_step(k):
        t = carried[k]

        @pl.when(r == detour["up_by"])
        def _():
            up_first(k, t).wait_recv()
            up_second(k, t).start()

        @pl.when(r == detour["down_by"])
        def _():
            down_first(k, t).wait_recv()
            down_second(k, t).start()

    for copy in wind_copies:
        copy.wait()
    east_wind, north_wind, lon, lat = (winds[k] for k in range(4))
    half_east, half_north = 0.5 * east_wind, 0.5 * north_wind
    made = [1.0 - 2.0 * lon - 2.0 * lat, lon - half_east, lon + half_east, lat - half_north, lat + half_north]
    grid_lines = lon.shape[0]
    edge = STEPS - 1
    spread = -(-(lines + 2 * edge) // SUBS) * SUBS
    for k, table in enumerate(made):
        pads[k, pl.ds(0, PAD), :] = jnp.zeros((PAD, LANES), jnp.float32)
        pads[k, pl.ds(PAD, grid_lines), :] = table
        pads[k, pl.ds(PAD + grid_lines, spread), :] = jnp.zeros((spread, LANES), jnp.float32)
    wide = -(-(tiles + 2 * edge) // SUBS) * SUBS
    for k in range(len(made)):
        rtab[k] = pads[k, pl.ds(c * tiles + PAD - edge, wide), :]
        mine = pads[k, pl.ds(r * lines + PAD - edge, spread), :]
        turned = jnp.transpose(jnp.concatenate([mine, jnp.zeros((LANES - spread, LANES), jnp.float32)], axis=0))
        for i in range(lines + 2 * edge):
            ctab[k, i] = jnp.broadcast_to(turned[:, i : i + 1], (NLON, LANES))

    @pl.when(~has_down)
    def _():
        def clear(t, _):
            big[t, before, :] = jnp.zeros((HALO, LANES), jnp.float32)
            return 0
        lax.fori_loop(0, tiles, clear, 0)

    @pl.when(~has_up)
    def _():
        def clear(t, _):
            big[t, after, :] = jnp.zeros((HALO, LANES), jnp.float32)
            return 0
        lax.fori_loop(0, tiles, clear, 0)

    @pl.when(~has_left)
    def _():
        fwd[pl.ds(0, STEPS)] = jnp.zeros((STEPS, rows, LANES), jnp.float32)

    @pl.when(~has_right)
    def _():
        fwd[pl.ds(tiles + STEPS, STEPS)] = jnp.zeros((STEPS, rows, LANES), jnp.float32)

    def in_big(pair, n, slot):
        return line_of(big, pair, n, slot)

    def in_fwd(pair, n, line):
        return fwd.at[pair[n] + STEPS], (line - STEPS) * NLON

    def inner_columns(pair):
        kept_one = {4: 5, 5: 6, lines: lines - 1, lines + 1: lines}
        kept_two = {5: 7, 6: 8, lines - 1: lines - 3, lines: lines - 2}

        def at_one(n, line):
            return one.at[n], PAD + (line - 4) * NLON

        def at_two(n, line):
            return two.at[n], PAD + (line - 5) * NLON

        def step1(line, _):
            line_step(ctab, pair, line, lambda n, d: in_big(pair, n, line + d), lambda n: [at_one(n, line)])
            return 0

        def step2(line, keep):
            places = lambda n: [at_two(n, line)] + ([in_big(pair, n, kept_two[line])] if keep else [])
            keeps = [(d, functools.partial(lambda n, slot: in_big(pair, n, slot), slot=kept_one[line + d]))
                     for d in ((-1, 0) if line == 5 else (0, 1))] if keep and line in (5, lines) else []
            line_step(ctab, pair, line, lambda n, d: at_one(n, line + d), places, keeps)

        def step2_plain(line, _):
            step2(line, False)
            return 0

        def step3(line, _):
            line_step(ctab, pair, line, lambda n, d: at_two(n, line + d), lambda n: [in_fwd(pair, n, line)])
            return 0

        lax.fori_loop(4, lines + 2, step1, 0)
        step2(5, True)
        step2(6, True)
        lax.fori_loop(7, lines - 1, step2_plain, 0)
        step2(lines - 1, True)
        step2(lines, True)
        lax.fori_loop(6, lines, step3, 0)

    def outer(pair, south):
        outer_columns(big, ctab, one, two, lines, pair, south, lambda n, line: in_fwd(pair, n, line))

    quick, slow = odd_rows(odd, rows)

    def quick_columns(pair):
        @pl.when(odd)
        def _():
            for t in pair:
                up(t).wait_recv()
            outer(pair, False)

        @pl.when(~odd)
        def _():
            for t in pair:
                down(t).wait_recv()
            outer(pair, True)

    def slow_arrive(pair):
        @pl.when(odd & has_up)
        def _():
            for t in pair:
                down(t).wait_recv()

        @pl.when(~odd & has_down)
        def _():
            for t in pair:
                up(t).wait_recv()

    def slow_columns(pair):
        slow_arrive(pair)

        @pl.when(odd)
        def _():
            outer(pair, True)

        @pl.when(~odd)
        def _():
            outer(pair, False)

    pieces = (rows - 2 * HALO) // PIECE
    side = HALO // PIECE

    def piece_start(part):
        on_quick, on_slow = quick + (part - pieces) * PIECE, slow + (part - pieces - side) * PIECE
        start = jnp.where(part < pieces, HALO + part * PIECE, jnp.where(part < pieces + side, on_quick, on_slow))
        return pl.multiple_of(start, PIECE)

    def z_copy(part, right):
        where = pl.ds(piece_start(part), PIECE)
        first, there = (tiles, 0) if right else (STEPS, tiles + STEPS)
        other = jnp.minimum(c + 1, col_devices - 1) if right else jnp.maximum(c - 1, 0)
        n = 2 * part + (1 if right else 0)
        return pltpu.make_async_remote_copy(fwd.at[pl.ds(first, STEPS), where, :], fwd.at[pl.ds(there, STEPS), where, :],
                                            z_send.at[n], z_recv.at[n], device_id={"col": other}, device_id_type=MESH)

    def z_start(part, _):
        @pl.when(has_right)
        def _():
            z_copy(part, True).start()

        @pl.when(has_left)
        def _():
            z_copy(part, False).start()
        return 0

    def z_wait(part, _):
        @pl.when(has_right)
        def _():
            z_copy(part, True).wait_send()
            z_copy(part, False).wait_recv()

        @pl.when(has_left)
        def _():
            z_copy(part, False).wait_send()
            z_copy(part, True).wait_recv()
        return 0

    def pair_of(i):
        got = []
        for n in range(PAIR):
            m = i * PAIR + n
            got.append(jnp.where(m < 2 * STEPS, m + (m // STEPS) * (tiles - 2 * STEPS), m - STEPS))
        return got

    edge_pairs, all_pairs = 2 * STEPS // PAIR, tiles // PAIR

    def early(i, _):
        pair = pair_of(i)
        for t in pair:
            load(t).wait()
        inner_columns(pair)
        quick_columns(pair)

        @pl.when(i == edge_pairs - 1)
        def _():
            @pl.when(has_right)
            def _():
                pl.semaphore_wait(ready_sem, 1)

            lax.fori_loop(0, pieces + side, z_start, 0)

        if detour:
            for k in range(len(carried)):
                @pl.when(i == k * all_pairs // len(carried))
                def _():
                    relay_step(k)
        return 0

    lax.fori_loop(0, all_pairs, early, 0)

    def held(tile, at):
        return fwd[tile + STEPS, pl.ds(at, RBLOCK), :]

    def keep(tile, at, value):
        fwd[tile, pl.ds(at, RBLOCK), :] = value

    def ready_rows(part, _):
        z_wait(part, 0)
        row_pass(held, rtab, 0, tiles, piece_start(part), PIECE, keep)
        return 0

    groups = slow_groups(all_pairs - edge_pairs)
    stops = []
    at = edge_pairs
    for n in groups[:-1]:
        at += n
        stops.append(at)

    def late(i, _):
        slow_columns(pair_of(i))

        @pl.when(i == edge_pairs - 1)
        def _():
            lax.fori_loop(pieces + side, pieces + 2 * side, z_start, 0)
            lax.fori_loop(0, pieces + side, ready_rows, 0)

        done = 0
        for n, stop in enumerate(stops):
            upto = stop * PAIR - 2 * STEPS

            @pl.when(i == stop - 1)
            def _():
                if n == 0:
                    lax.fori_loop(pieces + side, pieces + 2 * side, z_wait, 0)
                row_pass(held, rtab, done, upto, slow, HALO, keep)
            done = upto
        return 0

    def sent(t, _):
        @pl.when(has_up)
        def _():
            up(t).wait_send()

        @pl.when(has_down)
        def _():
            down(t).wait_send()
        return 0

    lax.fori_loop(0, all_pairs - 1, late, 0)
    for k, t in enumerate(carried):
        @pl.when(r == detour["up_by"])
        def _():
            up_second(k, t).wait_send()

        @pl.when(r == detour["down_by"])
        def _():
            down_second(k, t).wait_send()
    final = tiles - STEPS - PAIR
    lax.fori_loop(0, final, sent, 0)
    lax.fori_loop(final + PAIR, tiles, sent, 0)
    slow_arrive([final + n for n in range(PAIR)])
    lax.fori_loop(final, final + PAIR, sent, 0)


def slow_groups(pairs):
    groups = []
    while pairs > 3:
        groups.append(3)
        pairs -= 3
    return groups + [pairs - 1, 1] if pairs > 1 else groups + [pairs]


def rest(tiles):
    pairs = (tiles - 2 * STEPS) // PAIR
    return STEPS + (pairs - slow_groups(pairs)[-1]) * PAIR - STEPS


def odd_rows(odd, rows):
    return jnp.where(odd, 0, rows - HALO), jnp.where(odd, rows - HALO, 0)


def row_pass(read, rtab, a, b, start, count, store):
    edge = STEPS - 1

    def block(i, _):
        at = pl.multiple_of(start + i * RBLOCK, RBLOCK)
        got = {}
        for tile in range(a - STEPS, b + STEPS):
            got[0, tile] = read(tile, at)
            for step in range(1, STEPS + 1):
                mid = tile - step
                if mid < a - STEPS + step:
                    continue
                here = got[step - 1, mid]
                coef = [rtab[k, pl.ds(mid + edge, 1), :] for k in range(5)]
                value = (
                    (coef[0] * here + coef[1] * pltpu.roll(here, LANES - 1, 1))
                    + (coef[2] * pltpu.roll(here, 1, 1) + coef[3] * got[step - 1, mid + 1])
                    + coef[4] * got[step - 1, mid - 1]
                )
                got.pop((step - 1, mid - 1))
                if step < STEPS:
                    got[step, mid] = value
                else:
                    store(mid, at, value)
        return 0

    lax.fori_loop(0, count // RBLOCK, block, 0)


def finish_kernel(tiles, fwd, rtab, big, ctab, out, last, ends, one, two, done_sem, slow_sem):
    rows = out.shape[0]
    lines = rows // NLON
    begin = rest(tiles)
    odd = lax.axis_index("row") % 2 == 1
    quick, slow = odd_rows(odd, rows)
    ready = pl.ds(pl.multiple_of(jnp.where(quick == 0, 0, HALO), SUBS), rows - HALO)
    late = pl.ds(pl.multiple_of(slow, SUBS), HALO)

    def lanes(t):
        return pl.ds(t * LANES, LANES)

    copies = [pltpu.make_async_copy(fwd.at[t, ready, :], out.at[ready, lanes(t)], done_sem.at[t]) for t in range(tiles)]
    copies += [pltpu.make_async_copy(fwd.at[t, late, :], out.at[late, lanes(t)], slow_sem.at[t]) for t in range(begin)]
    for copy in copies:
        copy.start()

    pair = [tiles - STEPS - PAIR + n for n in range(PAIR)]

    @pl.when(odd)
    def _():
        outer_columns(big, ctab, one, two, lines, pair, True, lambda n, line: (ends.at[n], (line - lines) * NLON))

    @pl.when(~odd)
    def _():
        outer_columns(big, ctab, one, two, lines, pair, False, lambda n, line: (ends.at[n], (line - STEPS) * NLON))

    def held(tile, at):
        if tile in pair:
            return ends[tile - pair[0], pl.ds(pl.multiple_of(at - slow, SUBS), RBLOCK), :]
        return fwd[tile + STEPS, pl.ds(at, RBLOCK), :]

    def keep(tile, at, value):
        last[tile - begin, pl.ds(pl.multiple_of(at - slow, SUBS), RBLOCK), :] = value

    row_pass(held, rtab, begin, tiles, slow, HALO, keep)
    copies_left = [pltpu.make_async_copy(last.at[t - begin], out.at[late, lanes(t)], slow_sem.at[t]) for t in range(begin, tiles)]
    for copy in copies_left:
        copy.start()
    for copy in copies + copies_left:
        copy.wait()


def fused_body(row_devices, col_devices, covariance, east_wind, north_wind, diffuse_lon, diffuse_lat):
    rows, cols = covariance.shape
    lines, tiles = rows // NLON, cols // NLON
    edge = STEPS - 1
    spread = -(-(lines + 2 * edge) // SUBS) * SUBS
    wide = -(-(tiles + 2 * edge) // SUBS) * SUBS
    slack = PAD + east_wind.shape[0] + max(spread, wide)
    detour = detours(row_devices, tiles)
    hops = len(detour["tiles"]) if detour else 1
    f32 = jnp.float32
    kept = [
        (tiles + 2 * STEPS, rows, LANES),
        (5, wide, LANES),
        (tiles, 2 * PAD + 2 * HALO + rows, LANES),
        (5, lines + 2 * edge, NLON, LANES),
    ]
    room = 64 * 1024 * 1024 - sum(4 * math.prod(shape) for shape in kept) - 1024 * 1024
    made = pl.pallas_call(
        functools.partial(fused_kernel, row_devices, col_devices, lines, tiles),
        in_specs=[pl.BlockSpec(memory_space=pl.ANY)] * 5,
        out_specs=[pl.BlockSpec(memory_space=pltpu.VMEM)] * len(kept) + [pl.BlockSpec(memory_space=pl.ANY)],
        out_shape=[pltpu.VMEM(shape, f32) for shape in kept] + [jax.ShapeDtypeStruct((hops, HALO, LANES), f32)],
        scratch_shapes=[
            pltpu.VMEM((PAIR, 2 * PAD + (lines - 2) * NLON, LANES), f32),
            pltpu.VMEM((PAIR, 2 * PAD + (lines - 4) * NLON, LANES), f32),
            pltpu.VMEM((5, slack, LANES), f32),
            pltpu.VMEM((4,) + east_wind.shape, f32),
            pltpu.SemaphoreType.DMA((4,)),
            pltpu.SemaphoreType.DMA((tiles,)),
            pltpu.SemaphoreType.DMA((tiles,)),
            pltpu.SemaphoreType.DMA((tiles,)),
            pltpu.SemaphoreType.DMA((tiles,)),
            pltpu.SemaphoreType.DMA((tiles,)),
            pltpu.SemaphoreType.DMA((hops,)),
            pltpu.SemaphoreType.DMA((hops,)),
            pltpu.SemaphoreType.DMA((2 * rows // PIECE,)),
            pltpu.SemaphoreType.DMA((2 * rows // PIECE,)),
            pltpu.SemaphoreType.REGULAR,
        ],
        compiler_params=pltpu.CompilerParams(collective_id=0, has_side_effects=True, vmem_limit_bytes=room),
    )(covariance, east_wind, north_wind, diffuse_lon, diffuse_lat)
    return pl.pallas_call(
        functools.partial(finish_kernel, tiles),
        in_specs=[pl.BlockSpec(memory_space=pltpu.VMEM)] * len(kept),
        out_specs=pl.BlockSpec(memory_space=pl.ANY),
        out_shape=jax.ShapeDtypeStruct((rows, cols), f32),
        scratch_shapes=[
            pltpu.VMEM((tiles - rest(tiles), HALO, LANES), f32),
            pltpu.VMEM((PAIR, HALO, LANES), f32),
            pltpu.VMEM((PAIR, 2 * PAD + HALO, LANES), f32),
            pltpu.VMEM((PAIR, 2 * PAD + HALO, LANES), f32),
            pltpu.SemaphoreType.DMA((tiles,)),
            pltpu.SemaphoreType.DMA((tiles,)),
        ],
        compiler_params=pltpu.CompilerParams(vmem_limit_bytes=room),
    )(*[pltpu.with_memory_space_constraint(array, pltpu.VMEM) for array in made[: len(kept)]])


def solution(mesh):
    row_devices, col_devices = mesh.shape["row"], mesh.shape["col"]

    def run(covariance, *tables):
        lines, tiles = covariance.shape[0] // NLON, covariance.shape[1] // NLON
        if lines >= 4 * STEPS and tiles >= 4 * STEPS and (tiles - 2 * STEPS) % PAIR == 0:
            return fused_body(row_devices, col_devices, covariance, *tables)
        return body(covariance, *tables)

    return jax.shard_map(
        run,
        mesh=mesh,
        in_specs=(P("row", "col"), P(), P(), P(), P()),
        out_specs=P("row", "col"),
        check_vma=False,
    )
```

```python
import functools
import math

import jax
import jax.numpy as jnp
from jax import lax
from jax.experimental import pallas as pl
from jax.experimental.pallas import tpu as pltpu
from jax.sharding import PartitionSpec as P

NLON = 128
STEPS = 3
UNIT = STEPS * NLON
WIDE = 256
BLOCK = 192
VMEM = 52 * 1024 * 1024


OFFSETS = [(y, x) for y in range(-STEPS, STEPS + 1) for x in range(-STEPS + abs(y), STEPS + 1 - abs(y))]


def power_kernel(east_wind, north_wind, diffuse_lon, diffuse_lat, plain, rolled):
    lon, lat = diffuse_lon[...], diffuse_lat[...]
    half_east, half_north = 0.5 * east_wind[...], 0.5 * north_wind[...]
    one = {
        (0, 0): 1.0 - 2.0 * lon - 2.0 * lat,
        (0, 1): lon - half_east,
        (0, -1): lon + half_east,
        (1, 0): lat - half_north,
        (-1, 0): lat + half_north,
    }
    lines = lon.shape[0]
    line = lax.broadcasted_iota(jnp.int32, lon.shape, 0)

    def seen(field, y, x):
        if x:
            return pltpu.roll(field, -x % NLON, 1)
        if y:
            edge = lines - 1 if y > 0 else 0
            return jnp.where(line == edge, 0.0, pltpu.roll(field, -y % lines, 0))
        return field

    power = dict(one)
    for _ in range(STEPS - 1):
        made = {}
        for (y, x), field in power.items():
            for (sy, sx), scale in one.items():
                term = scale * seen(field, sy, sx)
                at = (y + sy, x + sx)
                made[at] = made[at] + term if at in made else term
        power = made
    for k, (y, x) in enumerate(OFFSETS):
        plain[k] = power[y, x]
        rolled[k] = pltpu.roll(power[y, x], x % NLON, 1)


def powers(tables):
    shape = jax.ShapeDtypeStruct((len(OFFSETS),) + tables[0].shape, jnp.float32)
    return pl.pallas_call(
        power_kernel,
        out_shape=(shape, shape),
        compiler_params=pltpu.CompilerParams(vmem_limit_bytes=VMEM),
        cost_estimate=pl.CostEstimate(flops=10**7, bytes_accessed=10**7, transcendentals=0),
    )(*tables)


def split(value):
    high = value.astype(jnp.bfloat16)
    return high, (value - high.astype(jnp.float32)).astype(jnp.bfloat16)


def block_kernel(made, transposed, offset, table, out):
    base = offset[0] + pl.program_id(0) * made
    sub = lax.broadcasted_iota(jnp.int32, (NLON, NLON), 0)
    lane = lax.broadcasted_iota(jnp.int32, (NLON, NLON), 1)
    away = (sub - lane if transposed else lane - sub) & (NLON - 1)
    read = made + 2 * STEPS
    for a in range(made):
        for b in range(read):
            y = b - a - STEPS
            value = jnp.zeros((NLON, NLON), jnp.float32)
            for k, (oy, x) in enumerate(OFFSETS):
                if oy == y:
                    line = table[k, pl.ds(base + a, 1), :]
                    value = jnp.where(away == x % NLON, jnp.broadcast_to(line, (NLON, NLON)), value)
            high, low = split(value)
            mine, theirs = slice(a * NLON, (a + 1) * NLON), slice(b * NLON, (b + 1) * NLON)
            if transposed:
                out[0, theirs, mine] = high
                out[0, slice((read + b) * NLON, (read + b + 1) * NLON), mine] = low
            else:
                out[0, mine, theirs] = high
                out[0, slice((made + a) * NLON, (made + a + 1) * NLON), theirs] = low


def blocks_of(table, offset, groups, made, transposed):
    read = made + 2 * STEPS
    shape = (2 * read * NLON, made * NLON) if transposed else (2 * made * NLON, read * NLON)
    return pl.pallas_call(
        functools.partial(block_kernel, made, transposed),
        grid=(groups,),
        in_specs=[
            pl.BlockSpec(memory_space=pltpu.SMEM),
            pl.BlockSpec(table.shape, lambda i: (0, 0, 0)),
        ],
        out_specs=pl.BlockSpec((1,) + shape, lambda i: (i, 0, 0)),
        out_shape=jax.ShapeDtypeStruct((groups,) + shape, jnp.bfloat16),
        compiler_params=pltpu.CompilerParams(vmem_limit_bytes=VMEM),
        cost_estimate=pl.CostEstimate(flops=10**7, bytes_accessed=2 * 10**7, transcendentals=0),
    )(offset.reshape(1).astype(jnp.int32), table)


def dot(a, b):
    return jnp.dot(a, b, preferred_element_type=jnp.float32)


def stencil(c, east, west, north, south, coef):
    return coef[0] * c + coef[1] * east + coef[2] * west + coef[3] * north + coef[4] * south


def column_kernel(parts, sides, *refs):
    ins, tables, out = refs[: len(parts)], refs[len(parts)], refs[-1]
    for side, (names, first, count) in enumerate(sides):

        def source(line):
            part, at = divmod(line, STEPS)
            return ins[names[part]][at * NLON : (at + 1) * NLON, :]

        lines = count + 2 * STEPS
        got = {}
        for line in range(lines):
            got[0, line] = source(line)
            for step in range(1, STEPS + 1):
                mid = line - step
                if mid < step:
                    continue
                c = got[step - 1, mid]
                row = first + mid - 1
                value = stencil(
                    c,
                    pltpu.roll(c, NLON - 1, 0),
                    pltpu.roll(c, 1, 0),
                    got[step - 1, mid + 1],
                    got[step - 1, mid - 1],
                    [tables[k, row] for k in range(5)],
                )
                got.pop((step - 1, mid - 1))
                if step < STEPS:
                    got[step, mid] = value
                else:
                    at = sum(s[2] for s in sides[:side]) + mid - STEPS
                    out[at * NLON : (at + 1) * NLON, :] = value


def column_sweep(arrays, sides, width, coefs):
    total = sum(count for _, _, count in sides) * NLON
    in_specs = [
        pl.BlockSpec((UNIT, NLON), functools.partial(lambda i, r, c, skip: (r, jnp.where(i < UNIT // NLON, i + c, i + c + skip)), r=r, c=c, skip=skip)) for _, r, c, skip in arrays
    ]
    in_specs.append(pl.BlockSpec(coefs.shape, lambda i: (0, 0, 0, 0)))
    work = total * width
    return pl.pallas_call(
        functools.partial(column_kernel, arrays, sides),
        grid=(width // NLON,),
        in_specs=in_specs,
        out_specs=pl.BlockSpec((total, NLON), lambda i: (0, i)),
        out_shape=jax.ShapeDtypeStruct((total, width), jnp.float32),
        compiler_params=pltpu.CompilerParams(vmem_limit_bytes=VMEM),
        cost_estimate=pl.CostEstimate(flops=work * 40, bytes_accessed=work * 12, transcendentals=0),
    )(*[a[0] for a in arrays], coefs)


def row_kernel(count, *refs):
    ins, tables, out, both = refs[: count + 2], refs[count + 2], refs[-2], refs[-1]
    rows = out.shape[0]
    read = (2 + 2 * STEPS) * NLON
    for n, ref in enumerate(ins):
        cols = slice(n * UNIT, (n + 1) * UNIT)
        both[:rows, cols], both[rows:, cols] = split(ref[...])
    for pair in range(count * STEPS // 2):
        cols = slice(pair * 2 * NLON, pair * 2 * NLON + read)
        first = dot(both[:, cols], tables[pair, :read, :])
        other = dot(both[:rows, cols], tables[pair, read:, :])
        out[:, pair * 2 * NLON : (pair + 1) * 2 * NLON] = first[:rows] + (first[rows:] + other)


def row_sweep(arrays, part, tables, out_rows, row_block, out_cols, col_block, buffer):
    count = len(arrays) - 2
    rows = arrays[0][0].shape[0]
    pairs = count * STEPS // 2
    in_specs = [pl.BlockSpec((BLOCK, UNIT), functools.partial(lambda i, c: (i, c), c=c)) for _, c in arrays]
    in_specs.append(
        pl.BlockSpec((pairs,) + tables.shape[1:], lambda i: (part, 0, 0), pipeline_mode=pl.Buffered(1))
    )
    operands = [a for a, _ in arrays] + [tables]
    aliases = {}
    if buffer is not None:
        in_specs.append(pl.BlockSpec(memory_space=pl.ANY))
        operands.append(buffer)
        aliases = {len(operands) - 1: 0}
    work = rows * count * UNIT
    return pl.pallas_call(
        functools.partial(row_kernel, count),
        grid=(rows // BLOCK,),
        in_specs=in_specs,
        out_specs=pl.BlockSpec((BLOCK, count * UNIT), lambda i: (row_block(i), col_block)),
        out_shape=jax.ShapeDtypeStruct((out_rows, out_cols), jnp.float32),
        input_output_aliases=aliases,
        scratch_shapes=[pltpu.VMEM((2 * BLOCK, len(arrays) * UNIT), jnp.bfloat16)],
        compiler_params=pltpu.CompilerParams(vmem_limit_bytes=VMEM),
        cost_estimate=pl.CostEstimate(flops=work * 40, bytes_accessed=work * 12, transcendentals=0),
    )(*operands)


def exchange(first, last, axis):
    devices = lax.axis_size(axis)
    up = [(i, i + 1) for i in range(devices - 1)]
    down = [(j, i) for i, j in up]
    return lax.ppermute(last, axis, up), lax.ppermute(first, axis, down)


def coefficients(tables, offset, lines):
    east_wind, north_wind, diffuse_lon, diffuse_lat = tables
    made = jnp.stack(
        [
            1.0 - 2.0 * diffuse_lon - 2.0 * diffuse_lat,
            diffuse_lon - 0.5 * east_wind,
            diffuse_lon + 0.5 * east_wind,
            diffuse_lat - 0.5 * north_wind,
            diffuse_lat + 0.5 * north_wind,
        ]
    )
    edge = STEPS - 1
    made = jnp.pad(made, ((0, 0), (edge, edge), (0, 0)))
    return lax.dynamic_slice_in_dim(made, offset, lines + 2 * edge, 1)


def body(covariance, east_wind, north_wind, diffuse_lon, diffuse_lat):
    tables = (east_wind, north_wind, diffuse_lon, diffuse_lat)
    rows, cols = covariance.shape
    row_lines, col_lines = rows // NLON, cols // NLON
    row_units, col_units = rows // UNIT, cols // UNIT
    row_coefs = coefficients(tables, lax.axis_index("row") * row_lines, row_lines)
    row_coefs = jnp.broadcast_to(row_coefs[:, :, :, None], row_coefs.shape + (NLON,))
    plain, _ = powers(tables)
    col_tables = blocks_of(plain, lax.axis_index("col") * col_lines, col_lines // 2, 2, True)

    if col_units == 1:
        pieces = [[0]]
    else:
        pieces = [[0, col_units - 1]]
        half = col_units // 2
        if col_units % 2 == 0 and col_units >= 6:
            pieces += [list(range(1, half + 1)), list(range(half + 1, col_units - 1))]
        elif col_units > 2:
            pieces += [list(range(1, col_units - 1))]

    def columns(units, low, high):
        parts = []
        for u in units:
            if parts and parts[-1][1] == u:
                parts[-1][1] = u + 1
            else:
                parts.append([u, u + 1])
        return jnp.concatenate([covariance[low:high, a * UNIT : b * UNIT] for a, b in parts], axis=1)

    halos = [exchange(columns(p, 0, UNIT), columns(p, rows - UNIT, rows), "row") for p in pieces]

    inner = None
    if row_units > 2:
        inner = column_sweep(
            [(covariance, r, 0, 0) for r in range(row_units)],
            [(list(range(row_units)), STEPS, row_lines - 2 * STEPS)],
            cols,
            row_coefs,
        )

    outer = []
    where = {}
    for k, (units, (before, after)) in enumerate(zip(pieces, halos)):
        width = len(units) * UNIT
        skip = (cols - 2 * UNIT) // NLON if k == 0 and col_units > 1 else 0
        blocks = [(covariance, r, units[0] * (UNIT // NLON), skip) for r in range(row_units)]
        if row_units == 1:
            arrays = [(before, 0, 0, 0), blocks[0], (after, 0, 0, 0)]
            sides = [([0, 1, 2], 0, STEPS)]
        else:
            arrays = [(before, 0, 0, 0), blocks[0], blocks[1], blocks[-2], blocks[-1], (after, 0, 0, 0)]
            sides = [([0, 1, 2], 0, STEPS), ([3, 4, 5], row_lines - STEPS, STEPS)]
        outer.append(column_sweep(arrays, sides, width, row_coefs))
        for at, u in enumerate(units):
            where[u] = (k, at)

    out_blocks, tiles = rows // BLOCK, UNIT // BLOCK
    halves = [list(range(col_units))]
    if len(pieces) == 3:
        halves = [list(range(half)), list(range(half, col_units))]

    edges = outer[0]
    outer_halo = exchange(edges[:, :UNIT], edges[:, -UNIT:], "col")
    out = None
    if inner is not None:
        inner_halo = exchange(inner[:, :UNIT], inner[:, cols - UNIT :], "col")
        arrays = [(inner_halo[0], 0)] + [(inner, u) for u in range(col_units)] + [(inner_halo[1], 0)]
        out = row_sweep(arrays, 0, col_tables, rows, lambda i: i + tiles, cols, 0, out)

    def outer_row(i):
        return jnp.where(i < tiles, i, i + out_blocks - 2 * tiles) if row_units > 1 else i

    for h, units in enumerate(halves):
        arrays = []
        for u in [units[0] - 1] + units + [units[-1] + 1]:
            if u < 0:
                arrays.append((outer_halo[0], 0))
            elif u == col_units:
                arrays.append((outer_halo[1], 0))
            else:
                arrays.append((outer[where[u][0]], where[u][1]))
        out = row_sweep(arrays, h, col_tables, rows, outer_row, cols, h, out)
    return out


LANES = 128
SUBS = 8
PAD = 8
HALO = STEPS * NLON
PAIR = 2
RBLOCK = 96
PIECE = 192
MESH = pl.DeviceIdType.MESH


def tile_order(tiles):
    edges = list(range(STEPS)) + list(range(tiles - STEPS, tiles))
    return edges, list(range(STEPS, tiles - STEPS))


def detours(row_devices, tiles):
    if row_devices != 8:
        return None
    _, middle = tile_order(tiles)
    carried = [t for n, t in enumerate(middle) if n % 3]
    return dict(low=3, high=4, up_by=7, down_by=0, tiles=carried)


def line_step(ctab, pair, line, source, stores, keeps=()):
    sub = lax.broadcasted_iota(jnp.int32, (SUBS, LANES), 0)
    for g in range(NLON // SUBS):
        at = g * SUBS
        coef = [ctab[k, line - 1, pl.ds(at, SUBS), :] for k in range(5)]
        for n in range(len(pair)):

            def read(d, shift=0, count=SUBS):
                ref, base = source(n, d)
                return ref[pl.ds(pl.multiple_of(base, SUBS) + shift, count), :]

            def write(place, value):
                ref, base = place
                ref[pl.ds(pl.multiple_of(base + at, SUBS), SUBS), :] = value

            seen = {d: read(d, at) for d in (-1, 0, 1)}
            east, west = read(0, at + 1), read(0, at - 1)
            if g == NLON // SUBS - 1:
                east = jnp.where(sub == SUBS - 1, read(0, 0, 1), east)
            if g == 0:
                west = jnp.where(sub == 0, read(0, NLON - 1, 1), west)
            value = (coef[0] * seen[0] + coef[1] * east) + (coef[2] * west + coef[3] * seen[1]) + coef[4] * seen[-1]
            for place in stores(n):
                write(place, value)
            for d, place in keeps:
                write(place(n), seen[d])


def line_of(big, pair, n, slot):
    return big.at[pair[n]], PAD + slot * NLON


def outer_columns(big, ctab, one, two, lines, pair, south, result):
    ones = [("one", k) for k in range(STEPS)]
    twos = [("two", k) for k in range(STEPS)]
    if south:
        first = [lines + 2, lines + 1, lines]
        after_one = [("big", lines - 1), ("big", lines)] + ones
        after_two = [("big", lines - 3), ("big", lines - 2)] + twos
    else:
        first = [1, 2, 3]
        after_one = ones + [("big", 5), ("big", 6)]
        after_two = twos + [("big", 7), ("big", 8)]

    def place(n, where):
        name, k = where
        if name == "big":
            return line_of(big, pair, n, k)
        return (one if name == "one" else two).at[n], PAD + k * NLON

    for k in range(STEPS):
        line = first[0] + k
        line_step(ctab, pair, line, lambda n, d: line_of(big, pair, n, line + d), lambda n: [place(n, ones[k])])
    for k in range(STEPS):
        line_step(ctab, pair, first[1] + k, lambda n, d: place(n, after_one[k + 1 + d]), lambda n: [place(n, twos[k])])
    for k in range(STEPS):
        line = first[2] + k
        line_step(ctab, pair, line, lambda n, d: place(n, after_two[k + 1 + d]), lambda n: [result(n, line)])


def fused_kernel(row_devices, col_devices, lines, tiles, cov, ew, nw, dlon, dlat, fwd, rtab, big, ctab, relay, one, two, pads, winds,
                 wind_sem, load_sem, up_send, up_recv, down_send, down_recv, hop_send, hop_recv, z_send, z_recv, ready_sem):
    r, c = lax.axis_index("row"), lax.axis_index("col")
    rows = lines * NLON
    edges, middle = tile_order(tiles)
    detour = detours(row_devices, tiles)
    carried = detour["tiles"] if detour else []
    has_up, has_down = r < row_devices - 1, r > 0
    has_right, has_left = c < col_devices - 1, c > 0

    partners = [(has_up, {"row": jnp.minimum(r + 1, row_devices - 1)}), (has_down, {"row": jnp.maximum(r - 1, 0)})]
    if detour:
        for a in (detour["low"], detour["high"]):
            for b in (detour["up_by"], detour["down_by"]):
                partners += [(r == a, {"row": b}), (r == b, {"row": a})]
    barrier = pltpu.get_barrier_semaphore()
    count = 0
    for there, place in partners:
        count = count + there.astype(jnp.int32)

        @pl.when(there)
        def _():
            pl.semaphore_signal(barrier, inc=1, device_id=place, device_id_type=MESH)

    def load(t):
        return pltpu.make_async_copy(cov.at[:, pl.ds(pl.multiple_of(t * LANES, LANES), LANES)], big.at[t, pl.ds(PAD + HALO, rows), :], load_sem.at[t])

    def lanes(t):
        return pl.ds(pl.multiple_of(t * LANES, LANES), LANES)

    top, bottom = pl.ds(0, HALO), pl.ds(rows - HALO, HALO)
    before, after = pl.ds(PAD, HALO), pl.ds(PAD + HALO + rows, HALO)

    def up(t):
        return pltpu.make_async_remote_copy(cov.at[bottom, lanes(t)], big.at[t, before, :], up_send.at[t], up_recv.at[t],
                                            device_id={"row": jnp.minimum(r + 1, row_devices - 1)}, device_id_type=MESH)

    def down(t):
        return pltpu.make_async_remote_copy(cov.at[top, lanes(t)], big.at[t, after, :], down_send.at[t], down_recv.at[t],
                                            device_id={"row": jnp.maximum(r - 1, 0)}, device_id_type=MESH)

    def up_first(k, t):
        return pltpu.make_async_remote_copy(cov.at[bottom, lanes(t)], relay.at[k], up_send.at[t], hop_recv.at[k],
                                            device_id={"row": detour["up_by"]}, device_id_type=MESH)

    def down_first(k, t):
        return pltpu.make_async_remote_copy(cov.at[top, lanes(t)], relay.at[k], down_send.at[t], hop_recv.at[k],
                                            device_id={"row": detour["down_by"]}, device_id_type=MESH)

    def up_second(k, t):
        return pltpu.make_async_remote_copy(relay.at[k], big.at[t, before, :], hop_send.at[k], up_recv.at[t],
                                            device_id={"row": detour["high"]}, device_id_type=MESH)

    def down_second(k, t):
        return pltpu.make_async_remote_copy(relay.at[k], big.at[t, after, :], hop_send.at[k], down_recv.at[t],
                                            device_id={"row": detour["low"]}, device_id_type=MESH)

    count = count + has_left.astype(jnp.int32)

    @pl.when(has_right)
    def _():
        pl.semaphore_signal(barrier, inc=1, device_id={"col": jnp.minimum(c + 1, col_devices - 1)}, device_id_type=MESH)

    wind_copies = [pltpu.make_async_copy(ref, winds.at[k], wind_sem.at[k]) for k, ref in enumerate((ew, nw, dlon, dlat))]
    pl.semaphore_wait(barrier, count)

    odd = r % 2 == 1

    def send_slow(t):
        low = high = r < 0
        if t in carried:
            k = carried.index(t)
            low, high = r == detour["low"], r == detour["high"]

            @pl.when(low)
            def _():
                up_first(k, t).start()

            @pl.when(high)
            def _():
                down_first(k, t).start()

        @pl.when(odd & has_up & ~low)
        def _():
            up(t).start()

        @pl.when(~odd & has_down & ~high)
        def _():
            down(t).start()

    def send_quick(t):
        @pl.when(odd)
        def _():
            down(t).start()

        @pl.when(~odd)
        def _():
            up(t).start()

    for t in edges:
        send_slow(t)
    for copy in wind_copies:
        copy.start()
    for t in edges:
        load(t).start()
        send_quick(t)
    for t in middle:
        send_slow(t)
    for t in middle:
        load(t).start()
    for t in middle:
        send_quick(t)

    @pl.when(has_left)
    def _():
        pl.semaphore_signal(ready_sem, inc=1, device_id={"col": jnp.maximum(c - 1, 0)}, device_id_type=MESH)

    def relay_step(k):
        t = carried[k]

        @pl.when(r == detour["up_by"])
        def _():
            up_first(k, t).wait_recv()
            up_second(k, t).start()

        @pl.when(r == detour["down_by"])
        def _():
            down_first(k, t).wait_recv()
            down_second(k, t).start()

    for copy in wind_copies:
        copy.wait()
    east_wind, north_wind, lon, lat = (winds[k] for k in range(4))
    half_east, half_north = 0.5 * east_wind, 0.5 * north_wind
    made = [1.0 - 2.0 * lon - 2.0 * lat, lon - half_east, lon + half_east, lat - half_north, lat + half_north]
    grid_lines = lon.shape[0]
    edge = STEPS - 1
    spread = -(-(lines + 2 * edge) // SUBS) * SUBS
    for k, table in enumerate(made):
        pads[k, pl.ds(0, PAD), :] = jnp.zeros((PAD, LANES), jnp.float32)
        pads[k, pl.ds(PAD, grid_lines), :] = table
        pads[k, pl.ds(PAD + grid_lines, spread), :] = jnp.zeros((spread, LANES), jnp.float32)
    wide = -(-(tiles + 2 * edge) // SUBS) * SUBS
    for k in range(len(made)):
        rtab[k] = pads[k, pl.ds(c * tiles + PAD - edge, wide), :]
        mine = pads[k, pl.ds(r * lines + PAD - edge, spread), :]
        turned = jnp.transpose(jnp.concatenate([mine, jnp.zeros((LANES - spread, LANES), jnp.float32)], axis=0))
        for i in range(lines + 2 * edge):
            ctab[k, i] = jnp.broadcast_to(turned[:, i : i + 1], (NLON, LANES))

    @pl.when(~has_down)
    def _():
        def clear(t, _):
            big[t, before, :] = jnp.zeros((HALO, LANES), jnp.float32)
            return 0
        lax.fori_loop(0, tiles, clear, 0)

    @pl.when(~has_up)
    def _():
        def clear(t, _):
            big[t, after, :] = jnp.zeros((HALO, LANES), jnp.float32)
            return 0
        lax.fori_loop(0, tiles, clear, 0)

    @pl.when(~has_left)
    def _():
        fwd[pl.ds(0, STEPS)] = jnp.zeros((STEPS, rows, LANES), jnp.float32)

    @pl.when(~has_right)
    def _():
        fwd[pl.ds(tiles + STEPS, STEPS)] = jnp.zeros((STEPS, rows, LANES), jnp.float32)

    def in_big(pair, n, slot):
        return line_of(big, pair, n, slot)

    def in_fwd(pair, n, line):
        return fwd.at[pair[n] + STEPS], (line - STEPS) * NLON

    def inner_columns(pair):
        kept_one = {4: 5, 5: 6, lines: lines - 1, lines + 1: lines}
        kept_two = {5: 7, 6: 8, lines - 1: lines - 3, lines: lines - 2}

        def at_one(n, line):
            return one.at[n], PAD + (line - 4) * NLON

        def at_two(n, line):
            return two.at[n], PAD + (line - 5) * NLON

        def step1(line, _):
            line_step(ctab, pair, line, lambda n, d: in_big(pair, n, line + d), lambda n: [at_one(n, line)])
            return 0

        def step2(line, keep):
            places = lambda n: [at_two(n, line)] + ([in_big(pair, n, kept_two[line])] if keep else [])
            keeps = [(d, functools.partial(lambda n, slot: in_big(pair, n, slot), slot=kept_one[line + d]))
                     for d in ((-1, 0) if line == 5 else (0, 1))] if keep and line in (5, lines) else []
            line_step(ctab, pair, line, lambda n, d: at_one(n, line + d), places, keeps)

        def step2_plain(line, _):
            step2(line, False)
            return 0

        def step3(line, _):
            line_step(ctab, pair, line, lambda n, d: at_two(n, line + d), lambda n: [in_fwd(pair, n, line)])
            return 0

        lax.fori_loop(4, lines + 2, step1, 0)
        step2(5, True)
        step2(6, True)
        lax.fori_loop(7, lines - 1, step2_plain, 0)
        step2(lines - 1, True)
        step2(lines, True)
        lax.fori_loop(6, lines, step3, 0)

    def outer(pair, south):
        outer_columns(big, ctab, one, two, lines, pair, south, lambda n, line: in_fwd(pair, n, line))

    quick, slow = odd_rows(odd, rows)

    def quick_columns(pair):
        @pl.when(odd)
        def _():
            for t in pair:
                up(t).wait_recv()
            outer(pair, False)

        @pl.when(~odd)
        def _():
            for t in pair:
                down(t).wait_recv()
            outer(pair, True)

    def slow_arrive(pair):
        @pl.when(odd & has_up)
        def _():
            for t in pair:
                down(t).wait_recv()

        @pl.when(~odd & has_down)
        def _():
            for t in pair:
                up(t).wait_recv()

    def slow_columns(pair):
        slow_arrive(pair)

        @pl.when(odd)
        def _():
            outer(pair, True)

        @pl.when(~odd)
        def _():
            outer(pair, False)

    pieces = (rows - 2 * HALO) // PIECE
    side = HALO // PIECE

    def piece_start(part):
        on_quick, on_slow = quick + (part - pieces) * PIECE, slow + (part - pieces - side) * PIECE
        start = jnp.where(part < pieces, HALO + part * PIECE, jnp.where(part < pieces + side, on_quick, on_slow))
        return pl.multiple_of(start, PIECE)

    def z_copy(part, right):
        where = pl.ds(piece_start(part), PIECE)
        first, there = (tiles, 0) if right else (STEPS, tiles + STEPS)
        other = jnp.minimum(c + 1, col_devices - 1) if right else jnp.maximum(c - 1, 0)
        n = 2 * part + (1 if right else 0)
        return pltpu.make_async_remote_copy(fwd.at[pl.ds(first, STEPS), where, :], fwd.at[pl.ds(there, STEPS), where, :],
                                            z_send.at[n], z_recv.at[n], device_id={"col": other}, device_id_type=MESH)

    def z_start(part, _):
        @pl.when(has_right)
        def _():
            z_copy(part, True).start()

        @pl.when(has_left)
        def _():
            z_copy(part, False).start()
        return 0

    def z_wait(part, _):
        @pl.when(has_right)
        def _():
            z_copy(part, True).wait_send()
            z_copy(part, False).wait_recv()

        @pl.when(has_left)
        def _():
            z_copy(part, False).wait_send()
            z_copy(part, True).wait_recv()
        return 0

    def pair_of(i):
        got = []
        for n in range(PAIR):
            m = i * PAIR + n
            got.append(jnp.where(m < 2 * STEPS, m + (m // STEPS) * (tiles - 2 * STEPS), m - STEPS))
        return got

    edge_pairs, all_pairs = 2 * STEPS // PAIR, tiles // PAIR

    def early(i, _):
        pair = pair_of(i)
        for t in pair:
            load(t).wait()
        inner_columns(pair)
        quick_columns(pair)

        @pl.when(i == edge_pairs - 1)
        def _():
            @pl.when(has_right)
            def _():
                pl.semaphore_wait(ready_sem, 1)

            lax.fori_loop(0, pieces + side, z_start, 0)

        if detour:
            for k in range(len(carried)):
                @pl.when(i == k * all_pairs // len(carried))
                def _():
                    relay_step(k)
        return 0

    lax.fori_loop(0, all_pairs, early, 0)

    def held(tile, at):
        return fwd[tile + STEPS, pl.ds(at, RBLOCK), :]

    def keep(tile, at, value):
        fwd[tile, pl.ds(at, RBLOCK), :] = value

    def ready_rows(part, _):
        z_wait(part, 0)
        row_pass(held, rtab, 0, tiles, piece_start(part), PIECE, keep)
        return 0

    groups = slow_groups(all_pairs - edge_pairs)
    stops = []
    at = edge_pairs
    for n in groups[:-1]:
        at += n
        stops.append(at)

    def late(i, _):
        slow_columns(pair_of(i))

        @pl.when(i == edge_pairs - 1)
        def _():
            lax.fori_loop(pieces + side, pieces + 2 * side, z_start, 0)
            lax.fori_loop(0, pieces + side, ready_rows, 0)

        done = 0
        for n, stop in enumerate(stops):
            upto = stop * PAIR - 2 * STEPS

            @pl.when(i == stop - 1)
            def _():
                if n == 0:
                    lax.fori_loop(pieces + side, pieces + 2 * side, z_wait, 0)
                row_pass(held, rtab, done, upto, slow, HALO, keep)
            done = upto
        return 0

    def sent(t, _):
        @pl.when(has_up)
        def _():
            up(t).wait_send()

        @pl.when(has_down)
        def _():
            down(t).wait_send()
        return 0

    lax.fori_loop(0, all_pairs - 1, late, 0)
    for k, t in enumerate(carried):
        @pl.when(r == detour["up_by"])
        def _():
            up_second(k, t).wait_send()

        @pl.when(r == detour["down_by"])
        def _():
            down_second(k, t).wait_send()
    final = tiles - STEPS - PAIR
    lax.fori_loop(0, final, sent, 0)
    lax.fori_loop(final + PAIR, tiles, sent, 0)
    slow_arrive([final + n for n in range(PAIR)])
    lax.fori_loop(final, final + PAIR, sent, 0)


def slow_groups(pairs):
    groups = []
    while pairs > 3:
        groups.append(3)
        pairs -= 3
    return groups + [pairs - 1, 1] if pairs > 1 else groups + [pairs]


def rest(tiles):
    pairs = (tiles - 2 * STEPS) // PAIR
    return STEPS + (pairs - slow_groups(pairs)[-1]) * PAIR - STEPS


def odd_rows(odd, rows):
    return jnp.where(odd, 0, rows - HALO), jnp.where(odd, rows - HALO, 0)


def row_pass(read, rtab, a, b, start, count, store):
    edge = STEPS - 1

    def block(i, _):
        at = pl.multiple_of(start + i * RBLOCK, RBLOCK)
        got = {}
        for tile in range(a - STEPS, b + STEPS):
            got[0, tile] = read(tile, at)
            for step in range(1, STEPS + 1):
                mid = tile - step
                if mid < a - STEPS + step:
                    continue
                here = got[step - 1, mid]
                coef = [rtab[k, pl.ds(mid + edge, 1), :] for k in range(5)]
                value = (
                    (coef[0] * here + coef[1] * pltpu.roll(here, LANES - 1, 1))
                    + (coef[2] * pltpu.roll(here, 1, 1) + coef[3] * got[step - 1, mid + 1])
                    + coef[4] * got[step - 1, mid - 1]
                )
                got.pop((step - 1, mid - 1))
                if step < STEPS:
                    got[step, mid] = value
                else:
                    store(mid, at, value)
        return 0

    lax.fori_loop(0, count // RBLOCK, block, 0)


def finish_kernel(tiles, fwd, rtab, big, ctab, out, last, ends, one, two, done_sem, slow_sem):
    rows = out.shape[0]
    lines = rows // NLON
    begin = rest(tiles)
    odd = lax.axis_index("row") % 2 == 1
    quick, slow = odd_rows(odd, rows)
    ready = pl.ds(pl.multiple_of(jnp.where(quick == 0, 0, HALO), SUBS), rows - HALO)
    late = pl.ds(pl.multiple_of(slow, SUBS), HALO)

    def lanes(t):
        return pl.ds(t * LANES, LANES)

    copies = [pltpu.make_async_copy(fwd.at[t, ready, :], out.at[ready, lanes(t)], done_sem.at[t]) for t in range(tiles)]
    copies += [pltpu.make_async_copy(fwd.at[t, late, :], out.at[late, lanes(t)], slow_sem.at[t]) for t in range(begin)]
    for copy in copies:
        copy.start()

    pair = [tiles - STEPS - PAIR + n for n in range(PAIR)]

    @pl.when(odd)
    def _():
        outer_columns(big, ctab, one, two, lines, pair, True, lambda n, line: (ends.at[n], (line - lines) * NLON))

    @pl.when(~odd)
    def _():
        outer_columns(big, ctab, one, two, lines, pair, False, lambda n, line: (ends.at[n], (line - STEPS) * NLON))

    def held(tile, at):
        if tile in pair:
            return ends[tile - pair[0], pl.ds(pl.multiple_of(at - slow, SUBS), RBLOCK), :]
        return fwd[tile + STEPS, pl.ds(at, RBLOCK), :]

    def keep(tile, at, value):
        last[tile - begin, pl.ds(pl.multiple_of(at - slow, SUBS), RBLOCK), :] = value

    row_pass(held, rtab, begin, tiles, slow, HALO, keep)
    copies_left = [pltpu.make_async_copy(last.at[t - begin], out.at[late, lanes(t)], slow_sem.at[t]) for t in range(begin, tiles)]
    for copy in copies_left:
        copy.start()
    for copy in copies + copies_left:
        copy.wait()


def fused_body(row_devices, col_devices, covariance, east_wind, north_wind, diffuse_lon, diffuse_lat):
    rows, cols = covariance.shape
    lines, tiles = rows // NLON, cols // NLON
    edge = STEPS - 1
    spread = -(-(lines + 2 * edge) // SUBS) * SUBS
    wide = -(-(tiles + 2 * edge) // SUBS) * SUBS
    slack = PAD + east_wind.shape[0] + max(spread, wide)
    detour = detours(row_devices, tiles)
    hops = len(detour["tiles"]) if detour else 1
    f32 = jnp.float32
    kept = [
        (tiles + 2 * STEPS, rows, LANES),
        (5, wide, LANES),
        (tiles, 2 * PAD + 2 * HALO + rows, LANES),
        (5, lines + 2 * edge, NLON, LANES),
    ]
    room = 64 * 1024 * 1024 - sum(4 * math.prod(shape) for shape in kept) - 1024 * 1024
    made = pl.pallas_call(
        functools.partial(fused_kernel, row_devices, col_devices, lines, tiles),
        in_specs=[pl.BlockSpec(memory_space=pl.ANY)] * 5,
        out_specs=[pl.BlockSpec(memory_space=pltpu.VMEM)] * len(kept) + [pl.BlockSpec(memory_space=pl.ANY)],
        out_shape=[pltpu.VMEM(shape, f32) for shape in kept] + [jax.ShapeDtypeStruct((hops, HALO, LANES), f32)],
        scratch_shapes=[
            pltpu.VMEM((PAIR, 2 * PAD + (lines - 2) * NLON, LANES), f32),
            pltpu.VMEM((PAIR, 2 * PAD + (lines - 4) * NLON, LANES), f32),
            pltpu.VMEM((5, slack, LANES), f32),
            pltpu.VMEM((4,) + east_wind.shape, f32),
            pltpu.SemaphoreType.DMA((4,)),
            pltpu.SemaphoreType.DMA((tiles,)),
            pltpu.SemaphoreType.DMA((tiles,)),
            pltpu.SemaphoreType.DMA((tiles,)),
            pltpu.SemaphoreType.DMA((tiles,)),
            pltpu.SemaphoreType.DMA((tiles,)),
            pltpu.SemaphoreType.DMA((hops,)),
            pltpu.SemaphoreType.DMA((hops,)),
            pltpu.SemaphoreType.DMA((2 * rows // PIECE,)),
            pltpu.SemaphoreType.DMA((2 * rows // PIECE,)),
            pltpu.SemaphoreType.REGULAR,
        ],
        compiler_params=pltpu.CompilerParams(collective_id=0, has_side_effects=True, vmem_limit_bytes=room),
    )(covariance, east_wind, north_wind, diffuse_lon, diffuse_lat)
    return pl.pallas_call(
        functools.partial(finish_kernel, tiles),
        in_specs=[pl.BlockSpec(memory_space=pltpu.VMEM)] * len(kept),
        out_specs=pl.BlockSpec(memory_space=pl.ANY),
        out_shape=jax.ShapeDtypeStruct((rows, cols), f32),
        scratch_shapes=[
            pltpu.VMEM((tiles - rest(tiles), HALO, LANES), f32),
            pltpu.VMEM((PAIR, HALO, LANES), f32),
            pltpu.VMEM((PAIR, 2 * PAD + HALO, LANES), f32),
            pltpu.VMEM((PAIR, 2 * PAD + HALO, LANES), f32),
            pltpu.SemaphoreType.DMA((tiles,)),
            pltpu.SemaphoreType.DMA((tiles,)),
        ],
        compiler_params=pltpu.CompilerParams(vmem_limit_bytes=room),
    )(*[pltpu.with_memory_space_constraint(array, pltpu.VMEM) for array in made[: len(kept)]])


def solution(mesh):
    row_devices, col_devices = mesh.shape["row"], mesh.shape["col"]

    def run(covariance, *tables):
        lines, tiles = covariance.shape[0] // NLON, covariance.shape[1] // NLON
        if lines >= 4 * STEPS and tiles >= 4 * STEPS and (tiles - 2 * STEPS) % PAIR == 0:
            return fused_body(row_devices, col_devices, covariance, *tables)
        return body(covariance, *tables)

    return jax.shard_map(
        run,
        mesh=mesh,
        in_specs=(P("row", "col"), P(), P(), P(), P()),
        out_specs=P("row", "col"),
        check_vma=False,
    )
```

```python
import functools
import math

import jax
import jax.numpy as jnp
from jax import lax
from jax.experimental import pallas as pl
from jax.experimental.pallas import tpu as pltpu
from jax.sharding import PartitionSpec as P

NLON = 128
STEPS = 3
UNIT = STEPS * NLON
WIDE = 256
BLOCK = 192
VMEM = 52 * 1024 * 1024


OFFSETS = [(y, x) for y in range(-STEPS, STEPS + 1) for x in range(-STEPS + abs(y), STEPS + 1 - abs(y))]


def power_kernel(east_wind, north_wind, diffuse_lon, diffuse_lat, plain, rolled):
    lon, lat = diffuse_lon[...], diffuse_lat[...]
    half_east, half_north = 0.5 * east_wind[...], 0.5 * north_wind[...]
    one = {
        (0, 0): 1.0 - 2.0 * lon - 2.0 * lat,
        (0, 1): lon - half_east,
        (0, -1): lon + half_east,
        (1, 0): lat - half_north,
        (-1, 0): lat + half_north,
    }
    lines = lon.shape[0]
    line = lax.broadcasted_iota(jnp.int32, lon.shape, 0)

    def seen(field, y, x):
        if x:
            return pltpu.roll(field, -x % NLON, 1)
        if y:
            edge = lines - 1 if y > 0 else 0
            return jnp.where(line == edge, 0.0, pltpu.roll(field, -y % lines, 0))
        return field

    power = dict(one)
    for _ in range(STEPS - 1):
        made = {}
        for (y, x), field in power.items():
            for (sy, sx), scale in one.items():
                term = scale * seen(field, sy, sx)
                at = (y + sy, x + sx)
                made[at] = made[at] + term if at in made else term
        power = made
    for k, (y, x) in enumerate(OFFSETS):
        plain[k] = power[y, x]
        rolled[k] = pltpu.roll(power[y, x], x % NLON, 1)


def powers(tables):
    shape = jax.ShapeDtypeStruct((len(OFFSETS),) + tables[0].shape, jnp.float32)
    return pl.pallas_call(
        power_kernel,
        out_shape=(shape, shape),
        compiler_params=pltpu.CompilerParams(vmem_limit_bytes=VMEM),
        cost_estimate=pl.CostEstimate(flops=10**7, bytes_accessed=10**7, transcendentals=0),
    )(*tables)


def split(value):
    high = value.astype(jnp.bfloat16)
    return high, (value - high.astype(jnp.float32)).astype(jnp.bfloat16)


def block_kernel(made, transposed, offset, table, out):
    base = offset[0] + pl.program_id(0) * made
    sub = lax.broadcasted_iota(jnp.int32, (NLON, NLON), 0)
    lane = lax.broadcasted_iota(jnp.int32, (NLON, NLON), 1)
    away = (sub - lane if transposed else lane - sub) & (NLON - 1)
    read = made + 2 * STEPS
    for a in range(made):
        for b in range(read):
            y = b - a - STEPS
            value = jnp.zeros((NLON, NLON), jnp.float32)
            for k, (oy, x) in enumerate(OFFSETS):
                if oy == y:
                    line = table[k, pl.ds(base + a, 1), :]
                    value = jnp.where(away == x % NLON, jnp.broadcast_to(line, (NLON, NLON)), value)
            high, low = split(value)
            mine, theirs = slice(a * NLON, (a + 1) * NLON), slice(b * NLON, (b + 1) * NLON)
            if transposed:
                out[0, theirs, mine] = high
                out[0, slice((read + b) * NLON, (read + b + 1) * NLON), mine] = low
            else:
                out[0, mine, theirs] = high
                out[0, slice((made + a) * NLON, (made + a + 1) * NLON), theirs] = low


def blocks_of(table, offset, groups, made, transposed):
    read = made + 2 * STEPS
    shape = (2 * read * NLON, made * NLON) if transposed else (2 * made * NLON, read * NLON)
    return pl.pallas_call(
        functools.partial(block_kernel, made, transposed),
        grid=(groups,),
        in_specs=[
            pl.BlockSpec(memory_space=pltpu.SMEM),
            pl.BlockSpec(table.shape, lambda i: (0, 0, 0)),
        ],
        out_specs=pl.BlockSpec((1,) + shape, lambda i: (i, 0, 0)),
        out_shape=jax.ShapeDtypeStruct((groups,) + shape, jnp.bfloat16),
        compiler_params=pltpu.CompilerParams(vmem_limit_bytes=VMEM),
        cost_estimate=pl.CostEstimate(flops=10**7, bytes_accessed=2 * 10**7, transcendentals=0),
    )(offset.reshape(1).astype(jnp.int32), table)


def dot(a, b):
    return jnp.dot(a, b, preferred_element_type=jnp.float32)


def stencil(c, east, west, north, south, coef):
    return coef[0] * c + coef[1] * east + coef[2] * west + coef[3] * north + coef[4] * south


def column_kernel(parts, sides, *refs):
    ins, tables, out = refs[: len(parts)], refs[len(parts)], refs[-1]
    for side, (names, first, count) in enumerate(sides):

        def source(line):
            part, at = divmod(line, STEPS)
            return ins[names[part]][at * NLON : (at + 1) * NLON, :]

        lines = count + 2 * STEPS
        got = {}
        for line in range(lines):
            got[0, line] = source(line)
            for step in range(1, STEPS + 1):
                mid = line - step
                if mid < step:
                    continue
                c = got[step - 1, mid]
                row = first + mid - 1
                value = stencil(
                    c,
                    pltpu.roll(c, NLON - 1, 0),
                    pltpu.roll(c, 1, 0),
                    got[step - 1, mid + 1],
                    got[step - 1, mid - 1],
                    [tables[k, row] for k in range(5)],
                )
                got.pop((step - 1, mid - 1))
                if step < STEPS:
                    got[step, mid] = value
                else:
                    at = sum(s[2] for s in sides[:side]) + mid - STEPS
                    out[at * NLON : (at + 1) * NLON, :] = value


def column_sweep(arrays, sides, width, coefs):
    total = sum(count for _, _, count in sides) * NLON
    in_specs = [
        pl.BlockSpec((UNIT, NLON), functools.partial(lambda i, r, c, skip: (r, jnp.where(i < UNIT // NLON, i + c, i + c + skip)), r=r, c=c, skip=skip)) for _, r, c, skip in arrays
    ]
    in_specs.append(pl.BlockSpec(coefs.shape, lambda i: (0, 0, 0, 0)))
    work = total * width
    return pl.pallas_call(
        functools.partial(column_kernel, arrays, sides),
        grid=(width // NLON,),
        in_specs=in_specs,
        out_specs=pl.BlockSpec((total, NLON), lambda i: (0, i)),
        out_shape=jax.ShapeDtypeStruct((total, width), jnp.float32),
        compiler_params=pltpu.CompilerParams(vmem_limit_bytes=VMEM),
        cost_estimate=pl.CostEstimate(flops=work * 40, bytes_accessed=work * 12, transcendentals=0),
    )(*[a[0] for a in arrays], coefs)


def row_kernel(count, *refs):
    ins, tables, out, both = refs[: count + 2], refs[count + 2], refs[-2], refs[-1]
    rows = out.shape[0]
    read = (2 + 2 * STEPS) * NLON
    for n, ref in enumerate(ins):
        cols = slice(n * UNIT, (n + 1) * UNIT)
        both[:rows, cols], both[rows:, cols] = split(ref[...])
    for pair in range(count * STEPS // 2):
        cols = slice(pair * 2 * NLON, pair * 2 * NLON + read)
        first = dot(both[:, cols], tables[pair, :read, :])
        other = dot(both[:rows, cols], tables[pair, read:, :])
        out[:, pair * 2 * NLON : (pair + 1) * 2 * NLON] = first[:rows] + (first[rows:] + other)


def row_sweep(arrays, part, tables, out_rows, row_block, out_cols, col_block, buffer):
    count = len(arrays) - 2
    rows = arrays[0][0].shape[0]
    pairs = count * STEPS // 2
    in_specs = [pl.BlockSpec((BLOCK, UNIT), functools.partial(lambda i, c: (i, c), c=c)) for _, c in arrays]
    in_specs.append(
        pl.BlockSpec((pairs,) + tables.shape[1:], lambda i: (part, 0, 0), pipeline_mode=pl.Buffered(1))
    )
    operands = [a for a, _ in arrays] + [tables]
    aliases = {}
    if buffer is not None:
        in_specs.append(pl.BlockSpec(memory_space=pl.ANY))
        operands.append(buffer)
        aliases = {len(operands) - 1: 0}
    work = rows * count * UNIT
    return pl.pallas_call(
        functools.partial(row_kernel, count),
        grid=(rows // BLOCK,),
        in_specs=in_specs,
        out_specs=pl.BlockSpec((BLOCK, count * UNIT), lambda i: (row_block(i), col_block)),
        out_shape=jax.ShapeDtypeStruct((out_rows, out_cols), jnp.float32),
        input_output_aliases=aliases,
        scratch_shapes=[pltpu.VMEM((2 * BLOCK, len(arrays) * UNIT), jnp.bfloat16)],
        compiler_params=pltpu.CompilerParams(vmem_limit_bytes=VMEM),
        cost_estimate=pl.CostEstimate(flops=work * 40, bytes_accessed=work * 12, transcendentals=0),
    )(*operands)


def exchange(first, last, axis):
    devices = lax.axis_size(axis)
    up = [(i, i + 1) for i in range(devices - 1)]
    down = [(j, i) for i, j in up]
    return lax.ppermute(last, axis, up), lax.ppermute(first, axis, down)


def coefficients(tables, offset, lines):
    east_wind, north_wind, diffuse_lon, diffuse_lat = tables
    made = jnp.stack(
        [
            1.0 - 2.0 * diffuse_lon - 2.0 * diffuse_lat,
            diffuse_lon - 0.5 * east_wind,
            diffuse_lon + 0.5 * east_wind,
            diffuse_lat - 0.5 * north_wind,
            diffuse_lat + 0.5 * north_wind,
        ]
    )
    edge = STEPS - 1
    made = jnp.pad(made, ((0, 0), (edge, edge), (0, 0)))
    return lax.dynamic_slice_in_dim(made, offset, lines + 2 * edge, 1)


def body(covariance, east_wind, north_wind, diffuse_lon, diffuse_lat):
    tables = (east_wind, north_wind, diffuse_lon, diffuse_lat)
    rows, cols = covariance.shape
    row_lines, col_lines = rows // NLON, cols // NLON
    row_units, col_units = rows // UNIT, cols // UNIT
    row_coefs = coefficients(tables, lax.axis_index("row") * row_lines, row_lines)
    row_coefs = jnp.broadcast_to(row_coefs[:, :, :, None], row_coefs.shape + (NLON,))
    plain, _ = powers(tables)
    col_tables = blocks_of(plain, lax.axis_index("col") * col_lines, col_lines // 2, 2, True)

    if col_units == 1:
        pieces = [[0]]
    else:
        pieces = [[0, col_units - 1]]
        half = col_units // 2
        if col_units % 2 == 0 and col_units >= 6:
            pieces += [list(range(1, half + 1)), list(range(half + 1, col_units - 1))]
        elif col_units > 2:
            pieces += [list(range(1, col_units - 1))]

    def columns(units, low, high):
        parts = []
        for u in units:
            if parts and parts[-1][1] == u:
                parts[-1][1] = u + 1
            else:
                parts.append([u, u + 1])
        return jnp.concatenate([covariance[low:high, a * UNIT : b * UNIT] for a, b in parts], axis=1)

    halos = [exchange(columns(p, 0, UNIT), columns(p, rows - UNIT, rows), "row") for p in pieces]

    inner = None
    if row_units > 2:
        inner = column_sweep(
            [(covariance, r, 0, 0) for r in range(row_units)],
            [(list(range(row_units)), STEPS, row_lines - 2 * STEPS)],
            cols,
            row_coefs,
        )

    outer = []
    where = {}
    for k, (units, (before, after)) in enumerate(zip(pieces, halos)):
        width = len(units) * UNIT
        skip = (cols - 2 * UNIT) // NLON if k == 0 and col_units > 1 else 0
        blocks = [(covariance, r, units[0] * (UNIT // NLON), skip) for r in range(row_units)]
        if row_units == 1:
            arrays = [(before, 0, 0, 0), blocks[0], (after, 0, 0, 0)]
            sides = [([0, 1, 2], 0, STEPS)]
        else:
            arrays = [(before, 0, 0, 0), blocks[0], blocks[1], blocks[-2], blocks[-1], (after, 0, 0, 0)]
            sides = [([0, 1, 2], 0, STEPS), ([3, 4, 5], row_lines - STEPS, STEPS)]
        outer.append(column_sweep(arrays, sides, width, row_coefs))
        for at, u in enumerate(units):
            where[u] = (k, at)

    out_blocks, tiles = rows // BLOCK, UNIT // BLOCK
    halves = [list(range(col_units))]
    if len(pieces) == 3:
        halves = [list(range(half)), list(range(half, col_units))]

    edges = outer[0]
    outer_halo = exchange(edges[:, :UNIT], edges[:, -UNIT:], "col")
    out = None
    if inner is not None:
        inner_halo = exchange(inner[:, :UNIT], inner[:, cols - UNIT :], "col")
        arrays = [(inner_halo[0], 0)] + [(inner, u) for u in range(col_units)] + [(inner_halo[1], 0)]
        out = row_sweep(arrays, 0, col_tables, rows, lambda i: i + tiles, cols, 0, out)

    def outer_row(i):
        return jnp.where(i < tiles, i, i + out_blocks - 2 * tiles) if row_units > 1 else i

    for h, units in enumerate(halves):
        arrays = []
        for u in [units[0] - 1] + units + [units[-1] + 1]:
            if u < 0:
                arrays.append((outer_halo[0], 0))
            elif u == col_units:
                arrays.append((outer_halo[1], 0))
            else:
                arrays.append((outer[where[u][0]], where[u][1]))
        out = row_sweep(arrays, h, col_tables, rows, outer_row, cols, h, out)
    return out


LANES = 128
SUBS = 8
PAD = 8
HALO = STEPS * NLON
PAIR = 2
RBLOCK = 96
PIECE = 192
MESH = pl.DeviceIdType.MESH


def tile_order(tiles):
    edges = list(range(STEPS)) + list(range(tiles - STEPS, tiles))
    return edges, list(range(STEPS, tiles - STEPS))


def detours(row_devices, tiles):
    if row_devices != 8:
        return None
    _, middle = tile_order(tiles)
    carried = [t for n, t in enumerate(middle) if n % 3]
    return dict(low=3, high=4, up_by=7, down_by=0, tiles=carried)


def line_step(ctab, pair, line, source, stores, keeps=()):
    sub = lax.broadcasted_iota(jnp.int32, (SUBS, LANES), 0)
    for g in range(NLON // SUBS):
        at = g * SUBS
        coef = [ctab[k, line - 1, pl.ds(at, SUBS), :] for k in range(5)]
        for n in range(len(pair)):

            def read(d, shift=0, count=SUBS):
                ref, base = source(n, d)
                return ref[pl.ds(pl.multiple_of(base, SUBS) + shift, count), :]

            def write(place, value):
                ref, base = place
                ref[pl.ds(pl.multiple_of(base + at, SUBS), SUBS), :] = value

            seen = {d: read(d, at) for d in (-1, 0, 1)}
            east, west = read(0, at + 1), read(0, at - 1)
            if g == NLON // SUBS - 1:
                east = jnp.where(sub == SUBS - 1, read(0, 0, 1), east)
            if g == 0:
                west = jnp.where(sub == 0, read(0, NLON - 1, 1), west)
            value = (coef[0] * seen[0] + coef[1] * east) + (coef[2] * west + coef[3] * seen[1]) + coef[4] * seen[-1]
            for place in stores(n):
                write(place, value)
            for d, place in keeps:
                write(place(n), seen[d])


def line_of(big, pair, n, slot):
    return big.at[pair[n]], PAD + slot * NLON


def outer_columns(big, ctab, one, two, lines, pair, south, result):
    ones = [("one", k) for k in range(STEPS)]
    twos = [("two", k) for k in range(STEPS)]
    if south:
        first = [lines + 2, lines + 1, lines]
        after_one = [("big", lines - 1), ("big", lines)] + ones
        after_two = [("big", lines - 3), ("big", lines - 2)] + twos
    else:
        first = [1, 2, 3]
        after_one = ones + [("big", 5), ("big", 6)]
        after_two = twos + [("big", 7), ("big", 8)]

    def place(n, where):
        name, k = where
        if name == "big":
            return line_of(big, pair, n, k)
        return (one if name == "one" else two).at[n], PAD + k * NLON

    for k in range(STEPS):
        line = first[0] + k
        line_step(ctab, pair, line, lambda n, d: line_of(big, pair, n, line + d), lambda n: [place(n, ones[k])])
    for k in range(STEPS):
        line_step(ctab, pair, first[1] + k, lambda n, d: place(n, after_one[k + 1 + d]), lambda n: [place(n, twos[k])])
    for k in range(STEPS):
        line = first[2] + k
        line_step(ctab, pair, line, lambda n, d: place(n, after_two[k + 1 + d]), lambda n: [result(n, line)])


def fused_kernel(row_devices, col_devices, lines, tiles, cov, ew, nw, dlon, dlat, fwd, rtab, big, ctab, relay, one, two, pads, winds,
                 wind_sem, load_sem, up_send, up_recv, down_send, down_recv, hop_send, hop_recv, z_send, z_recv, ready_sem):
    r, c = lax.axis_index("row"), lax.axis_index("col")
    rows = lines * NLON
    edges, middle = tile_order(tiles)
    detour = detours(row_devices, tiles)
    carried = detour["tiles"] if detour else []
    has_up, has_down = r < row_devices - 1, r > 0
    has_right, has_left = c < col_devices - 1, c > 0

    partners = [(has_up, {"row": jnp.minimum(r + 1, row_devices - 1)}), (has_down, {"row": jnp.maximum(r - 1, 0)})]
    if detour:
        for a in (detour["low"], detour["high"]):
            for b in (detour["up_by"], detour["down_by"]):
                partners += [(r == a, {"row": b}), (r == b, {"row": a})]
    barrier = pltpu.get_barrier_semaphore()
    count = 0
    for there, place in partners:
        count = count + there.astype(jnp.int32)

        @pl.when(there)
        def _():
            pl.semaphore_signal(barrier, inc=1, device_id=place, device_id_type=MESH)

    def load(t):
        return pltpu.make_async_copy(cov.at[:, pl.ds(pl.multiple_of(t * LANES, LANES), LANES)], big.at[t, pl.ds(PAD + HALO, rows), :], load_sem.at[t])

    def lanes(t):
        return pl.ds(pl.multiple_of(t * LANES, LANES), LANES)

    top, bottom = pl.ds(0, HALO), pl.ds(rows - HALO, HALO)
    before, after = pl.ds(PAD, HALO), pl.ds(PAD + HALO + rows, HALO)

    def up(t):
        return pltpu.make_async_remote_copy(cov.at[bottom, lanes(t)], big.at[t, before, :], up_send.at[t], up_recv.at[t],
                                            device_id={"row": jnp.minimum(r + 1, row_devices - 1)}, device_id_type=MESH)

    def down(t):
        return pltpu.make_async_remote_copy(cov.at[top, lanes(t)], big.at[t, after, :], down_send.at[t], down_recv.at[t],
                                            device_id={"row": jnp.maximum(r - 1, 0)}, device_id_type=MESH)

    def up_first(k, t):
        return pltpu.make_async_remote_copy(cov.at[bottom, lanes(t)], relay.at[k], up_send.at[t], hop_recv.at[k],
                                            device_id={"row": detour["up_by"]}, device_id_type=MESH)

    def down_first(k, t):
        return pltpu.make_async_remote_copy(cov.at[top, lanes(t)], relay.at[k], down_send.at[t], hop_recv.at[k],
                                            device_id={"row": detour["down_by"]}, device_id_type=MESH)

    def up_second(k, t):
        return pltpu.make_async_remote_copy(relay.at[k], big.at[t, before, :], hop_send.at[k], up_recv.at[t],
                                            device_id={"row": detour["high"]}, device_id_type=MESH)

    def down_second(k, t):
        return pltpu.make_async_remote_copy(relay.at[k], big.at[t, after, :], hop_send.at[k], down_recv.at[t],
                                            device_id={"row": detour["low"]}, device_id_type=MESH)

    count = count + has_left.astype(jnp.int32)

    @pl.when(has_right)
    def _():
        pl.semaphore_signal(barrier, inc=1, device_id={"col": jnp.minimum(c + 1, col_devices - 1)}, device_id_type=MESH)

    wind_copies = [pltpu.make_async_copy(ref, winds.at[k], wind_sem.at[k]) for k, ref in enumerate((ew, nw, dlon, dlat))]
    pl.semaphore_wait(barrier, count)

    odd = r % 2 == 1

    def send_slow(t):
        low = high = r < 0
        if t in carried:
            k = carried.index(t)
            low, high = r == detour["low"], r == detour["high"]

            @pl.when(low)
            def _():
                up_first(k, t).start()

            @pl.when(high)
            def _():
                down_first(k, t).start()

        @pl.when(odd & has_up & ~low)
        def _():
            up(t).start()

        @pl.when(~odd & has_down & ~high)
        def _():
            down(t).start()

    def send_quick(t):
        @pl.when(odd)
        def _():
            down(t).start()

        @pl.when(~odd)
        def _():
            up(t).start()

    for t in edges:
        send_slow(t)
    for copy in wind_copies:
        copy.start()
    for t in edges:
        load(t).start()
        send_quick(t)
    for t in middle:
        send_slow(t)
    for t in middle:
        load(t).start()
    for t in middle:
        send_quick(t)

    @pl.when(has_left)
    def _():
        pl.semaphore_signal(ready_sem, inc=1, device_id={"col": jnp.maximum(c - 1, 0)}, device_id_type=MESH)

    def relay_step(k):
        t = carried[k]

        @pl.when(r == detour["up_by"])
        def _():
            up_first(k, t).wait_recv()
            up_second(k, t).start()

        @pl.when(r == detour["down_by"])
        def _():
            down_first(k, t).wait_recv()
            down_second(k, t).start()

    for copy in wind_copies:
        copy.wait()
    east_wind, north_wind, lon, lat = (winds[k] for k in range(4))
    half_east, half_north = 0.5 * east_wind, 0.5 * north_wind
    made = [1.0 - 2.0 * lon - 2.0 * lat, lon - half_east, lon + half_east, lat - half_north, lat + half_north]
    grid_lines = lon.shape[0]
    edge = STEPS - 1
    spread = -(-(lines + 2 * edge) // SUBS) * SUBS
    for k, table in enumerate(made):
        pads[k, pl.ds(0, PAD), :] = jnp.zeros((PAD, LANES), jnp.float32)
        pads[k, pl.ds(PAD, grid_lines), :] = table
        pads[k, pl.ds(PAD + grid_lines, spread), :] = jnp.zeros((spread, LANES), jnp.float32)
    wide = -(-(tiles + 2 * edge) // SUBS) * SUBS
    for k in range(len(made)):
        rtab[k] = pads[k, pl.ds(c * tiles + PAD - edge, wide), :]
        mine = pads[k, pl.ds(r * lines + PAD - edge, spread), :]
        turned = jnp.transpose(jnp.concatenate([mine, jnp.zeros((LANES - spread, LANES), jnp.float32)], axis=0))
        for i in range(lines + 2 * edge):
            ctab[k, i] = jnp.broadcast_to(turned[:, i : i + 1], (NLON, LANES))

    @pl.when(~has_down)
    def _():
        def clear(t, _):
            big[t, before, :] = jnp.zeros((HALO, LANES), jnp.float32)
            return 0
        lax.fori_loop(0, tiles, clear, 0)

    @pl.when(~has_up)
    def _():
        def clear(t, _):
            big[t, after, :] = jnp.zeros((HALO, LANES), jnp.float32)
            return 0
        lax.fori_loop(0, tiles, clear, 0)

    @pl.when(~has_left)
    def _():
        fwd[pl.ds(0, STEPS)] = jnp.zeros((STEPS, rows, LANES), jnp.float32)

    @pl.when(~has_right)
    def _():
        fwd[pl.ds(tiles + STEPS, STEPS)] = jnp.zeros((STEPS, rows, LANES), jnp.float32)

    def in_big(pair, n, slot):
        return line_of(big, pair, n, slot)

    def in_fwd(pair, n, line):
        return fwd.at[pair[n] + STEPS], (line - STEPS) * NLON

    def inner_columns(pair):
        kept_one = {4: 5, 5: 6, lines: lines - 1, lines + 1: lines}
        kept_two = {5: 7, 6: 8, lines - 1: lines - 3, lines: lines - 2}

        def at_one(n, line):
            return one.at[n], PAD + (line - 4) * NLON

        def at_two(n, line):
            return two.at[n], PAD + (line - 5) * NLON

        def step1(line, _):
            line_step(ctab, pair, line, lambda n, d: in_big(pair, n, line + d), lambda n: [at_one(n, line)])
            return 0

        def step2(line, keep):
            places = lambda n: [at_two(n, line)] + ([in_big(pair, n, kept_two[line])] if keep else [])
            keeps = [(d, functools.partial(lambda n, slot: in_big(pair, n, slot), slot=kept_one[line + d]))
                     for d in ((-1, 0) if line == 5 else (0, 1))] if keep and line in (5, lines) else []
            line_step(ctab, pair, line, lambda n, d: at_one(n, line + d), places, keeps)

        def step2_plain(line, _):
            step2(line, False)
            return 0

        def step3(line, _):
            line_step(ctab, pair, line, lambda n, d: at_two(n, line + d), lambda n: [in_fwd(pair, n, line)])
            return 0

        lax.fori_loop(4, lines + 2, step1, 0)
        step2(5, True)
        step2(6, True)
        lax.fori_loop(7, lines - 1, step2_plain, 0)
        step2(lines - 1, True)
        step2(lines, True)
        lax.fori_loop(6, lines, step3, 0)

    def outer(pair, south):
        outer_columns(big, ctab, one, two, lines, pair, south, lambda n, line: in_fwd(pair, n, line))

    quick, slow = odd_rows(odd, rows)

    def quick_columns(pair):
        @pl.when(odd)
        def _():
            for t in pair:
                up(t).wait_recv()
            outer(pair, False)

        @pl.when(~odd)
        def _():
            for t in pair:
                down(t).wait_recv()
            outer(pair, True)

    def slow_arrive(pair):
        @pl.when(odd & has_up)
        def _():
            for t in pair:
                down(t).wait_recv()

        @pl.when(~odd & has_down)
        def _():
            for t in pair:
                up(t).wait_recv()

    def slow_columns(pair):
        slow_arrive(pair)

        @pl.when(odd)
        def _():
            outer(pair, True)

        @pl.when(~odd)
        def _():
            outer(pair, False)

    pieces = (rows - 2 * HALO) // PIECE
    side = HALO // PIECE

    def piece_start(part):
        on_quick, on_slow = quick + (part - pieces) * PIECE, slow + (part - pieces - side) * PIECE
        start = jnp.where(part < pieces, HALO + part * PIECE, jnp.where(part < pieces + side, on_quick, on_slow))
        return pl.multiple_of(start, PIECE)

    def z_copy(part, right):
        where = pl.ds(piece_start(part), PIECE)
        first, there = (tiles, 0) if right else (STEPS, tiles + STEPS)
        other = jnp.minimum(c + 1, col_devices - 1) if right else jnp.maximum(c - 1, 0)
        n = 2 * part + (1 if right else 0)
        return pltpu.make_async_remote_copy(fwd.at[pl.ds(first, STEPS), where, :], fwd.at[pl.ds(there, STEPS), where, :],
                                            z_send.at[n], z_recv.at[n], device_id={"col": other}, device_id_type=MESH)

    def z_start(part, _):
        @pl.when(has_right)
        def _():
            z_copy(part, True).start()

        @pl.when(has_left)
        def _():
            z_copy(part, False).start()
        return 0

    def z_wait(part, _):
        @pl.when(has_right)
        def _():
            z_copy(part, True).wait_send()
            z_copy(part, False).wait_recv()

        @pl.when(has_left)
        def _():
            z_copy(part, False).wait_send()
            z_copy(part, True).wait_recv()
        return 0

    def pair_of(i):
        got = []
        for n in range(PAIR):
            m = i * PAIR + n
            got.append(jnp.where(m < 2 * STEPS, m + (m // STEPS) * (tiles - 2 * STEPS), m - STEPS))
        return got

    edge_pairs, all_pairs = 2 * STEPS // PAIR, tiles // PAIR

    def early(i, _):
        pair = pair_of(i)
        for t in pair:
            load(t).wait()
        inner_columns(pair)
        quick_columns(pair)

        @pl.when(i == edge_pairs - 1)
        def _():
            @pl.when(has_right)
            def _():
                pl.semaphore_wait(ready_sem, 1)

            lax.fori_loop(0, pieces + side, z_start, 0)

        if detour:
            for k in range(len(carried)):
                @pl.when(i == k * all_pairs // len(carried))
                def _():
                    relay_step(k)
        return 0

    lax.fori_loop(0, all_pairs, early, 0)

    def held(tile, at):
        return fwd[tile + STEPS, pl.ds(at, RBLOCK), :]

    def keep(tile, at, value):
        fwd[tile, pl.ds(at, RBLOCK), :] = value

    def ready_rows(part, _):
        z_wait(part, 0)
        row_pass(held, rtab, 0, tiles, piece_start(part), PIECE, keep)
        return 0

    groups = slow_groups(all_pairs - edge_pairs)
    stops = []
    at = edge_pairs
    for n in groups[:-1]:
        at += n
        stops.append(at)

    def late(i, _):
        slow_columns(pair_of(i))

        @pl.when(i == edge_pairs - 1)
        def _():
            lax.fori_loop(pieces + side, pieces + 2 * side, z_start, 0)
            lax.fori_loop(0, pieces + side, ready_rows, 0)

        done = 0
        for n, stop in enumerate(stops):
            upto = stop * PAIR - 2 * STEPS

            @pl.when(i == stop - 1)
            def _():
                if n == 0:
                    lax.fori_loop(pieces + side, pieces + 2 * side, z_wait, 0)
                row_pass(held, rtab, done, upto, slow, HALO, keep)
            done = upto
        return 0

    def sent(t, _):
        @pl.when(has_up)
        def _():
            up(t).wait_send()

        @pl.when(has_down)
        def _():
            down(t).wait_send()
        return 0

    lax.fori_loop(0, all_pairs - 1, late, 0)
    for k, t in enumerate(carried):
        @pl.when(r == detour["up_by"])
        def _():
            up_second(k, t).wait_send()

        @pl.when(r == detour["down_by"])
        def _():
            down_second(k, t).wait_send()
    final = tiles - STEPS - PAIR
    lax.fori_loop(0, final, sent, 0)
    lax.fori_loop(final + PAIR, tiles, sent, 0)
    slow_arrive([final + n for n in range(PAIR)])
    lax.fori_loop(final, final + PAIR, sent, 0)


def slow_groups(pairs):
    groups = []
    while pairs > 3:
        groups.append(3)
        pairs -= 3
    return groups + [pairs - 1, 1] if pairs > 1 else groups + [pairs]


def rest(tiles):
    pairs = (tiles - 2 * STEPS) // PAIR
    return STEPS + (pairs - slow_groups(pairs)[-1]) * PAIR - STEPS


def odd_rows(odd, rows):
    return jnp.where(odd, 0, rows - HALO), jnp.where(odd, rows - HALO, 0)


def row_pass(read, rtab, a, b, start, count, store):
    edge = STEPS - 1

    def block(i, _):
        at = pl.multiple_of(start + i * RBLOCK, RBLOCK)
        got = {}
        for tile in range(a - STEPS, b + STEPS):
            got[0, tile] = read(tile, at)
            for step in range(1, STEPS + 1):
                mid = tile - step
                if mid < a - STEPS + step:
                    continue
                here = got[step - 1, mid]
                coef = [rtab[k, pl.ds(mid + edge, 1), :] for k in range(5)]
                value = (
                    (coef[0] * here + coef[1] * pltpu.roll(here, LANES - 1, 1))
                    + (coef[2] * pltpu.roll(here, 1, 1) + coef[3] * got[step - 1, mid + 1])
                    + coef[4] * got[step - 1, mid - 1]
                )
                got.pop((step - 1, mid - 1))
                if step < STEPS:
                    got[step, mid] = value
                else:
                    store(mid, at, value)
        return 0

    lax.fori_loop(0, count // RBLOCK, block, 0)


def finish_kernel(tiles, fwd, rtab, big, ctab, out, last, ends, one, two, done_sem, slow_sem):
    rows = out.shape[0]
    lines = rows // NLON
    begin = rest(tiles)
    odd = lax.axis_index("row") % 2 == 1
    quick, slow = odd_rows(odd, rows)
    ready = pl.ds(pl.multiple_of(jnp.where(quick == 0, 0, HALO), SUBS), rows - HALO)
    late = pl.ds(pl.multiple_of(slow, SUBS), HALO)

    def lanes(t):
        return pl.ds(t * LANES, LANES)

    copies = [pltpu.make_async_copy(fwd.at[t], out.at[:, lanes(t)], done_sem.at[t]) for t in range(begin)]
    copies += [pltpu.make_async_copy(fwd.at[t, ready, :], out.at[ready, lanes(t)], done_sem.at[t]) for t in range(begin, tiles)]
    for copy in copies:
        copy.start()

    pair = [tiles - STEPS - PAIR + n for n in range(PAIR)]

    @pl.when(odd)
    def _():
        outer_columns(big, ctab, one, two, lines, pair, True, lambda n, line: (ends.at[n], (line - lines) * NLON))

    @pl.when(~odd)
    def _():
        outer_columns(big, ctab, one, two, lines, pair, False, lambda n, line: (ends.at[n], (line - STEPS) * NLON))

    def held(tile, at):
        if tile in pair:
            return ends[tile - pair[0], pl.ds(pl.multiple_of(at - slow, SUBS), RBLOCK), :]
        return fwd[tile + STEPS, pl.ds(at, RBLOCK), :]

    def keep(tile, at, value):
        last[tile - begin, pl.ds(pl.multiple_of(at - slow, SUBS), RBLOCK), :] = value

    row_pass(held, rtab, begin, tiles, slow, HALO, keep)
    copies_left = [pltpu.make_async_copy(last.at[t - begin], out.at[late, lanes(t)], slow_sem.at[t]) for t in range(begin, tiles)]
    for copy in copies_left:
        copy.start()
    for copy in copies + copies_left:
        copy.wait()


def fused_body(row_devices, col_devices, covariance, east_wind, north_wind, diffuse_lon, diffuse_lat):
    rows, cols = covariance.shape
    lines, tiles = rows // NLON, cols // NLON
    edge = STEPS - 1
    spread = -(-(lines + 2 * edge) // SUBS) * SUBS
    wide = -(-(tiles + 2 * edge) // SUBS) * SUBS
    slack = PAD + east_wind.shape[0] + max(spread, wide)
    detour = detours(row_devices, tiles)
    hops = len(detour["tiles"]) if detour else 1
    f32 = jnp.float32
    kept = [
        (tiles + 2 * STEPS, rows, LANES),
        (5, wide, LANES),
        (tiles, 2 * PAD + 2 * HALO + rows, LANES),
        (5, lines + 2 * edge, NLON, LANES),
    ]
    room = 64 * 1024 * 1024 - sum(4 * math.prod(shape) for shape in kept) - 1024 * 1024
    made = pl.pallas_call(
        functools.partial(fused_kernel, row_devices, col_devices, lines, tiles),
        in_specs=[pl.BlockSpec(memory_space=pl.ANY)] * 5,
        out_specs=[pl.BlockSpec(memory_space=pltpu.VMEM)] * len(kept) + [pl.BlockSpec(memory_space=pl.ANY)],
        out_shape=[pltpu.VMEM(shape, f32) for shape in kept] + [jax.ShapeDtypeStruct((hops, HALO, LANES), f32)],
        scratch_shapes=[
            pltpu.VMEM((PAIR, 2 * PAD + (lines - 2) * NLON, LANES), f32),
            pltpu.VMEM((PAIR, 2 * PAD + (lines - 4) * NLON, LANES), f32),
            pltpu.VMEM((5, slack, LANES), f32),
            pltpu.VMEM((4,) + east_wind.shape, f32),
            pltpu.SemaphoreType.DMA((4,)),
            pltpu.SemaphoreType.DMA((tiles,)),
            pltpu.SemaphoreType.DMA((tiles,)),
            pltpu.SemaphoreType.DMA((tiles,)),
            pltpu.SemaphoreType.DMA((tiles,)),
            pltpu.SemaphoreType.DMA((tiles,)),
            pltpu.SemaphoreType.DMA((hops,)),
            pltpu.SemaphoreType.DMA((hops,)),
            pltpu.SemaphoreType.DMA((2 * rows // PIECE,)),
            pltpu.SemaphoreType.DMA((2 * rows // PIECE,)),
            pltpu.SemaphoreType.REGULAR,
        ],
        compiler_params=pltpu.CompilerParams(collective_id=0, has_side_effects=True, vmem_limit_bytes=room),
    )(covariance, east_wind, north_wind, diffuse_lon, diffuse_lat)
    return pl.pallas_call(
        functools.partial(finish_kernel, tiles),
        in_specs=[pl.BlockSpec(memory_space=pltpu.VMEM)] * len(kept),
        out_specs=pl.BlockSpec(memory_space=pl.ANY),
        out_shape=jax.ShapeDtypeStruct((rows, cols), f32),
        scratch_shapes=[
            pltpu.VMEM((tiles - rest(tiles), HALO, LANES), f32),
            pltpu.VMEM((PAIR, HALO, LANES), f32),
            pltpu.VMEM((PAIR, 2 * PAD + HALO, LANES), f32),
            pltpu.VMEM((PAIR, 2 * PAD + HALO, LANES), f32),
            pltpu.SemaphoreType.DMA((tiles,)),
            pltpu.SemaphoreType.DMA((tiles,)),
        ],
        compiler_params=pltpu.CompilerParams(vmem_limit_bytes=room),
    )(*[pltpu.with_memory_space_constraint(array, pltpu.VMEM) for array in made[: len(kept)]])


def solution(mesh):
    row_devices, col_devices = mesh.shape["row"], mesh.shape["col"]

    def run(covariance, *tables):
        lines, tiles = covariance.shape[0] // NLON, covariance.shape[1] // NLON
        if lines >= 4 * STEPS and tiles >= 4 * STEPS and (tiles - 2 * STEPS) % PAIR == 0:
            return fused_body(row_devices, col_devices, covariance, *tables)
        return body(covariance, *tables)

    return jax.shard_map(
        run,
        mesh=mesh,
        in_specs=(P("row", "col"), P(), P(), P(), P()),
        out_specs=P("row", "col"),
        check_vma=False,
    )
```
